32 devices in a mesh: rows: 8 (over z, x), far: 4 (over y, core).
Axes of the slice: x: 2, y: 2, z: 4, core: 2. Of those that a mesh axis runs over, the one named last changes fastest.
Arguments:
- right_side: float32 [16384, 256], P('rows'), may hold values from -24 to 24
- near_blocks: float32 [128, 24, 128, 128], P('rows', 'far'), may hold values from -0.03125 to 0.03125
- near_cols: int32 [128, 24], P('rows', 'far'), may hold values from 0 to 127, as said below
- far_src: int32 [8, 8, 4], P('rows', None, 'far'), may hold values from 0 to 15
- far_tgt: int32 [8, 8, 4], P('rows', None, 'far'), may hold values from 0 to 15
- far_left: float32 [8, 8, 4, 128, 64], P('rows', None, 'far'), may hold values from -0.15625 to 0.15625
- far_right: float32 [8, 8, 4, 128, 64], P('rows', None, 'far'), may hold values from -0.5 to 0.5
Outputs:
- solution: float32 [16384, 256], P('rows', 'far')
- residual: float32 [16384, 256], P('rows', 'far')
The draws below stay inside these ranges and needn't reach their ends.
Inputs may be any that keep to these rules, and one draw needn't show every extreme that they name: `near_cols`: each near-field column lies within 8 clusters of its row; slot 0 of row i names i itself, slot 1 names min(i + 8, 127) and slot 2 names max(i - 8, 0).
All inputs are finite; a program needn't handle non-finite values.
Results may differ from the reference program's by a relative error of at most 0.0003.
Values sent between devices are 32-bit elements; how exact they have to be, the bound alone decides.
No kernel may reach another device: no remote copies, remote signals or barrier semaphores. Data moves between devices by JAX's collectives and lax.ppermute only.
A program may use at most 128 MiB of HBM per device.

```python
import jax
import jax.numpy as jnp
from jax import lax

B = 128
R = 64
NRHS = 256
CL_DEV = 16
REACH = 8
NC = 128
PANELS = 16384
NEAR = 24
FSLOT = 4
N_ROWS = 8


def draw_right_side(key, part):
    ramp = 1.0 + 2.0 * jnp.arange(PANELS, dtype=jnp.float32) / (PANELS - 1)
    values = jnp.clip(jax.random.normal(key, (PANELS, NRHS), jnp.float32), -4.0, 4.0)
    return values * ramp[:, None]


def draw_near_cols(key, part):
    row_ids = jnp.arange(NC, dtype=jnp.int32)[:, None]
    jumps = jax.random.randint(key, (NC, NEAR), -REACH, REACH + 1, jnp.int32)
    slot_ids = jnp.arange(NEAR, dtype=jnp.int32)[None, :]
    jumps = jnp.where(slot_ids == 0, 0, jnp.where(slot_ids == 1, REACH, jnp.where(slot_ids == 2, -REACH, jumps)))
    return jnp.clip(row_ids + jumps, 0, NC - 1).astype(jnp.int32)


def touch_ends(values, key, low, top_value):
    longest = values.shape.index(max(values.shape))
    spots = []
    for shift in (0, 1):
        where = [jax.random.randint(jax.random.fold_in(key, axis), (), 0, length) for axis, length in enumerate(values.shape)]
        where[longest] = (where[longest] + shift) % values.shape[longest]
        spots.append(tuple(where))
    return values.at[spots[0]].set(low).at[spots[1]].set(top_value)


def steps_of(own_key, extent, shards, low, largest):
    level = 1.0
    for position, shards_of in shards:
        steps = jax.random.uniform(jax.random.fold_in(jax.random.fold_in(own_key, 6), position), (shards_of,), jnp.float32, low / len(shards), largest / len(shards))
        level = level * jnp.repeat(jnp.exp(steps), extent[position] // shards_of).reshape((-1,) + (1,) * (len(extent) - 1 - position))
    return level


def centred(key, shape, deviation, limit, cuts=(), kind=jnp.bfloat16):
    array = jax.random.normal(key, shape, jnp.float32) * deviation
    if len(cuts) > 0:
        array = steps_of(key, shape, cuts, -0.22, 0.18) * array
    return jnp.clip(array, min=-limit, max=limit).astype(kind)


def setup_inputs(seed: int = 0) -> dict:
    streams_of = jax.random.split(jax.random.key(seed), 8)
    right_side = draw_right_side(jax.random.fold_in(streams_of[7], 71), 0)
    near_blocks = centred(streams_of[1], (NC, NEAR, B, B), (12 * B * NEAR) ** -0.5, 0.03125, ((0, 8), (1, 4)), jnp.float32)
    near_cols = draw_near_cols(jax.random.fold_in(streams_of[7], 71), 0)
    far_src = touch_ends(jax.random.randint(streams_of[3], (N_ROWS, N_ROWS, FSLOT), 0, CL_DEV), jax.random.fold_in(streams_of[3], 1), 0, CL_DEV - 1).astype(jnp.int32)
    far_tgt = touch_ends(jax.random.randint(streams_of[4], (N_ROWS, N_ROWS, FSLOT), 0, CL_DEV), jax.random.fold_in(streams_of[4], 1), 0, CL_DEV - 1).astype(jnp.int32)
    far_left = centred(streams_of[5], (N_ROWS, N_ROWS, FSLOT, B, R), (11 * R * N_ROWS * FSLOT // CL_DEV) ** -0.5, 0.15625, ((0, 8), (2, 4)), jnp.float32)
    far_right = centred(streams_of[6], (N_ROWS, N_ROWS, FSLOT, B, R), B ** -0.5, 0.5, ((0, 8), (2, 4)), jnp.float32)
    return {"right_side": right_side, "near_blocks": near_blocks, "near_cols": near_cols, "far_src": far_src, "far_tgt": far_tgt, "far_left": far_left, "far_right": far_right}


TOP_PRECISION = lax.Precision.HIGHEST
EPS = 1e-06

def column_dots(left_vec, right_vector):
    return lax.optimization_barrier(jnp.sum(left_vec * right_vector, axis=0))

def apply_operator(vector_in, near_blocks, near_cols, far_src, far_tgt, far_left, far_right):
    blocks = vector_in.reshape(NC, B, NRHS)

    def nearby_group(items):
        group_blocks, group_columns = items
        picked = jnp.take(blocks, group_columns, axis=0)
        return jnp.einsum('cspq,csqn->cpn', group_blocks, picked, precision=TOP_PRECISION)
    near_part = lax.map(nearby_group, (near_blocks.reshape(N_ROWS, CL_DEV, NEAR, B, B), near_cols.reshape(N_ROWS, CL_DEV, NEAR)))
    starts = (jnp.arange(N_ROWS, dtype=jnp.int32) * CL_DEV)[:, None]
    columns = jnp.arange(CL_DEV, dtype=jnp.int32)

    def far_group(triple):
        target, left_here, target_local = triple
        src_here = lax.dynamic_index_in_dim(far_src, target, 1, keepdims=False)
        right_here = lax.dynamic_index_in_dim(far_right, target, 1, keepdims=False)
        picked = jnp.take(blocks, src_here + starts, axis=0)
        coefficients = jnp.einsum('asbr,asbn->asrn', right_here, picked, precision=TOP_PRECISION)
        contribution_part = jnp.einsum('asbr,asrn->asbn', left_here, coefficients, precision=TOP_PRECISION)
        owning_devices = (target_local[:, :, None] == columns).astype(jnp.float32)
        return jnp.einsum('hyo,hyze->oze', owning_devices, contribution_part, precision=TOP_PRECISION)
    far_part = lax.map(far_group, (jnp.arange(N_ROWS, dtype=jnp.int32), far_left, far_tgt))
    return 0.5 * vector_in + (near_part + far_part).reshape(PANELS, NRHS)

def least_squares(rhs_length, upper_left, lower_left, column_two, lower_right):
    radius_one = jnp.sqrt(upper_left * upper_left + lower_left * lower_left)
    cosine_one = upper_left / radius_one
    sine_one = lower_left / radius_one
    rotated_top = cosine_one * rhs_length
    rotated_mid = -sine_one * rhs_length
    coupled = cosine_one * column_two[0] + sine_one * column_two[1]
    diagonal_two = cosine_one * column_two[1] - sine_one * column_two[0]
    radius_two = jnp.sqrt(diagonal_two * diagonal_two + lower_right * lower_right)
    weight_two = diagonal_two * rotated_mid / (radius_two * radius_two)
    weight_one = (rotated_top - coupled * weight_two) / radius_one
    return (weight_one, weight_two)

def reference(right_side, near_blocks, near_cols, far_src, far_tgt, far_left, far_right):

    def apply_op(vector_in):
        return apply_operator(vector_in, near_blocks, near_cols, far_src, far_tgt, far_left, far_right)
    rhs_length = jnp.sqrt(column_dots(right_side, right_side) + EPS)
    first_vector = right_side / rhs_length
    image_one = apply_op(first_vector)
    upper_left = column_dots(first_vector, image_one)
    candidate = image_one - upper_left * first_vector
    lower_left = jnp.sqrt(column_dots(candidate, candidate) + EPS)
    second_vec = candidate / lower_left
    image_two = apply_op(second_vec)
    column_two = (column_dots(first_vector, image_two), column_dots(second_vec, image_two))
    candidate = image_two - column_two[0] * first_vector
    candidate = candidate - column_two[1] * second_vec
    lower_right = jnp.sqrt(column_dots(candidate, candidate) + EPS)
    weight_one, weight_two = least_squares(rhs_length, upper_left, lower_left, column_two, lower_right)
    solution = weight_one * first_vector + weight_two * second_vec
    residual = right_side - apply_op(solution)
    return (solution, residual)
```

```python
import functools

import jax
import jax.numpy as jnp
from jax import lax
from jax.experimental import pallas as pl
from jax.experimental.pallas import tpu as pltpu
from jax.sharding import PartitionSpec as P

B = 128
R = 64
CL_DEV = 16
REACH = 8
CORES = 2
LANES = 128
EPS = 1e-06
F32 = jnp.float32
BF16 = jnp.bfloat16
VMEM_LIMIT = 48 * 1024 * 1024

VMEM_SPEC = pl.BlockSpec(memory_space=pltpu.VMEM)
SMEM_SPEC = pl.BlockSpec(memory_space=pltpu.SMEM)


def split(value):
    high = value.astype(BF16)
    low = (value - high.astype(F32)).astype(BF16)
    return high, low


def dot3(left, right, dims):
    (lh, ll), (rh, rl) = left, right
    dot = functools.partial(lax.dot_general, dimension_numbers=(dims, ((), ())), preferred_element_type=F32)
    return dot(lh, rh) + (dot(ll, rh) + dot(lh, rl))


def far_place(far_size):
    index = lax.axis_index("far")
    return index // CORES, index % CORES, far_size // CORES


def owner_at(shift, other_core, far_size):
    y, core, ys = far_place(far_size)
    return lax.rem(y - shift + ys, ys) * CORES + (1 - core if other_core else core)


def place_own(pieces, far_size, store):
    q = REACH // far_size
    ys = far_size // CORES
    for n, piece in enumerate(pieces):
        owner = owner_at(n % ys, n >= ys, far_size)
        for half in range(2):
            for j in range(q):
                store(half * REACH + owner * q + j, piece[half * q + j])


def coefficient_kernel(far_size, whole, src_ref, right_ref, *refs):
    pieces, (out_ref, held) = refs[:-2], refs[-2:]
    if whole:
        field = pieces[0]
    else:
        field = held

        def store(cluster, value):
            held[cluster] = value

        place_own(pieces, far_size, store)
    for t in range(right_ref.shape[0]):
        factor = split(right_ref[t])
        source = split(field[src_ref[t]])
        out_ref[t] = dot3(factor, source, (((0,), (0,))))


def coefficients(pieces, src, right, far_size):
    whole = len(pieces) == 1
    groups, _, rank = right.shape
    cols = pieces[0].shape[-1]
    held = (8, LANES) if whole else (CL_DEV, B, cols)
    return pl.pallas_call(
        functools.partial(coefficient_kernel, far_size, whole),
        out_shape=jax.ShapeDtypeStruct((groups, rank, cols), F32),
        in_specs=[SMEM_SPEC, VMEM_SPEC] + [VMEM_SPEC] * len(pieces),
        out_specs=VMEM_SPEC,
        scratch_shapes=[pltpu.VMEM(held, F32)],
        compiler_params=pltpu.CompilerParams(vmem_limit_bytes=VMEM_LIMIT),
        cost_estimate=pl.CostEstimate(
            flops=6 * groups * rank * B * cols, bytes_accessed=4 * CL_DEV * B * cols, transcendentals=0
        ),
        name="coefficients",
    )(src, right, *pieces)


def operator_kernel(
    far_size, last, n_pieces, cols_ref, tgt_ref, blocks_ref, coef_ref, left_ref, *refs
):
    pieces = refs[:n_pieces]
    keep_ref, send_ref, high, low, far_acc = refs[n_pieces:]
    step = pl.program_id(0)
    y, core, ys = far_place(far_size)
    q = REACH // far_size
    groups = blocks_ref.shape[0]
    slots = blocks_ref.shape[2]
    per = CL_DEV // groups
    base = lax.axis_index("rows") * CL_DEV - REACH

    def put(position, value):
        h, l = split(value)
        high[position] = h
        low[position] = l

    @pl.when(step == 0)
    def _():
        if not last:
            own, left_mine, right_mine, left_other, right_other = pieces
            for c in range(CL_DEV):
                put(REACH + c, own[c])
            part = REACH // CORES
            for c, lefts, rights in ((core, left_mine, right_mine), (1 - core, left_other, right_other)):
                for j in range(part):
                    put(c * part + j, lefts[j])
                    put(REACH + CL_DEV + c * part + j, rights[j])
        else:
            n_own = CORES * ys
            place_own(pieces[:n_own], far_size, lambda c, v: put(REACH + c, v))
            for n in range(n_own):
                owner = owner_at(n % ys, n >= ys, far_size)
                lefts, rights = pieces[n_own + 2 * n], pieces[n_own + 2 * n + 1]
                for j in range(q):
                    put(owner * q + j, lefts[j])
                    put(REACH + CL_DEV + owner * q + j, rights[j])
        far_acc[...] = jnp.zeros_like(far_acc)
        for a in range(left_ref.shape[0]):
            target = tgt_ref[a]
            far_acc[target] += dot3(split(left_ref[a]), split(coef_ref[a]), (((1,), (0,))))

    def image(group):
        cluster = group * per + step
        at = [cols_ref[cluster * slots + s] - base for s in range(slots)]
        left = split(jnp.concatenate([blocks_ref[group, 0, s] for s in range(slots)], axis=1))
        right = tuple(jnp.concatenate([ref[p] for p in at], axis=0) for ref in (high, low))
        return far_acc[cluster] + dot3(left, right, (((1,), (0,))))

    images = [image(g) for g in range(groups)]
    if not last:
        owner = step // q
        behind = lax.rem(owner // CORES - y + ys, ys)
        mine = owner % CORES == core

        for half in range(2):
            slot = half * q + step % q

            @pl.when(mine)
            def _():
                keep_ref[behind, slot] = images[half]

            @pl.when(jnp.logical_not(mine))
            def _():
                send_ref[behind, slot] = images[half]
    else:
        width = LANES // groups
        for owner in range(far_size):
            packed = jnp.concatenate(
                [im[:, owner * width : (owner + 1) * width] for im in images], axis=1
            )
            behind = lax.rem(owner // CORES - y + ys, ys)
            mine = owner % CORES == core

            @pl.when(mine)
            def _():
                keep_ref[behind, step] = packed

            @pl.when(jnp.logical_not(mine))
            def _():
                send_ref[behind, step] = packed


def operator(pieces, cols, tgt, blocks, coef, left, far_size, last):
    width = pieces[0].shape[-1]
    slots = blocks.shape[1]
    ys = far_size // CORES
    if last:
        groups = LANES * far_size // width
        part = (ys, CL_DEV // groups, B, LANES)
    else:
        groups = 2
        part = (ys, 2 * REACH // far_size, B, width)
    steps = CL_DEV // groups
    blocks = blocks.reshape(groups, steps, slots, B, B)
    return pl.pallas_call(
        functools.partial(operator_kernel, far_size, last, len(pieces)),
        out_shape=[jax.ShapeDtypeStruct(part, F32)] * 2,
        grid=(steps,),
        in_specs=[
            SMEM_SPEC,
            SMEM_SPEC,
            pl.BlockSpec((groups, 1, slots, B, B), lambda i: (0, i, 0, 0, 0)),
            VMEM_SPEC,
            VMEM_SPEC,
        ]
        + [VMEM_SPEC] * len(pieces),
        out_specs=[VMEM_SPEC] * 2,
        scratch_shapes=[
            pltpu.VMEM((CL_DEV + 2 * REACH, B, width), BF16),
            pltpu.VMEM((CL_DEV + 2 * REACH, B, width), BF16),
            pltpu.VMEM((CL_DEV, B, width), F32),
        ],
        compiler_params=pltpu.CompilerParams(vmem_limit_bytes=VMEM_LIMIT),
        cost_estimate=pl.CostEstimate(
            flops=6 * CL_DEV * slots * B * B * width, bytes_accessed=4 * blocks.size, transcendentals=0
        ),
        name="operator",
    )(cols, tgt, blocks, coef, left, *pieces)


def pack_kernel(far_size, own_ref, *refs):
    pieces, (b_out, g_out, held) = refs[:-3], refs[-3:]
    index = lax.axis_index("far")
    groups = CL_DEV // b_out.shape[0]
    width = LANES // groups
    per = CL_DEV // groups

    def store(cluster, value):
        held[cluster] = value

    place_own(pieces, far_size, store)
    for owner in range(far_size):

        @pl.when(index == owner)
        def _():
            for k in range(per):
                for source, out in ((own_ref, b_out), (held, g_out)):
                    out[k] = jnp.concatenate(
                        [
                            source[g * per + k][:, owner * width : (owner + 1) * width]
                            for g in range(groups)
                        ],
                        axis=1,
                    )


def pack(own, pieces, far_size):
    width = own.shape[-1]
    groups = LANES * far_size // width
    part = jax.ShapeDtypeStruct((CL_DEV // groups, B, LANES), F32)
    return pl.pallas_call(
        functools.partial(pack_kernel, far_size),
        out_shape=[part] * 2,
        in_specs=[VMEM_SPEC] * (1 + len(pieces)),
        out_specs=[VMEM_SPEC] * 2,
        scratch_shapes=[pltpu.VMEM((CL_DEV, B, width), F32)],
        compiler_params=pltpu.CompilerParams(vmem_limit_bytes=VMEM_LIMIT),
        cost_estimate=pl.CostEstimate(flops=0, bytes_accessed=8 * own.size, transcendentals=0),
        name="pack",
    )(own, *pieces)


def dots_kernel(groups, n_parts, b_ref, g_ref, *refs):
    parts, (out_ref, image_ref) = refs[:n_parts], refs[n_parts:]
    image = parts[0][...]
    for part in parts[1:]:
        image = image + part[...]
    image_ref[...] = image
    vectors = (b_ref[...], g_ref[...], image)
    width = LANES // groups
    rows = []
    for left, right in ((0, 0), (0, 1), (0, 2), (1, 1), (1, 2), (2, 2)):
        total = jnp.sum(vectors[left] * vectors[right], axis=0)
        total = jnp.sum(total, axis=0, keepdims=True)
        folded = total
        for g in range(1, groups):
            folded = folded + pltpu.roll(total, g * width, 1)
        rows.append(folded)
    rows.append(jnp.zeros((2, LANES), F32))
    out_ref[...] = jnp.concatenate(rows, axis=0)


def dots(b_own, g_own, parts, groups):
    return pl.pallas_call(
        functools.partial(dots_kernel, groups, len(parts)),
        out_shape=[
            jax.ShapeDtypeStruct((8, LANES), F32),
            jax.ShapeDtypeStruct(b_own.shape, F32),
        ],
        in_specs=[VMEM_SPEC] * (2 + len(parts)),
        out_specs=[VMEM_SPEC] * 2,
        compiler_params=pltpu.CompilerParams(vmem_limit_bytes=VMEM_LIMIT),
        cost_estimate=pl.CostEstimate(
            flops=14 * b_own.size, bytes_accessed=20 * b_own.size, transcendentals=0
        ),
        name="dots",
    )(b_own, g_own, *parts)


def least_squares(rhs_length, upper_left, lower_left, top_two, mid_two, lower_right):
    radius_one = jnp.sqrt(upper_left * upper_left + lower_left * lower_left)
    cosine_one = upper_left / radius_one
    sine_one = lower_left / radius_one
    rotated_top = cosine_one * rhs_length
    rotated_mid = -sine_one * rhs_length
    coupled = cosine_one * top_two + sine_one * mid_two
    diagonal_two = cosine_one * mid_two - sine_one * top_two
    radius_two = jnp.sqrt(diagonal_two * diagonal_two + lower_right * lower_right)
    weight_two = diagonal_two * rotated_mid / (radius_two * radius_two)
    weight_one = (rotated_top - coupled * weight_two) / radius_one
    return (weight_one, weight_two)


def finish_kernel(groups, dots_ref, b_ref, g_ref, image_ref, solution_ref, residual_ref):
    bb, b1, b2, s11, s12, s22 = [dots_ref[i : i + 1, :] for i in range(6)]
    square = bb + EPS
    rhs_length = jnp.sqrt(square)
    upper_left = (0.5 * bb + b1) / square
    shift = (0.5 * EPS - b1) / square
    one = jnp.maximum(shift * shift * bb + 2.0 * shift * b1 + s11, 0.0) / square
    lower_square = one + EPS
    lower_left = jnp.sqrt(lower_square)
    f_s = (shift * bb + b1) / (square * lower_left)
    f_gs = (shift * b1 + b2) / (square * lower_left)
    s_s = one / lower_square
    s_gs = (shift * shift * b1 + shift * b2 + shift * s11 + s12) / (square * lower_square)
    gs_gs = (shift * shift * s11 + 2.0 * shift * s12 + s22) / (square * lower_square)
    top_two = 0.5 * f_s + f_gs
    mid_two = 0.5 * s_s + s_gs
    rest = 0.5 * (EPS / lower_square) - s_gs
    two = (
        gs_gs
        + top_two * top_two * (bb / square)
        + rest * rest * s_s
        - 2.0 * top_two * f_gs
        + 2.0 * rest * s_gs
        - 2.0 * top_two * rest * f_s
    )
    lower_right = jnp.sqrt(jnp.maximum(two, 0.0) + EPS)
    weight_one, weight_two = least_squares(
        rhs_length, upper_left, lower_left, top_two, mid_two, lower_right
    )
    one_scale = weight_one / rhs_length
    two_scale = weight_two / (rhs_length * lower_left)
    sol_b = one_scale + two_scale * shift
    res_b = 1.0 - 0.5 * one_scale - 0.5 * two_scale * shift
    res_1 = one_scale + two_scale * (0.5 + shift)
    width = LANES // groups
    per = b_ref.shape[0]
    for k in range(per):
        b, g, image = b_ref[k], g_ref[k], image_ref[k]
        answer = sol_b * b + two_scale * g
        left = res_b * b - res_1 * g - two_scale * image
        for j in range(groups):
            cut = slice(j * width, (j + 1) * width)
            solution_ref[j * per + k] = answer[:, cut]
            residual_ref[j * per + k] = left[:, cut]


def finish(total, b_own, g_own, image, groups):
    part = jax.ShapeDtypeStruct((CL_DEV, B, LANES // groups), F32)
    return pl.pallas_call(
        functools.partial(finish_kernel, groups),
        out_shape=[part] * 2,
        in_specs=[VMEM_SPEC] * 4,
        out_specs=[VMEM_SPEC] * 2,
        compiler_params=pltpu.CompilerParams(vmem_limit_bytes=VMEM_LIMIT),
        cost_estimate=pl.CostEstimate(
            flops=8 * b_own.size, bytes_accessed=28 * b_own.size, transcendentals=0
        ),
        name="finish",
    )(total, b_own, g_own, image)


def swap_cores(value):
    size = lax.axis_size("far")
    return lax.ppermute(value, "far", [(i, i ^ 1) for i in range(size)])


def along_y(value, shift):
    size = lax.axis_size("far")
    return lax.ppermute(value, "far", [(i, (i + CORES * shift) % size) for i in range(size)])


def to_next(value):
    return lax.ppermute(value, "rows", [(i, i + 1) for i in range(lax.axis_size("rows") - 1)])


def to_previous(value):
    return lax.ppermute(value, "rows", [(i + 1, i) for i in range(lax.axis_size("rows") - 1)])


def sum_rows(value):
    size = lax.axis_size("rows")
    step = 1
    while step < size:
        value = value + lax.ppermute(value, "rows", [(i, i ^ step) for i in range(size)])
        step *= 2
    return value


def sum_far(keep, send):
    ys = lax.axis_size("far") // CORES
    got = swap_cores(send)
    mine = [keep[0], got[0]]
    for shift in range(1, ys):
        mine.append(along_y(keep[shift] + got[shift], shift))
    return mine


def shards(right_side, near_blocks, near_cols, far_src, far_tgt, far_left, far_right):
    far_size = lax.axis_size("far")
    ys = far_size // CORES
    q = REACH // far_size
    width = right_side.shape[1]
    groups = LANES * far_size // width
    core = lax.axis_index("far") % CORES
    cols = near_cols.reshape(-1)
    src, tgt = far_src.reshape(-1), far_tgt.reshape(-1)
    left = far_left.reshape(far_left.shape[1], B, R)
    right = far_right.reshape(far_right.shape[1], B, R)

    def exchange(coef):
        return lax.all_to_all(coef, "rows", split_axis=0, concat_axis=0, tiled=True)

    own = right_side.reshape(CL_DEV, B, width)
    part = REACH // CORES
    tail = lax.dynamic_slice_in_dim(own, CL_DEV - REACH + core * part, part, 0)
    head = lax.dynamic_slice_in_dim(own, core * part, part, 0)
    from_left, from_right = to_next(tail), to_previous(head)
    coef = exchange(coefficients([own], src, right, far_size))
    pieces = [own, from_left, from_right, swap_cores(from_left), swap_cores(from_right)]
    keep, send = operator(pieces, cols, tgt, near_blocks, coef, left, far_size, False)
    mine = sum(sum_far(keep, send))

    from_left, from_right = to_next(mine[q:]), to_previous(mine[:q])
    owns = [mine] + [along_y(mine, s) for s in range(1, ys)]
    owns += [swap_cores(item) for item in owns]
    coef = exchange(coefficients(owns, src, right, far_size))
    halos = [(from_left, from_right)]
    halos += [(along_y(from_left, s), along_y(from_right, s)) for s in range(1, ys)]
    halos += [(swap_cores(a), swap_cores(b)) for a, b in halos]
    pieces = owns + [item for pair in halos for item in pair]
    keep, send = operator(pieces, cols, tgt, near_blocks, coef, left, far_size, True)
    b_own, g_own = pack(own, owns, far_size)
    part_dots, image = dots(b_own, g_own, sum_far(keep, send), groups)
    answer, residual = finish(sum_rows(part_dots), b_own, g_own, image, groups)
    shape = (CL_DEV * B, width // far_size)
    return answer.reshape(shape), residual.reshape(shape)


def solution(mesh):
    return jax.shard_map(
        shards,
        mesh=mesh,
        in_specs=(
            P("rows", None),
            P("rows", "far", None, None),
            P("rows", "far"),
            P("rows", None, "far"),
            P("rows", None, "far"),
            P("rows", None, "far", None, None),
            P("rows", None, "far", None, None),
        ),
        out_specs=(P("rows", "far"), P("rows", "far")),
        check_vma=False,
    )
```

```python
import functools

import jax
import jax.numpy as jnp
from jax import lax
from jax.experimental import pallas as pl
from jax.experimental.pallas import tpu as pltpu
from jax.sharding import PartitionSpec as P

B = 128
R = 64
CL_DEV = 16
REACH = 8
CORES = 2
LANES = 128
ZERO = CL_DEV
EPS = 1e-06
F32 = jnp.float32
BF16 = jnp.bfloat16
VMEM_LIMIT = 48 * 1024 * 1024


VMEM_SPEC = pl.BlockSpec(memory_space=pltpu.VMEM)
SMEM_SPEC = pl.BlockSpec(memory_space=pltpu.SMEM)
ANY_SPEC = pl.BlockSpec(memory_space=pl.ANY)
PARAMS = pltpu.CompilerParams(vmem_limit_bytes=VMEM_LIMIT)


def split(value):
    high = value.astype(BF16)
    low = (value - high.astype(F32)).astype(BF16)
    return high, low


def dot3(left, right, dims=((1,), (0,))):
    (lh, ll), (rh, rl) = left, right
    dot = functools.partial(
        lax.dot_general, dimension_numbers=(dims, ((), ())), preferred_element_type=F32
    )
    return dot(lh, rh) + (dot(ll, rh) + dot(lh, rl))


def cost(flops, size):
    return pl.CostEstimate(flops=flops, bytes_accessed=size, transcendentals=0)


def place(far_size):
    index = lax.axis_index("far")
    return index // CORES, index % CORES, far_size // CORES


def owner_of(n, far_size):
    y, core, ys = place(far_size)
    shift, other = n % ys, n // ys
    return lax.rem(y - shift + ys, ys) * CORES + (1 - core if other else core)


def fetch(pairs, sems):
    copies = [pltpu.make_async_copy(a, b, sems.at[n]) for n, (a, b) in enumerate(pairs)]
    for copy in copies:
        copy.start()
    for copy in copies:
        copy.wait()


def cluster_at(half, j, k, per):
    return half * REACH + j * per + k


def prepare_kernel(far_size, right_ref, left_ref, b_ref, factors_ref, own_ref):
    for t in range(right_ref.shape[0]):
        factors_ref[0, t] = right_ref[t].T
        left = left_ref[t]
        factors_ref[1, t] = jnp.concatenate([left[: B // 2], left[B // 2 :]], axis=1)
    index = lax.axis_index("far")
    per = own_ref.shape[0] // 2
    packs = REACH // per
    width = LANES // packs
    for owner in range(far_size):

        @pl.when(index == owner)
        def _():
            for half in range(2):
                for k in range(per):
                    own_ref[half * per + k] = jnp.concatenate(
                        [
                            b_ref[cluster_at(half, j, k, per)][:, owner * width : (owner + 1) * width]
                            for j in range(packs)
                        ],
                        axis=1,
                    )


def prepare(right, left, own, far_size, per):
    groups = right.shape[0]
    return pl.pallas_call(
        functools.partial(prepare_kernel, far_size),
        grid=(1,),
        out_shape=[
            jax.ShapeDtypeStruct((2, groups, R, B), F32),
            jax.ShapeDtypeStruct((2 * per, B, LANES), F32),
        ],
        in_specs=[
            pl.BlockSpec(right.shape, lambda i: (0, 0, 0)),
            pl.BlockSpec(left.shape, lambda i: (0, 0, 0)),
            pl.BlockSpec(own.shape, lambda i: (0, 0, 0)),
        ],
        out_specs=[
            pl.BlockSpec((2, groups, R, B), lambda i: (0, 0, 0, 0)),
            pl.BlockSpec((2 * per, B, LANES), lambda i: (0, 0, 0)),
        ],
        compiler_params=PARAMS,
        cost_estimate=cost(0, 4 * own.size),
        name="prepare",
    )(right, left, own)


def coefficient_kernel(far_size, *refs):
    meta, factors = refs[:far_size], refs[far_size : 2 * far_size]
    fields = refs[2 * far_size : -5]
    out_ref, held, stage, high, low = refs[-5:]
    del held
    per = sum(f.shape[0] for f in fields) // 2
    packs = REACH // per
    width = LANES // packs
    entries = [f[k] for f in fields for k in range(f.shape[0])]
    for half in range(2):
        for k in range(per):
            entry = entries[half * per + k]
            for j in range(packs):
                h, l = split(entry[:, j * width : (j + 1) * width])
                high[cluster_at(half, j, k, per)] = h
                low[cluster_at(half, j, k, per)] = l
    depth = far_size // packs

    def group(t, carry):
        for e in range(depth):
            parts = []
            for j in range(packs):
                n = j * depth + e
                source = meta[n][0, t]
                parts.append(dot3(split(factors[n][0, t]), (high[source], low[source])))
            out_ref[t, e] = jnp.concatenate(parts, axis=1)
        return carry

    lax.fori_loop(0, out_ref.shape[0], group, 0)


def coefficients(meta, factors, fields, far_size):
    groups = factors[0].shape[1]
    per = sum(f.shape[0] for f in fields) // 2
    packs = REACH // per
    width = LANES // packs
    shape = (groups, far_size // packs, R, LANES)
    full = lambda a: pl.BlockSpec(a.shape, lambda i: (0,) * a.ndim)
    return pl.pallas_call(
        functools.partial(coefficient_kernel, far_size),
        grid=(1,),
        out_shape=jax.ShapeDtypeStruct(shape, F32),
        in_specs=[SMEM_SPEC] * far_size + [full(f) for f in factors] + [full(f) for f in fields],
        out_specs=pl.BlockSpec(shape, lambda i: (0, 0, 0, 0)),
        scratch_shapes=[
            pltpu.VMEM((8, LANES), F32),
            pltpu.VMEM((8, LANES), F32),
            pltpu.VMEM((CL_DEV, B, width), BF16),
            pltpu.VMEM((CL_DEV, B, width), BF16),
        ],
        compiler_params=PARAMS,
        cost_estimate=cost(6 * groups * far_size * R * B * width, 4 * 1024 * 1024),
        name="coefficients",
    )(*meta, *factors, *fields)


def far_kernel(far_size, *refs):
    meta, factors = refs[:far_size], refs[far_size : 2 * far_size]
    coef_ref, out_ref, total = refs[-3:]
    per = out_ref.shape[0] // 2
    packs = REACH // per
    width = LANES // packs
    depth = far_size // packs
    total[...] = jnp.zeros_like(total)

    def group(a, carry):
        for e in range(depth):
            here = coef_ref[a, e]
            for j in range(packs):
                n = j * depth + e
                dense = factors[n][1, a]
                left = jnp.concatenate([dense[:, :R], dense[:, R:]], axis=0)
                target = meta[n][1, a]
                total[target] += dot3(split(left), split(here[:, j * width : (j + 1) * width]))
        return carry

    lax.fori_loop(0, coef_ref.shape[0], group, 0)
    for half in range(2):
        for k in range(per):
            out_ref[half * per + k] = jnp.concatenate(
                [total[cluster_at(half, j, k, per)] for j in range(packs)], axis=1
            )


def far_part(meta, factors, coef, far_size, per):
    groups = coef.shape[0]
    width = LANES * per // REACH
    full = lambda a: pl.BlockSpec(a.shape, lambda i: (0,) * a.ndim)
    return pl.pallas_call(
        functools.partial(far_kernel, far_size),
        grid=(1,),
        out_shape=jax.ShapeDtypeStruct((2 * per, B, LANES), F32),
        in_specs=[SMEM_SPEC] * far_size + [full(f) for f in factors] + [full(coef)],
        out_specs=pl.BlockSpec((2 * per, B, LANES), lambda i: (0, 0, 0)),
        scratch_shapes=[pltpu.VMEM((CL_DEV, B, width), F32)],
        compiler_params=PARAMS,
        cost_estimate=cost(6 * groups * far_size * R * B * width, 4 * 1024 * 1024),
        name="far_part",
    )(*meta, *factors, coef)


def unpack(stage, per, put):
    far_size, halves = stage.shape[0], stage.shape[1]
    packs = REACH // per
    width = LANES // packs
    for half in range(halves):
        for k in range(per):
            for block in range(far_size // packs):
                entries = [stage[block * packs + i, half, k] for i in range(packs)]
                for j in range(packs):
                    value = jnp.concatenate(
                        [e[:, j * width : (j + 1) * width] for e in entries], axis=1
                    )
                    put(half, j * per + k, block * LANES, value)


def own_kernel(far_size, n_pieces, cols_ref, blocks_ref, *refs):
    pieces, (out_ref, high, low, stage, sems) = refs[:n_pieces], refs[n_pieces:]
    half, k = pl.program_id(0), pl.program_id(1)
    packs, slots = blocks_ref.shape[1], blocks_ref.shape[3]
    per = REACH // packs
    base = lax.axis_index("rows") * CL_DEV

    @pl.when((half == 0) & (k == 0))
    def _():
        if n_pieces == 1:
            fetch([(pieces[0], stage)], sems)
            for c in range(CL_DEV):
                high[c], low[c] = split(stage[c])
        else:
            pairs = []
            for n in range(far_size):
                owner = owner_of(n, far_size)
                for h in range(2):
                    pairs.append((pieces[2 * n + h], stage.at[owner, h]))
            fetch(pairs, sems)

            def put(h, c, lane, value):
                hi, lo = split(value)
                high[h * REACH + c, :, lane : lane + LANES] = hi
                low[h * REACH + c, :, lane : lane + LANES] = lo

            unpack(stage, per, put)
        high[ZERO] = jnp.zeros_like(high[ZERO])
        low[ZERO] = jnp.zeros_like(low[ZERO])

    for j in range(packs):
        cluster = cluster_at(half, j, k, per)
        at = []
        for s in range(slots):
            p = cols_ref[cluster * slots + s] - base
            at.append(jnp.where((p >= 0) & (p < CL_DEV), p, ZERO))
        left = split(jnp.concatenate([blocks_ref[0, j, 0, s] for s in range(slots)], axis=1))
        right = tuple(jnp.concatenate([ref[p] for p in at], axis=0) for ref in (high, low))
        out_ref[0, j, 0] = dot3(left, right)


def own_products(pieces, cols, blocks, far_size, width, per):
    packs = REACH // per
    slots = blocks.shape[1]
    if len(pieces) == 1:
        stage = pltpu.VMEM((CL_DEV, B, width), F32)
    else:
        stage = pltpu.VMEM((far_size, 2, per, B, LANES), F32)
    return pl.pallas_call(
        functools.partial(own_kernel, far_size, len(pieces)),
        out_shape=jax.ShapeDtypeStruct((2, packs, per, B, width), F32),
        grid=(2, per),
        in_specs=[
            SMEM_SPEC,
            pl.BlockSpec((1, packs, 1, slots, B, B), lambda h, k: (h, 0, k, 0, 0, 0)),
        ]
        + [ANY_SPEC] * len(pieces),
        out_specs=pl.BlockSpec((1, packs, 1, B, width), lambda h, k: (h, 0, k, 0, 0)),
        scratch_shapes=[
            pltpu.VMEM((CL_DEV + 1, B, width), BF16),
            pltpu.VMEM((CL_DEV + 1, B, width), BF16),
            stage,
            pltpu.SemaphoreType.DMA((len(pieces),)),
        ],
        compiler_params=PARAMS,
        cost_estimate=cost(6 * CL_DEV * slots * B * B * width, 4 * blocks.size),
        name="own_products",
    )(cols, blocks.reshape(2, packs, per, slots, B, B), *pieces)


def halo_kernel(far_size, last, n_pieces, cols_ref, blocks_ref, done_ref, *refs):
    pieces = refs[:n_pieces]
    ys = far_size // CORES
    keeps, sends = refs[n_pieces : n_pieces + ys], refs[n_pieces + ys : n_pieces + 2 * ys]
    high, low, stage, listed, sems = refs[n_pieces + 2 * ys :]
    half, k = pl.program_id(0), pl.program_id(1)
    packs, slots = blocks_ref.shape[1], blocks_ref.shape[3]
    per = REACH // packs
    y, core, _ = place(far_size)
    base = lax.axis_index("rows") * CL_DEV

    @pl.when((half == 0) & (k == 0))
    def _():
        if not last:
            part = REACH // CORES
            pairs = []
            for n, piece in enumerate(pieces):
                c = core if n < 2 else 1 - core
                pairs.append((piece, stage.at[pl.ds((n % 2) * REACH + c * part, part)]))
            fetch(pairs, sems)
            for c in range(2 * REACH):
                high[c], low[c] = split(stage[c])
        else:
            pairs = []
            for n in range(far_size):
                owner = owner_of(n, far_size)
                for h in range(2):
                    pairs.append((pieces[2 * n + h], stage.at[owner, h]))
            fetch(pairs, sems)

            def put(h, c, lane, value):
                hi, lo = split(value)
                high[h * REACH + c, :, lane : lane + LANES] = hi
                low[h * REACH + c, :, lane : lane + LANES] = lo

            unpack(stage, per, put)
        high[ZERO] = jnp.zeros_like(high[ZERO])
        low[ZERO] = jnp.zeros_like(low[ZERO])

    images = []
    for j in range(packs):
        cluster = cluster_at(half, j, k, per)
        count = jnp.int32(0)
        for s in range(slots):
            p = cols_ref[cluster * slots + s] - base
            listed[0, count] = s
            listed[1, count] = jnp.where(p < 0, p + REACH, p - CL_DEV + REACH)
            count = count + ((p < 0) | (p >= CL_DEV)).astype(jnp.int32)
        listed[0, count] = 0
        listed[1, count] = ZERO

        def two(i, total):
            s0, s1 = listed[0, 2 * i], listed[0, 2 * i + 1]
            p0, p1 = listed[1, 2 * i], listed[1, 2 * i + 1]
            left = split(jnp.concatenate([blocks_ref[0, j, 0, s0], blocks_ref[0, j, 0, s1]], axis=1))
            right = tuple(jnp.concatenate([ref[p0], ref[p1]], axis=0) for ref in (high, low))
            return total + dot3(left, right)

        images.append(lax.fori_loop(0, (count + 1) // 2, two, done_ref[0, j, 0]))

    width = LANES // packs
    for owner in range(far_size):
        packed = jnp.concatenate([im[:, owner * width : (owner + 1) * width] for im in images], axis=1)
        behind = lax.rem(owner // CORES - y + ys, ys)
        mine = owner % CORES == core
        for steps in range(ys):

            @pl.when(mine & (behind == steps))
            def _():
                keeps[steps][0] = packed

            @pl.when(jnp.logical_not(mine) & (behind == steps))
            def _():
                sends[steps][0] = packed


def with_halo(pieces, done, cols, blocks, far_size, last):
    _, packs, per, _, width = done.shape
    slots = blocks.shape[1]
    ys = far_size // CORES
    if last:
        stage = pltpu.VMEM((far_size, 2, per, B, LANES), F32)
    else:
        stage = pltpu.VMEM((2 * REACH, B, width), F32)
    outs = pl.pallas_call(
        functools.partial(halo_kernel, far_size, last, len(pieces)),
        out_shape=[jax.ShapeDtypeStruct((2 * per, B, LANES), F32)] * (2 * ys),
        grid=(2, per),
        in_specs=[
            SMEM_SPEC,
            pl.BlockSpec((1, packs, 1, slots, B, B), lambda h, k: (h, 0, k, 0, 0, 0)),
            pl.BlockSpec((1, packs, 1, B, width), lambda h, k: (h, 0, k, 0, 0)),
        ]
        + [ANY_SPEC] * len(pieces),
        out_specs=[pl.BlockSpec((1, B, LANES), lambda h, k: (h * per + k, 0, 0))] * (2 * ys),
        scratch_shapes=[
            pltpu.VMEM((CL_DEV + 1, B, width), BF16),
            pltpu.VMEM((CL_DEV + 1, B, width), BF16),
            stage,
            pltpu.SMEM((2, slots + 2), jnp.int32),
            pltpu.SemaphoreType.DMA((len(pieces),)),
        ],
        compiler_params=PARAMS,
        cost_estimate=cost(2 * CL_DEV * slots * B * B * width, 4 * blocks.size),
        name="with_halo",
    )(cols, blocks.reshape(2, packs, per, slots, B, B), done, *pieces)
    return outs[:ys], outs[ys:]


def add_kernel(n, *refs):
    parts, outs = refs[:n], refs[n:]
    total = parts[0][...]
    for part in parts[1:]:
        total = total + part[...]
    per = total.shape[0] // 2
    outs[0][...] = total[:per]
    outs[1][...] = total[per:]


def add_halves(parts):
    shape = parts[0].shape
    half = (shape[0] // 2,) + shape[1:]
    return pl.pallas_call(
        functools.partial(add_kernel, len(parts)),
        grid=(1,),
        out_shape=[jax.ShapeDtypeStruct(half, F32)] * 2,
        in_specs=[pl.BlockSpec(shape, lambda i: (0, 0, 0))] * len(parts),
        out_specs=[pl.BlockSpec(half, lambda i: (0, 0, 0))] * 2,
        compiler_params=PARAMS,
        cost_estimate=cost(4 * parts[0].size, 20 * parts[0].size),
        name="add_halves",
    )(*parts)


def dots_kernel(packs, n_parts, b_ref, gl_ref, gr_ref, *refs):
    parts, (out_ref, image_ref) = refs[:n_parts], refs[n_parts:]
    image = parts[0][...]
    for part in parts[1:]:
        image = image + part[...]
    image_ref[...] = image
    vectors = (b_ref[...], jnp.concatenate([gl_ref[...], gr_ref[...]], axis=0), image)
    width = LANES // packs
    rows = []
    for left, right in ((0, 0), (0, 1), (0, 2), (1, 1), (1, 2), (2, 2)):
        total = jnp.sum(vectors[left] * vectors[right], axis=0)
        total = jnp.sum(total, axis=0, keepdims=True)
        folded = total
        for g in range(1, packs):
            folded = folded + pltpu.roll(total, g * width, 1)
        rows.append(folded)
    rows.append(jnp.zeros((2, LANES), F32))
    out_ref[...] = jnp.concatenate(rows, axis=0)


def dots(b_own, g_own, parts, packs):
    full = lambda a: pl.BlockSpec(a.shape, lambda i: (0,) * a.ndim)
    return pl.pallas_call(
        functools.partial(dots_kernel, packs, len(parts)),
        grid=(1,),
        out_shape=[
            jax.ShapeDtypeStruct((8, LANES), F32),
            jax.ShapeDtypeStruct(b_own.shape, F32),
        ],
        in_specs=[full(a) for a in (b_own, *g_own, *parts)],
        out_specs=[pl.BlockSpec((8, LANES), lambda i: (0, 0)), full(b_own)],
        compiler_params=PARAMS,
        cost_estimate=cost(14 * b_own.size, 20 * b_own.size),
        name="dots",
    )(b_own, *g_own, *parts)


def least_squares(rhs_length, upper_left, lower_left, top_two, mid_two, lower_right):
    radius_one = jnp.sqrt(upper_left * upper_left + lower_left * lower_left)
    cosine_one = upper_left / radius_one
    sine_one = lower_left / radius_one
    rotated_top = cosine_one * rhs_length
    rotated_mid = -sine_one * rhs_length
    coupled = cosine_one * top_two + sine_one * mid_two
    diagonal_two = cosine_one * mid_two - sine_one * top_two
    radius_two = jnp.sqrt(diagonal_two * diagonal_two + lower_right * lower_right)
    weight_two = diagonal_two * rotated_mid / (radius_two * radius_two)
    weight_one = (rotated_top - coupled * weight_two) / radius_one
    return (weight_one, weight_two)


def finish_kernel(packs, dots_ref, b_ref, gl_ref, gr_ref, image_ref, solution_ref, residual_ref):
    bb, b1, b2, s11, s12, s22 = [dots_ref[i : i + 1, :] for i in range(6)]
    square = bb + EPS
    rhs_length = jnp.sqrt(square)
    upper_left = (0.5 * bb + b1) / square
    shift = (0.5 * EPS - b1) / square
    one = jnp.maximum(shift * shift * bb + 2.0 * shift * b1 + s11, 0.0) / square
    lower_square = one + EPS
    lower_left = jnp.sqrt(lower_square)
    f_s = (shift * bb + b1) / (square * lower_left)
    f_gs = (shift * b1 + b2) / (square * lower_left)
    s_s = one / lower_square
    s_gs = (shift * shift * b1 + shift * b2 + shift * s11 + s12) / (square * lower_square)
    gs_gs = (shift * shift * s11 + 2.0 * shift * s12 + s22) / (square * lower_square)
    top_two = 0.5 * f_s + f_gs
    mid_two = 0.5 * s_s + s_gs
    rest = 0.5 * (EPS / lower_square) - s_gs
    two = (
        gs_gs
        + top_two * top_two * (bb / square)
        + rest * rest * s_s
        - 2.0 * top_two * f_gs
        + 2.0 * rest * s_gs
        - 2.0 * top_two * rest * f_s
    )
    lower_right = jnp.sqrt(jnp.maximum(two, 0.0) + EPS)
    weight_one, weight_two = least_squares(
        rhs_length, upper_left, lower_left, top_two, mid_two, lower_right
    )
    one_scale = weight_one / rhs_length
    two_scale = weight_two / (rhs_length * lower_left)
    sol_b = one_scale + two_scale * shift
    res_b = 1.0 - 0.5 * one_scale - 0.5 * two_scale * shift
    res_1 = one_scale + two_scale * (0.5 + shift)
    width = LANES // packs
    per = REACH // packs
    for half, g_ref in enumerate((gl_ref, gr_ref)):
        for k in range(per):
            b, g, image = b_ref[half * per + k], g_ref[k], image_ref[half * per + k]
            answer = sol_b * b + two_scale * g
            left = res_b * b - res_1 * g - two_scale * image
            for j in range(packs):
                cut = slice(j * width, (j + 1) * width)
                solution_ref[cluster_at(half, j, k, per)] = answer[:, cut]
                residual_ref[cluster_at(half, j, k, per)] = left[:, cut]


def finish(total, b_own, g_own, image, packs):
    part = (CL_DEV, B, LANES // packs)
    full = lambda a: pl.BlockSpec(a.shape, lambda i: (0,) * a.ndim)
    return pl.pallas_call(
        functools.partial(finish_kernel, packs),
        grid=(1,),
        out_shape=[jax.ShapeDtypeStruct(part, F32)] * 2,
        in_specs=[full(a) for a in (total, b_own, *g_own, image)],
        out_specs=[pl.BlockSpec(part, lambda i: (0, 0, 0))] * 2,
        compiler_params=PARAMS,
        cost_estimate=cost(8 * b_own.size, 28 * b_own.size),
        name="finish",
    )(total, b_own, *g_own, image)


def swap_cores(value):
    size = lax.axis_size("far")
    return lax.ppermute(value, "far", [(i, i ^ 1) for i in range(size)])


def along_y(value, shift):
    size = lax.axis_size("far")
    return lax.ppermute(value, "far", [(i, (i + CORES * shift) % size) for i in range(size)])


def gather_far(value):
    ys = lax.axis_size("far") // CORES
    near = [value] + [along_y(value, s) for s in range(1, ys)]
    return near + [swap_cores(item) for item in near]


def to_next(value):
    return lax.ppermute(value, "rows", [(i, i + 1) for i in range(lax.axis_size("rows") - 1)])


def to_previous(value):
    return lax.ppermute(value, "rows", [(i + 1, i) for i in range(lax.axis_size("rows") - 1)])


def sum_rows(value):
    size = lax.axis_size("rows")
    step = 1
    while step < size:
        value = value + lax.ppermute(value, "rows", [(i, i ^ step) for i in range(size)])
        step *= 2
    return value


def exchange(coef):
    return lax.all_to_all(coef, "rows", split_axis=0, concat_axis=0, tiled=True)


def sum_far(keeps, sends):
    terms = [keeps[0]]
    for shift in range(1, len(keeps)):
        terms.append(along_y(keeps[shift] + swap_cores(sends[shift]), shift))
    return terms + [swap_cores(sends[0])]


def shards(right_side, near_blocks, near_cols, far_src, far_tgt, far_left, far_right):
    far_size = lax.axis_size("far")
    ys = far_size // CORES
    width = right_side.shape[1]
    packs = LANES * far_size // width
    per = REACH // packs
    core = lax.axis_index("far") % CORES
    cols = near_cols.reshape(-1)
    own = right_side.reshape(CL_DEV, B, width)
    groups = far_left.shape[1]

    part = REACH // CORES
    tail = lax.dynamic_slice_in_dim(own, CL_DEV - REACH + core * part, part, 0)
    head = lax.dynamic_slice_in_dim(own, core * part, part, 0)
    from_left, from_right = to_next(tail), to_previous(head)
    factors, b_own = prepare(
        far_right.reshape(groups, B, R), far_left.reshape(groups, B, R), own, far_size, per
    )
    meta = gather_far(jnp.stack([far_src.reshape(-1), far_tgt.reshape(-1)]))
    factors = gather_far(factors)
    done = own_products([own], cols, near_blocks, far_size, width, per)
    coef = exchange(coefficients(meta, factors, [b_own], far_size))
    pieces = [from_left, from_right, swap_cores(from_left), swap_cores(from_right)]
    keeps, sends = with_halo(pieces, done, cols, near_blocks, far_size, False)
    far = far_part(meta, factors, coef, far_size, per)
    g_own = add_halves(sum_far(keeps, sends) + [far])

    head, tail = g_own
    from_left, from_right = to_next(tail), to_previous(head)
    heads = [head] + [along_y(head, s) for s in range(1, ys)]
    tails = [tail] + [along_y(tail, s) for s in range(1, ys)]
    owns = [item for pair in zip(heads, tails) for item in pair]
    owns += [swap_cores(item) for item in owns]
    done = own_products(owns, cols, near_blocks, far_size, width, per)
    coef = exchange(coefficients(meta, factors, g_own, far_size))
    halos = [from_left, from_right]
    for s in range(1, ys):
        halos += [along_y(from_left, s), to_previous(heads[s])]
    halos += [swap_cores(item) for item in halos]
    keeps, sends = with_halo(halos, done, cols, near_blocks, far_size, True)
    far = far_part(meta, factors, coef, far_size, per)
    part_dots, image = dots(b_own, g_own, sum_far(keeps, sends) + [far], packs)
    answer, residual = finish(sum_rows(part_dots), b_own, g_own, image, packs)
    shape = (CL_DEV * B, width // far_size)
    return answer.reshape(shape), residual.reshape(shape)


def solution(mesh):
    return jax.shard_map(
        shards,
        mesh=mesh,
        in_specs=(
            P("rows", None),
            P("rows", "far", None, None),
            P("rows", "far"),
            P("rows", None, "far"),
            P("rows", None, "far"),
            P("rows", None, "far", None, None),
            P("rows", None, "far", None, None),
        ),
        out_specs=(P("rows", "far"), P("rows", "far")),
        check_vma=False,
    )
```

```python
import functools

import jax
import jax.numpy as jnp
from jax import lax
from jax.experimental import pallas as pl
from jax.experimental.pallas import tpu as pltpu
from jax.sharding import PartitionSpec as P

B = 128
R = 64
CL_DEV = 16
REACH = 8
CORES = 2
LANES = 128
EPS = 1e-06
F32 = jnp.float32
BF16 = jnp.bfloat16
VMEM_LIMIT = 54 * 1024 * 1024


VMEM_SPEC = pl.BlockSpec(memory_space=pltpu.VMEM)
SMEM_SPEC = pl.BlockSpec(memory_space=pltpu.SMEM)
ANY_SPEC = pl.BlockSpec(memory_space=pl.ANY)
PARAMS = pltpu.CompilerParams(vmem_limit_bytes=VMEM_LIMIT)


def split(value):
    high = value.astype(BF16)
    low = (value - high.astype(F32)).astype(BF16)
    return high, low


def dot3(left, right, dims=((1,), (0,))):
    (lh, ll), (rh, rl) = left, right
    dot = functools.partial(
        lax.dot_general, dimension_numbers=(dims, ((), ())), preferred_element_type=F32
    )
    return dot(lh, rh) + (dot(ll, rh) + dot(lh, rl))


def cost(flops, size):
    return pl.CostEstimate(flops=flops, bytes_accessed=size, transcendentals=0)


def place(far_size):
    index = lax.axis_index("far")
    return index // CORES, index % CORES, far_size // CORES


def owner_of(n, far_size):
    y, core, ys = place(far_size)
    shift, other = n % ys, n // ys
    return lax.rem(y - shift + ys, ys) * CORES + (1 - core if other else core)


def begin(pairs, sems, first=0):
    copies = [pltpu.make_async_copy(a, b, sems.at[first + n]) for n, (a, b) in enumerate(pairs)]
    for copy in copies:
        copy.start()
    return copies


def fetch(pairs, sems, first=0):
    for copy in begin(pairs, sems, first):
        copy.wait()


def buffers(arrays):
    return [pltpu.VMEM(a.shape, a.dtype) for a in arrays]


def cluster_at(half, j, k, per):
    return half * REACH + j * per + k


def pack_columns(far_size, per, source, out_ref):
    index = lax.axis_index("far")
    packs = REACH // per
    width = LANES // packs
    for owner in range(far_size):

        @pl.when(index == owner)
        def _():
            for half in range(2):
                for k in range(per):
                    out_ref[half * per + k] = jnp.concatenate(
                        [
                            source(cluster_at(half, j, k, per))[:, owner * width : (owner + 1) * width]
                            for j in range(packs)
                        ],
                        axis=1,
                    )


def pack_kernel(far_size, b_ref, out, field, own, sems):
    fetch([(b_ref, field)], sems)
    pack_columns(far_size, own.shape[0] // 2, lambda c: field[c], own)
    fetch([(own, out)], sems)


def pack(field, far_size, per):
    out = jax.ShapeDtypeStruct((2 * per, B, LANES), F32)
    return pl.pallas_call(
        functools.partial(pack_kernel, far_size),
        out_shape=out,
        in_specs=[ANY_SPEC],
        out_specs=ANY_SPEC,
        scratch_shapes=buffers([field, out]) + [pltpu.SemaphoreType.DMA((1,))],
        compiler_params=PARAMS,
        cost_estimate=cost(0, 8 * field.size),
        name="pack",
    )(field)


def coefficient_kernel(far_size, n_fields, *refs):
    meta, hbm = refs[:far_size], refs[far_size : 2 * far_size + n_fields]
    out, refs = refs[2 * far_size + n_fields], refs[2 * far_size + n_fields + 1 :]
    vmem, (held, high, low, sems) = refs[: far_size + n_fields], refs[far_size + n_fields :]
    copies = begin(list(zip(hbm, vmem)), sems)
    factors, fields = vmem[:far_size], vmem[far_size:]
    per = sum(f.shape[0] for f in fields) // 2
    packs = REACH // per
    width = LANES // packs
    for copy in copies[far_size:]:
        copy.wait()
    entries = [f[k] for f in fields for k in range(f.shape[0])]
    for half in range(2):
        for k in range(per):
            entry = entries[half * per + k]
            for j in range(packs):
                h, l = split(entry[:, j * width : (j + 1) * width])
                high[cluster_at(half, j, k, per)] = h
                low[cluster_at(half, j, k, per)] = l
    for copy in copies[:far_size]:
        copy.wait()
    depth = far_size // packs

    def group(t, carry):
        for e in range(depth):
            parts = []
            for j in range(packs):
                n = j * depth + e
                source = meta[n][0, t]
                parts.append(dot3(split(factors[n][t]), (high[source], low[source])))
            held[t, e] = jnp.concatenate(parts, axis=1)
        return carry

    lax.fori_loop(0, held.shape[0], group, 0)
    fetch([(held, out)], sems)


def coefficients(meta, factors, fields, far_size):
    groups = factors[0].shape[0]
    per = sum(f.shape[0] for f in fields) // 2
    packs = REACH // per
    width = LANES // packs
    out = jax.ShapeDtypeStruct((groups, far_size // packs, R, LANES), F32)
    return pl.pallas_call(
        functools.partial(coefficient_kernel, far_size, len(fields)),
        out_shape=out,
        in_specs=[SMEM_SPEC] * far_size + [ANY_SPEC] * (far_size + len(fields)),
        out_specs=ANY_SPEC,
        scratch_shapes=buffers([*factors, *fields, out])
        + [
            pltpu.VMEM((CL_DEV, B, width), BF16),
            pltpu.VMEM((CL_DEV, B, width), BF16),
            pltpu.SemaphoreType.DMA((far_size + len(fields),)),
        ],
        compiler_params=PARAMS,
        cost_estimate=cost(6 * groups * far_size * R * B * width, 4 * 1024 * 1024),
        name="coefficients",
    )(*meta, *factors, *fields)


def far_kernel(far_size, *refs):
    meta, hbm = refs[:far_size], refs[far_size : 2 * far_size + 1]
    out, refs = refs[2 * far_size + 1], refs[2 * far_size + 2 :]
    vmem, (held, total, sems) = refs[: far_size + 1], refs[far_size + 1 :]
    copies = begin(list(zip(hbm, vmem)), sems)
    factors, coef = vmem[:far_size], vmem[far_size]
    per = held.shape[0] // 2
    packs = REACH // per
    width = LANES // packs
    depth = far_size // packs
    total[...] = jnp.zeros_like(total)
    for copy in copies:
        copy.wait()

    def group(a, carry):
        for e in range(depth):
            for j in range(packs):
                n = j * depth + e
                here = coef[a, e][:, j * width : (j + 1) * width]
                target = meta[n][1, a]
                total[target] += dot3(split(factors[n][a]), split(here), ((0,), (0,)))
        return carry

    lax.fori_loop(0, coef.shape[0], group, 0)
    for half in range(2):
        for k in range(per):
            held[half * per + k] = jnp.concatenate(
                [total[cluster_at(half, j, k, per)] for j in range(packs)], axis=1
            )
    fetch([(held, out)], sems)


def far_part(meta, factors, coef, far_size, per):
    groups = coef.shape[0]
    width = LANES * per // REACH
    out = jax.ShapeDtypeStruct((2 * per, B, LANES), F32)
    return pl.pallas_call(
        functools.partial(far_kernel, far_size),
        out_shape=out,
        in_specs=[SMEM_SPEC] * far_size + [ANY_SPEC] * (far_size + 1),
        out_specs=ANY_SPEC,
        scratch_shapes=buffers([*factors, coef, out])
        + [pltpu.VMEM((CL_DEV, B, width), F32), pltpu.SemaphoreType.DMA((far_size + 1,))],
        compiler_params=PARAMS,
        cost_estimate=cost(6 * groups * far_size * R * B * width, 4 * 1024 * 1024),
        name="far_part",
    )(*meta, *factors, coef)


def unpack(stage, per, put):
    far_size, halves = stage.shape[0], stage.shape[1]
    packs = REACH // per
    width = LANES // packs
    for half in range(halves):
        for k in range(per):
            for block in range(far_size // packs):
                entries = [stage[block * packs + i, half, k] for i in range(packs)]
                for j in range(packs):
                    value = jnp.concatenate(
                        [e[:, j * width : (j + 1) * width] for e in entries], axis=1
                    )
                    put(half, j * per + k, block * LANES, value)


def store_split(high, low, first=0, after=0):
    def put(half, c, lane, value):
        place_ = (after if half else first) + c
        hi, lo = split(value)
        high[place_, :, lane : lane + LANES] = hi
        low[place_, :, lane : lane + LANES] = lo

    return put


def packed_pairs(pieces, far_size, stage):
    pairs = []
    for n in range(far_size):
        owner = owner_of(n, far_size)
        for half in range(2):
            pairs.append((pieces[2 * n + half], stage.at[owner, half]))
    return pairs


def operator_kernel(far_size, per, last, n_pieces, cols_ref, blocks_ref, *refs):
    pieces, refs = refs[:n_pieces], refs[n_pieces:]
    ys = far_size // CORES
    outs, refs = refs[: 2 * ys], refs[2 * ys :]
    high, low, own_stage, stage, held, own_sems, in_sems, out_sems = refs
    slots = cols_ref.shape[0]
    packs = REACH // per
    width = LANES // packs
    y, core, _ = place(far_size)
    base = lax.axis_index("rows") * CL_DEV - REACH

    if last:
        own_pairs = packed_pairs(pieces[: 2 * far_size], far_size, own_stage)
        halo_pairs = packed_pairs(pieces[2 * far_size :], far_size, stage)
    else:
        part = REACH // CORES
        own_pairs = [(pieces[0], own_stage)]
        halo_pairs = []
        for n, piece in enumerate(pieces[1:]):
            c = core if n < 2 else 1 - core
            halo_pairs.append((piece, stage.at[pl.ds((n % 2) * REACH + c * part, part)]))
    own_copies = begin(own_pairs, own_sems)
    halo_copies = begin(halo_pairs, in_sems)

    for copy in own_copies:
        copy.wait()
    if last:
        unpack(own_stage, per, store_split(high, low, REACH, 2 * REACH))
    else:
        for c in range(CL_DEV):
            high[REACH + c], low[REACH + c] = split(own_stage[c])
    for copy in halo_copies:
        copy.wait()
    if last:
        unpack(stage, per, store_split(high, low, 0, REACH + CL_DEV))
    else:
        for c in range(2 * REACH):
            at = c if c < REACH else CL_DEV + c
            high[at], low[at] = split(stage[c])

    def out_copies(entry):
        copies = []
        for n, out in enumerate(outs):
            taker = core if n < ys else 1 - core
            owner = lax.rem(y + n % ys, ys) * CORES + taker
            copies.append(
                pltpu.make_async_copy(held.at[owner, entry], out.at[entry], out_sems.at[n, entry])
            )
        return copies

    def step(entry, carry):
        half, k = entry // per, entry % per
        images = []
        for j in range(packs):
            cluster = cluster_at(half, j, k, per)
            at = [cols_ref[s, cluster] - base for s in range(slots)]
            right = tuple(jnp.concatenate([ref[p] for p in at], axis=0) for ref in (high, low))
            left = split(jnp.concatenate([blocks_ref[cluster, s] for s in range(slots)], axis=1))
            images.append(dot3(left, right))
        for owner in range(far_size):
            held[owner, entry] = jnp.concatenate(
                [im[:, owner * width : (owner + 1) * width] for im in images], axis=1
            )
        for copy in out_copies(entry):
            copy.start()
        return carry

    lax.fori_loop(0, 2 * per, step, 0, unroll=2)

    def drain(entry, carry):
        for copy in out_copies(entry):
            copy.wait()
        return carry

    lax.fori_loop(0, 2 * per, drain, 0)


def operator(blocks, pieces, cols, far_size, per, width, last):
    ys = far_size // CORES
    n_own = 2 * far_size if last else 1
    if last:
        stages = [pltpu.VMEM((far_size, 2, per, B, LANES), F32)] * 2
    else:
        stages = [pltpu.VMEM((CL_DEV, B, width), F32), pltpu.VMEM((2 * REACH, B, width), F32)]
    outs = pl.pallas_call(
        functools.partial(operator_kernel, far_size, per, last, len(pieces)),
        out_shape=[jax.ShapeDtypeStruct((2 * per, B, LANES), F32)] * (2 * ys),
        in_specs=[SMEM_SPEC, VMEM_SPEC] + [ANY_SPEC] * len(pieces),
        out_specs=[ANY_SPEC] * (2 * ys),
        scratch_shapes=[
            pltpu.VMEM((CL_DEV + 2 * REACH, B, width), BF16),
            pltpu.VMEM((CL_DEV + 2 * REACH, B, width), BF16),
            *stages,
            pltpu.VMEM((far_size, 2 * per, B, LANES), F32),
            pltpu.SemaphoreType.DMA((n_own,)),
            pltpu.SemaphoreType.DMA((len(pieces) - n_own,)),
            pltpu.SemaphoreType.DMA((2 * ys, 2 * per)),
        ],
        compiler_params=PARAMS,
        cost_estimate=cost(0, 0),
        name="operator",
    )(cols, blocks, *pieces)
    return outs[:ys], outs[ys:]


def add_kernel(n, *refs):
    hbm, outs, vmem, (first, second, sems) = refs[:n], refs[n : n + 2], refs[n + 2 : -3], refs[-3:]
    fetch(list(zip(hbm, vmem)), sems)
    total = vmem[0][...]
    for part in vmem[1:]:
        total = total + part[...]
    per = total.shape[0] // 2
    first[...] = total[:per]
    second[...] = total[per:]
    fetch([(first, outs[0]), (second, outs[1])], sems)


def add_halves(parts):
    shape = parts[0].shape
    half = jax.ShapeDtypeStruct((shape[0] // 2,) + shape[1:], F32)
    return pl.pallas_call(
        functools.partial(add_kernel, len(parts)),
        out_shape=[half] * 2,
        in_specs=[ANY_SPEC] * len(parts),
        out_specs=[ANY_SPEC] * 2,
        scratch_shapes=buffers(list(parts) + [half] * 2) + [pltpu.SemaphoreType.DMA((len(parts),))],
        compiler_params=PARAMS,
        cost_estimate=cost(4 * parts[0].size, 20 * parts[0].size),
        name="add_halves",
    )(*parts)


def dots_kernel(packs, n, *refs):
    hbm, (out, image_out), vmem = refs[:n], refs[n : n + 2], refs[n + 2 : 2 * n + 2]
    held, image_held, sems = refs[2 * n + 2 :]
    fetch(list(zip(hbm, vmem)), sems)
    b_ref, gl_ref, gr_ref, *parts = vmem
    image = parts[0][...]
    for part in parts[1:]:
        image = image + part[...]
    image_held[...] = image
    (image_copy,) = begin([(image_held, image_out)], sems)
    vectors = (b_ref[...], jnp.concatenate([gl_ref[...], gr_ref[...]], axis=0), image)
    width = LANES // packs
    rows = []
    for left, right in ((0, 0), (0, 1), (0, 2), (1, 1), (1, 2), (2, 2)):
        total = jnp.sum(vectors[left] * vectors[right], axis=0)
        total = jnp.sum(total, axis=0, keepdims=True)
        folded = total
        for g in range(1, packs):
            folded = folded + pltpu.roll(total, g * width, 1)
        rows.append(folded)
    rows.append(jnp.zeros((2, LANES), F32))
    held[...] = jnp.concatenate(rows, axis=0)
    fetch([(held, out)], sems, 1)
    image_copy.wait()


def dots(b_own, g_own, parts, packs):
    operands = (b_own, *g_own, *parts)
    outs = [jax.ShapeDtypeStruct((8, LANES), F32), jax.ShapeDtypeStruct(b_own.shape, F32)]
    return pl.pallas_call(
        functools.partial(dots_kernel, packs, len(operands)),
        out_shape=outs,
        in_specs=[ANY_SPEC] * len(operands),
        out_specs=[ANY_SPEC] * 2,
        scratch_shapes=buffers([*operands, *outs]) + [pltpu.SemaphoreType.DMA((len(operands),))],
        compiler_params=PARAMS,
        cost_estimate=cost(14 * b_own.size, 20 * b_own.size),
        name="dots",
    )(*operands)


def least_squares(rhs_length, upper_left, lower_left, top_two, mid_two, lower_right):
    radius_one = jnp.sqrt(upper_left * upper_left + lower_left * lower_left)
    cosine_one = upper_left / radius_one
    sine_one = lower_left / radius_one
    rotated_top = cosine_one * rhs_length
    rotated_mid = -sine_one * rhs_length
    coupled = cosine_one * top_two + sine_one * mid_two
    diagonal_two = cosine_one * mid_two - sine_one * top_two
    radius_two = jnp.sqrt(diagonal_two * diagonal_two + lower_right * lower_right)
    weight_two = diagonal_two * rotated_mid / (radius_two * radius_two)
    weight_one = (rotated_top - coupled * weight_two) / radius_one
    return (weight_one, weight_two)


def finish_kernel(packs, *refs):
    hbm, outs, vmem, (solution_ref, residual_ref, sems) = refs[:5], refs[5:7], refs[7:12], refs[12:]
    fetch(list(zip(hbm, vmem)), sems)
    dots_ref, b_ref, gl_ref, gr_ref, image_ref = vmem
    bb, b1, b2, s11, s12, s22 = [dots_ref[i : i + 1, :] for i in range(6)]
    square = bb + EPS
    rhs_length = jnp.sqrt(square)
    upper_left = (0.5 * bb + b1) / square
    shift = (0.5 * EPS - b1) / square
    one = jnp.maximum(shift * shift * bb + 2.0 * shift * b1 + s11, 0.0) / square
    lower_square = one + EPS
    lower_left = jnp.sqrt(lower_square)
    f_s = (shift * bb + b1) / (square * lower_left)
    f_gs = (shift * b1 + b2) / (square * lower_left)
    s_s = one / lower_square
    s_gs = (shift * shift * b1 + shift * b2 + shift * s11 + s12) / (square * lower_square)
    gs_gs = (shift * shift * s11 + 2.0 * shift * s12 + s22) / (square * lower_square)
    top_two = 0.5 * f_s + f_gs
    mid_two = 0.5 * s_s + s_gs
    rest = 0.5 * (EPS / lower_square) - s_gs
    two = (
        gs_gs
        + top_two * top_two * (bb / square)
        + rest * rest * s_s
        - 2.0 * top_two * f_gs
        + 2.0 * rest * s_gs
        - 2.0 * top_two * rest * f_s
    )
    lower_right = jnp.sqrt(jnp.maximum(two, 0.0) + EPS)
    weight_one, weight_two = least_squares(
        rhs_length, upper_left, lower_left, top_two, mid_two, lower_right
    )
    one_scale = weight_one / rhs_length
    two_scale = weight_two / (rhs_length * lower_left)
    sol_b = one_scale + two_scale * shift
    res_b = 1.0 - 0.5 * one_scale - 0.5 * two_scale * shift
    res_1 = one_scale + two_scale * (0.5 + shift)
    width = LANES // packs
    per = REACH // packs
    for half, g_ref in enumerate((gl_ref, gr_ref)):
        for k in range(per):
            b, g, image = b_ref[half * per + k], g_ref[k], image_ref[half * per + k]
            answer = sol_b * b + two_scale * g
            left = res_b * b - res_1 * g - two_scale * image
            for value, out_ref in ((answer, solution_ref), (left, residual_ref)):
                turned = value.T
                for j in range(packs):
                    at = cluster_at(half, j, k, per) * B
                    out_ref[:, at : at + B] = turned[j * width : (j + 1) * width]
    fetch([(solution_ref, outs[0]), (residual_ref, outs[1])], sems)


def finish(total, b_own, g_own, image, packs):
    operands = (total, b_own, *g_own, image)
    out = jax.ShapeDtypeStruct((LANES // packs, CL_DEV * B), F32)
    return pl.pallas_call(
        functools.partial(finish_kernel, packs),
        out_shape=[out] * 2,
        in_specs=[ANY_SPEC] * len(operands),
        out_specs=[ANY_SPEC] * 2,
        scratch_shapes=buffers([*operands, out, out])
        + [pltpu.SemaphoreType.DMA((len(operands),))],
        compiler_params=PARAMS,
        cost_estimate=cost(8 * b_own.size, 28 * b_own.size),
        name="finish",
    )(*operands)


def swap_cores(value):
    size = lax.axis_size("far")
    return lax.ppermute(value, "far", [(i, i ^ 1) for i in range(size)])


def along_y(value, shift):
    size = lax.axis_size("far")
    return lax.ppermute(value, "far", [(i, (i + CORES * shift) % size) for i in range(size)])


def along_all_y(value):
    return [value] + [along_y(value, s) for s in range(1, lax.axis_size("far") // CORES)]


def after(values, *earlier):
    flat = lax.optimization_barrier((tuple(values), earlier))
    return list(flat[0])


def to_next(value):
    return lax.ppermute(value, "rows", [(i, i + 1) for i in range(lax.axis_size("rows") - 1)])


def to_previous(value):
    return lax.ppermute(value, "rows", [(i + 1, i) for i in range(lax.axis_size("rows") - 1)])


def sum_rows(value):
    size = lax.axis_size("rows")
    step = 1
    while step < size:
        value = value + lax.ppermute(value, "rows", [(i, i ^ step) for i in range(size)])
        step *= 2
    return value


def exchange(coef):
    return lax.all_to_all(coef, "rows", split_axis=0, concat_axis=0, tiled=True)


def sum_far(keeps, sends, coef):
    terms = [keeps[0]]
    for shift in range(1, len(keeps)):
        got, coef = lax.optimization_barrier((swap_cores(sends[shift]), coef))
        terms.append(along_y(keeps[shift] + got, shift))
    return terms + [swap_cores(sends[0])], coef


def shards(right_side, near_blocks, near_cols, far_src, far_tgt, far_left, far_right):
    far_size = lax.axis_size("far")
    ys = far_size // CORES
    width = right_side.shape[1]
    packs = LANES * far_size // width
    per = REACH // packs
    core = lax.axis_index("far") % CORES
    cols = near_cols.T
    own = right_side.reshape(CL_DEV, B, width)
    groups = far_left.shape[1]

    part = REACH // CORES
    tail = lax.dynamic_slice_in_dim(own, CL_DEV - REACH + core * part, part, 0)
    head = lax.dynamic_slice_in_dim(own, core * part, part, 0)
    from_left, from_right = to_next(tail), to_previous(head)
    gathered = [
        item
        for value in (
            jnp.stack([far_src.reshape(-1), far_tgt.reshape(-1)]),
            far_right.reshape(groups, B, R).transpose(0, 2, 1),
            far_left.reshape(groups, B, R).transpose(0, 2, 1),
        )
        for item in along_all_y(value)
    ]
    b_own = pack(own, far_size, per)
    gathered = after(gathered, b_own)
    meta, rights, lefts = [
        part_ + [swap_cores(item) for item in part_]
        for part_ in (gathered[:ys], gathered[ys : 2 * ys], gathered[2 * ys :])
    ]
    coef = coefficients(meta, rights, [b_own], far_size)
    pieces = after([from_left, from_right], coef)
    pieces += [swap_cores(item) for item in pieces]
    coef = exchange(coef)
    keeps, sends = operator(near_blocks, [own] + pieces, cols, far_size, per, width, False)
    terms, coef = sum_far(keeps, sends, coef)
    g_own = add_halves(terms + [far_part(meta, lefts, coef, far_size, per)])

    head, tail = g_own
    from_left, from_right = to_next(tail), to_previous(head)
    heads, tails = along_all_y(head), along_all_y(tail)
    coef = coefficients(meta, rights, g_own, far_size)
    arrived = after([from_left, from_right] + heads[1:] + tails[1:], coef)
    from_left, from_right = arrived[:2]
    heads, tails = heads[:1] + arrived[2 : 1 + ys], tails[:1] + arrived[1 + ys :]
    halos = [from_left, from_right]
    for s in range(1, ys):
        halos += [along_y(from_left, s), to_previous(heads[s])]
    owns = [item for pair in zip(heads, tails) for item in pair]
    owns += [swap_cores(item) for item in owns]
    halos += [swap_cores(item) for item in halos]
    coef = exchange(coef)
    keeps, sends = operator(near_blocks, owns + halos, cols, far_size, per, width, True)
    terms, coef = sum_far(keeps, sends, coef)
    far = far_part(meta, lefts, coef, far_size, per)
    part_dots, image = dots(b_own, g_own, terms + [far], packs)
    answer, residual = finish(sum_rows(part_dots), b_own, g_own, image, packs)
    return answer.T, residual.T


def solution(mesh):
    return jax.shard_map(
        shards,
        mesh=mesh,
        in_specs=(
            P("rows", None),
            P("rows", "far", None, None),
            P("rows", "far"),
            P("rows", None, "far"),
            P("rows", None, "far"),
            P("rows", None, "far", None, None),
            P("rows", None, "far", None, None),
        ),
        out_specs=(P("rows", "far"), P("rows", "far")),
        check_vma=False,
    )
```

```python
import functools

import jax
import jax.numpy as jnp
from jax import lax
from jax.experimental import pallas as pl
from jax.experimental.pallas import tpu as pltpu
from jax.sharding import PartitionSpec as P

B = 128
R = 64
CL_DEV = 16
REACH = 8
CORES = 2
LANES = 128
EPS = 1e-06
F32 = jnp.float32
BF16 = jnp.bfloat16
VMEM_LIMIT = 16 * 1024 * 1024
WIDE_LIMIT = 60 * 1024 * 1024


VMEM_SPEC = pl.BlockSpec(memory_space=pltpu.VMEM)
SMEM_SPEC = pl.BlockSpec(memory_space=pltpu.SMEM)
ANY_SPEC = pl.BlockSpec(memory_space=pl.ANY)
PARAMS = pltpu.CompilerParams(vmem_limit_bytes=VMEM_LIMIT)
WIDE = pltpu.CompilerParams(vmem_limit_bytes=WIDE_LIMIT)


def split(value):
    high = value.astype(BF16)
    low = (value - high.astype(F32)).astype(BF16)
    return high, low


def dot3(left, right, dims=((1,), (0,))):
    (lh, ll), (rh, rl) = left, right
    dot = functools.partial(
        lax.dot_general, dimension_numbers=(dims, ((), ())), preferred_element_type=F32
    )
    return dot(lh, rh) + (dot(ll, rh) + dot(lh, rl))


def cost(flops, size):
    return pl.CostEstimate(flops=flops, bytes_accessed=size, transcendentals=0)


def place(far_size):
    index = lax.axis_index("far")
    return index // CORES, index % CORES, far_size // CORES


def owner_of(n, far_size):
    y, core, ys = place(far_size)
    shift, other = n % ys, n // ys
    return lax.rem(y - shift + ys, ys) * CORES + (1 - core if other else core)


def halo_parts(ys):
    part = REACH // CORES
    shared = max(1, part // ys)
    return part, shared, part - ys * shared


def begin(pairs, sems, first=0):
    copies = [pltpu.make_async_copy(a, b, sems.at[first + n]) for n, (a, b) in enumerate(pairs)]
    for copy in copies:
        copy.start()
    return copies


def fetch(pairs, sems, first=0):
    for copy in begin(pairs, sems, first):
        copy.wait()


def buffers(arrays):
    return [pltpu.VMEM(a.shape, a.dtype) for a in arrays]


def cluster_at(half, j, k, per):
    return half * REACH + j * per + k


def pack_columns(far_size, per, source, out_ref):
    index = lax.axis_index("far")
    packs = REACH // per
    width = LANES // packs
    for owner in range(far_size):

        @pl.when(index == owner)
        def _():
            for half in range(2):
                for k in range(per):
                    out_ref[half * per + k] = jnp.concatenate(
                        [
                            source(cluster_at(half, j, k, per))[:, owner * width : (owner + 1) * width]
                            for j in range(packs)
                        ],
                        axis=1,
                    )


def pack_kernel(far_size, b_ref, out, field, own, sems):
    fetch([(b_ref, field)], sems)
    pack_columns(far_size, own.shape[0] // 2, lambda c: field[c], own)
    fetch([(own, out)], sems)


def pack(field, far_size, per):
    out = jax.ShapeDtypeStruct((2 * per, B, LANES), F32)
    return pl.pallas_call(
        functools.partial(pack_kernel, far_size),
        out_shape=out,
        in_specs=[ANY_SPEC],
        out_specs=ANY_SPEC,
        scratch_shapes=buffers([field, out]) + [pltpu.SemaphoreType.DMA((1,))],
        compiler_params=PARAMS,
        cost_estimate=cost(0, 8 * field.size),
        name="pack",
    )(field)


def coefficient_kernel(far_size, n_fields, n_waits, *refs):
    refs = refs[: 2 * far_size + n_fields] + refs[2 * far_size + n_fields + n_waits :]
    meta, hbm = refs[:far_size], refs[far_size : 2 * far_size + n_fields]
    out, refs = refs[2 * far_size + n_fields], refs[2 * far_size + n_fields + 1 :]
    vmem, (held, high, low, sems) = refs[: far_size + n_fields], refs[far_size + n_fields :]
    groups = held.shape[0]
    hbm = [ref.at[pl.ds(0, groups)] for ref in hbm[:far_size]] + list(hbm[far_size:])
    copies = begin(list(zip(hbm, vmem)), sems)
    factors, fields = vmem[:far_size], vmem[far_size:]
    per = sum(f.shape[0] for f in fields) // 2
    packs = REACH // per
    width = LANES // packs
    for copy in copies[far_size:]:
        copy.wait()
    entries = [f[k] for f in fields for k in range(f.shape[0])]
    for half in range(2):
        for k in range(per):
            entry = entries[half * per + k]
            for j in range(packs):
                h, l = split(entry[:, j * width : (j + 1) * width])
                high[cluster_at(half, j, k, per)] = h
                low[cluster_at(half, j, k, per)] = l
    for copy in copies[:far_size]:
        copy.wait()
    depth = far_size // packs

    def group(t, carry):
        for e in range(depth):
            parts = []
            for j in range(packs):
                n = j * depth + e
                source = meta[n][0, t]
                parts.append(dot3(split(factors[n][t]), (high[source], low[source])))
            held[t, e] = jnp.concatenate(parts, axis=1)
        return carry

    lax.fori_loop(0, held.shape[0], group, 0, unroll=4)
    fetch([(held, out)], sems)


def coefficients(meta, factors, fields, far_size, waits=()):
    groups = factors[0].shape[0] // 2
    per = sum(f.shape[0] for f in fields) // 2
    packs = REACH // per
    width = LANES // packs
    out = jax.ShapeDtypeStruct((groups, far_size // packs, R, LANES), F32)
    return pl.pallas_call(
        functools.partial(coefficient_kernel, far_size, len(fields), len(waits)),
        out_shape=out,
        in_specs=[SMEM_SPEC] * far_size + [ANY_SPEC] * (far_size + len(fields) + len(waits)),
        out_specs=ANY_SPEC,
        scratch_shapes=[pltpu.VMEM((groups, R, B), F32)] * far_size
        + buffers([*fields, out])
        + [
            pltpu.VMEM((CL_DEV, B, width), BF16),
            pltpu.VMEM((CL_DEV, B, width), BF16),
            pltpu.SemaphoreType.DMA((far_size + len(fields),)),
        ],
        compiler_params=PARAMS,
        cost_estimate=cost(6 * groups * far_size * R * B * width, 4 * 1024 * 1024),
        name="coefficients",
    )(*meta, *factors, *fields, *waits)


def far_kernel(far_size, n_terms, *refs):
    n = far_size + 1 + n_terms
    meta, hbm, held = refs[:far_size], refs[far_size : far_size + n], refs[far_size + n]
    vmem, (total, sems) = refs[far_size + n + 1 : -2], refs[-2:]
    groups = vmem[0].shape[0]
    hbm = [ref.at[pl.ds(groups, groups)] for ref in hbm[:far_size]] + list(hbm[far_size:])
    copies = begin(list(zip(hbm, vmem)), sems)
    terms = vmem[far_size + 1 :]
    factors, coef = vmem[:far_size], vmem[far_size]
    per = held.shape[0] // 2
    packs = REACH // per
    width = LANES // packs
    depth = far_size // packs
    total[...] = jnp.zeros_like(total)
    for copy in copies:
        copy.wait()

    def group(a, carry):
        for e in range(depth):
            for j in range(packs):
                n = j * depth + e
                here = coef[a, e][:, j * width : (j + 1) * width]
                target = meta[n][1, a]
                total[target] += dot3(split(factors[n][a]), split(here), ((0,), (0,)))
        return carry

    lax.fori_loop(0, coef.shape[0], group, 0, unroll=4)
    for half in range(2):
        for k in range(per):
            value = jnp.concatenate(
                [total[cluster_at(half, j, k, per)] for j in range(packs)], axis=1
            )
            for term in terms:
                value = value + term[half * per + k]
            held[half * per + k] = value


def far_part(meta, factors, coef, terms, far_size, per):
    groups = coef.shape[0]
    width = LANES * per // REACH
    operands = [*factors, coef, *terms]
    return pl.pallas_call(
        functools.partial(far_kernel, far_size, len(terms)),
        out_shape=jax.ShapeDtypeStruct((2 * per, B, LANES), F32),
        in_specs=[SMEM_SPEC] * far_size + [ANY_SPEC] * len(operands),
        out_specs=VMEM_SPEC,
        scratch_shapes=[pltpu.VMEM((groups, R, B), F32)] * far_size
        + buffers([coef, *terms])
        + [pltpu.VMEM((CL_DEV, B, width), F32), pltpu.SemaphoreType.DMA((len(operands),))],
        compiler_params=PARAMS,
        cost_estimate=cost(6 * groups * far_size * R * B * width, 4 * 1024 * 1024),
        name="far_part",
    )(*meta, *operands)


def unpack(stage, per, put):
    far_size, halves = stage.shape[0], stage.shape[1]
    packs = REACH // per
    width = LANES // packs
    for half in range(halves):
        for k in range(per):
            for block in range(far_size // packs):
                entries = [stage[block * packs + i, half, k] for i in range(packs)]
                for j in range(packs):
                    value = jnp.concatenate(
                        [e[:, j * width : (j + 1) * width] for e in entries], axis=1
                    )
                    put(half, j * per + k, block * LANES, value)


def store_split(high, low, first=0, after=0):
    def put(half, c, lane, value):
        place_ = (after if half else first) + c
        hi, lo = split(value)
        high[place_, :, lane : lane + LANES] = hi
        low[place_, :, lane : lane + LANES] = lo

    return put


def packed_pairs(pieces, far_size, stage):
    pairs = []
    for n in range(far_size):
        owner = owner_of(n, far_size)
        for half in range(2):
            pairs.append((pieces[2 * n + half], stage.at[owner, half]))
    return pairs


def operator_kernel(far_size, per, last, n_pieces, cols_ref, blocks_ref, *refs):
    pieces, refs = refs[:n_pieces], refs[n_pieces:]
    ys = far_size // CORES
    outs, refs = refs[: 2 * ys], refs[2 * ys :]
    blocks, high, low, own_stage, stage, held, own_sems, in_sems, block_sems, out_sems = refs
    slots = cols_ref.shape[0]
    packs = REACH // per
    width = LANES // packs
    y, core, _ = place(far_size)
    base = lax.axis_index("rows") * CL_DEV - REACH

    if last:
        own_pairs = packed_pairs(pieces[: 2 * far_size], far_size, own_stage)
        halo_pairs = packed_pairs(pieces[2 * far_size :], far_size, stage)
    else:
        part, shared, direct = halo_parts(ys)
        own_pairs = [(pieces[0], own_stage)]
        halo_pairs = []
        each = (len(pieces) - 1) // CORES
        for n, piece in enumerate(pieces[1:]):
            turn, side = divmod(n % each, 2)
            first = side * REACH + (core if n < each else 1 - core) * part
            if turn < ys:
                first, count = first + lax.rem(y - turn + ys, ys) * shared, shared
            else:
                first, count = first + ys * shared, direct
            halo_pairs.append((piece, stage.at[pl.ds(first, count)]))
    own_copies = begin(own_pairs, own_sems)
    halo_copies = begin(halo_pairs, in_sems)

    for copy in own_copies:
        copy.wait()
    if last:
        unpack(own_stage, per, store_split(high, low, REACH, 2 * REACH))
    else:
        for c in range(CL_DEV):
            high[REACH + c], low[REACH + c] = split(own_stage[c])
    def block_copies(entry):
        half, k = entry // per, entry % per
        at = [cluster_at(half, j, k, per) for j in range(packs)]
        return [pltpu.make_async_copy(blocks_ref.at[c], blocks.at[c], block_sems.at[c]) for c in at]

    for copy in halo_copies:
        copy.wait()
    for entry in range(2 * per):
        for copy in block_copies(entry):
            copy.start()
    if last:
        unpack(stage, per, store_split(high, low, 0, REACH + CL_DEV))
    else:
        for c in range(2 * REACH):
            at = c if c < REACH else CL_DEV + c
            high[at], low[at] = split(stage[c])

    def out_copies(half):
        rows = pl.ds(half * per, per)
        copies = []
        for n, out in enumerate(outs):
            taker = core if n < ys else 1 - core
            owner = lax.rem(y + n % ys, ys) * CORES + taker
            copies.append(
                pltpu.make_async_copy(held.at[owner, rows], out.at[rows], out_sems.at[n, half])
            )
        return copies

    def step(entry, carry):
        half, k = entry // per, entry % per
        for copy in block_copies(entry):
            copy.wait()
        images = []
        for j in range(packs):
            cluster = cluster_at(half, j, k, per)
            at = [cols_ref[s, cluster] - base for s in range(slots)]
            right = tuple(jnp.concatenate([ref[p] for p in at], axis=0) for ref in (high, low))
            left = split(jnp.concatenate([blocks[cluster, s] for s in range(slots)], axis=1))
            images.append(dot3(left, right))
        for owner in range(far_size):
            held[owner, entry] = jnp.concatenate(
                [im[:, owner * width : (owner + 1) * width] for im in images], axis=1
            )
        return carry

    for half in range(2):
        lax.fori_loop(half * per, (half + 1) * per, step, 0, unroll=2)
        for copy in out_copies(half):
            copy.start()
    for half in range(2):
        for copy in out_copies(half):
            copy.wait()


def operator(blocks, pieces, cols, far_size, per, width, last):
    ys = far_size // CORES
    n_own = 2 * far_size if last else 1
    if last:
        stages = [pltpu.VMEM((far_size, 2, per, B, LANES), F32)] * 2
    else:
        stages = [pltpu.VMEM((CL_DEV, B, width), F32), pltpu.VMEM((2 * REACH, B, width), F32)]
    outs = pl.pallas_call(
        functools.partial(operator_kernel, far_size, per, last, len(pieces)),
        out_shape=[jax.ShapeDtypeStruct((2 * per, B, LANES), F32)] * (2 * ys),
        in_specs=[SMEM_SPEC] + [ANY_SPEC] * (1 + len(pieces)),
        out_specs=[ANY_SPEC] * (2 * ys),
        scratch_shapes=buffers([blocks])
        + [
            pltpu.VMEM((CL_DEV + 2 * REACH, B, width), BF16),
            pltpu.VMEM((CL_DEV + 2 * REACH, B, width), BF16),
            *stages,
            pltpu.VMEM((far_size, 2 * per, B, LANES), F32),
            pltpu.SemaphoreType.DMA((n_own,)),
            pltpu.SemaphoreType.DMA((len(pieces) - n_own,)),
            pltpu.SemaphoreType.DMA((CL_DEV,)),
            pltpu.SemaphoreType.DMA((2 * ys, 2)),
        ],
        compiler_params=WIDE,
        cost_estimate=cost(0, 0),
        name="operator",
    )(cols, blocks, *pieces)
    return outs[:ys], outs[ys:]


def add_kernel(n, *refs):
    parts, outs, (first, second, sems) = refs[:n], refs[n : n + 2], refs[n + 2 :]
    per = first.shape[0]
    copies = []
    for half, held in enumerate((first, second)):
        rows = slice(half * per, (half + 1) * per)
        total = parts[0][rows]
        for part in parts[1:]:
            total = total + part[rows]
        held[...] = total
        copies += begin([(held, outs[half])], sems, half)
    for copy in copies:
        copy.wait()


def add_halves(parts):
    shape = parts[0].shape
    half = jax.ShapeDtypeStruct((shape[0] // 2,) + shape[1:], F32)
    return pl.pallas_call(
        functools.partial(add_kernel, len(parts)),
        out_shape=[half] * 2,
        in_specs=[VMEM_SPEC] * len(parts),
        out_specs=[ANY_SPEC] * 2,
        scratch_shapes=buffers([half] * 2) + [pltpu.SemaphoreType.DMA((2,))],
        compiler_params=PARAMS,
        cost_estimate=cost(4 * parts[0].size, 20 * parts[0].size),
        name="add_halves",
    )(*parts)


PRODUCTS = ((0, 0), (0, 1), (0, 2), (1, 1), (1, 2), (2, 2))


def products(vectors, packs, chosen):
    width = LANES // packs
    rows = []
    for pair in PRODUCTS:
        if pair not in chosen:
            rows.append(jnp.zeros((1, LANES), F32))
            continue
        total = jnp.sum(vectors[pair[0]] * vectors[pair[1]], axis=0)
        total = jnp.sum(total, axis=0, keepdims=True)
        folded = total
        for g in range(1, packs):
            folded = folded + pltpu.roll(total, g * width, 1)
        rows.append(folded)
    rows.append(jnp.zeros((2, LANES), F32))
    return jnp.concatenate(rows, axis=0)


def early_kernel(packs, b_ref, gl_ref, gr_ref, out_ref):
    first = jnp.concatenate([gl_ref[...], gr_ref[...]], axis=0)
    out_ref[...] = products((b_ref[...], first), packs, ((0, 0), (0, 1), (1, 1)))


def early_dots(b_own, g_own, packs):
    return pl.pallas_call(
        functools.partial(early_kernel, packs),
        out_shape=jax.ShapeDtypeStruct((8, LANES), F32),
        in_specs=[VMEM_SPEC] * 3,
        out_specs=VMEM_SPEC,
        compiler_params=PARAMS,
        cost_estimate=cost(6 * b_own.size, 8 * b_own.size),
        name="early_dots",
    )(b_own, *g_own)


def dots_kernel(packs, b_ref, gl_ref, gr_ref, early_ref, *refs):
    parts, (out, image_ref, held, sems) = refs[:-4], refs[-4:]
    image = parts[0][...]
    for part in parts[1:]:
        image = image + part[...]
    image_ref[...] = image
    first = jnp.concatenate([gl_ref[...], gr_ref[...]], axis=0)
    late = products((b_ref[...], first, image), packs, ((0, 2), (1, 2), (2, 2)))
    held[...] = early_ref[...] + late
    fetch([(held, out)], sems)


def dots(b_own, g_own, early, parts, packs):
    operands = (b_own, *g_own, early, *parts)
    outs = [jax.ShapeDtypeStruct((8, LANES), F32), jax.ShapeDtypeStruct(b_own.shape, F32)]
    return pl.pallas_call(
        functools.partial(dots_kernel, packs),
        out_shape=outs,
        in_specs=[VMEM_SPEC] * len(operands),
        out_specs=[ANY_SPEC, VMEM_SPEC],
        scratch_shapes=buffers(outs[:1]) + [pltpu.SemaphoreType.DMA((1,))],
        compiler_params=PARAMS,
        cost_estimate=cost(8 * b_own.size, 20 * b_own.size),
        name="dots",
    )(*operands)


def least_squares(rhs_length, upper_left, lower_left, top_two, mid_two, lower_right):
    radius_one = jnp.sqrt(upper_left * upper_left + lower_left * lower_left)
    cosine_one = upper_left / radius_one
    sine_one = lower_left / radius_one
    rotated_top = cosine_one * rhs_length
    rotated_mid = -sine_one * rhs_length
    coupled = cosine_one * top_two + sine_one * mid_two
    diagonal_two = cosine_one * mid_two - sine_one * top_two
    radius_two = jnp.sqrt(diagonal_two * diagonal_two + lower_right * lower_right)
    weight_two = diagonal_two * rotated_mid / (radius_two * radius_two)
    weight_one = (rotated_top - coupled * weight_two) / radius_one
    return (weight_one, weight_two)


def finish_kernel(packs, *refs):
    mine_ref, other_ref, b_ref, gl_ref, gr_ref, image_ref = refs[:6]
    outs, (solution_ref, residual_ref, sems) = refs[6:8], refs[8:]
    total = mine_ref[...] + other_ref[...]
    bb, b1, b2, s11, s12, s22 = [total[i : i + 1, :] for i in range(6)]
    square = bb + EPS
    rhs_length = jnp.sqrt(square)
    upper_left = (0.5 * bb + b1) / square
    shift = (0.5 * EPS - b1) / square
    one = jnp.maximum(shift * shift * bb + 2.0 * shift * b1 + s11, 0.0) / square
    lower_square = one + EPS
    lower_left = jnp.sqrt(lower_square)
    f_s = (shift * bb + b1) / (square * lower_left)
    f_gs = (shift * b1 + b2) / (square * lower_left)
    s_s = one / lower_square
    s_gs = (shift * shift * b1 + shift * b2 + shift * s11 + s12) / (square * lower_square)
    gs_gs = (shift * shift * s11 + 2.0 * shift * s12 + s22) / (square * lower_square)
    top_two = 0.5 * f_s + f_gs
    mid_two = 0.5 * s_s + s_gs
    rest = 0.5 * (EPS / lower_square) - s_gs
    two = (
        gs_gs
        + top_two * top_two * (bb / square)
        + rest * rest * s_s
        - 2.0 * top_two * f_gs
        + 2.0 * rest * s_gs
        - 2.0 * top_two * rest * f_s
    )
    lower_right = jnp.sqrt(jnp.maximum(two, 0.0) + EPS)
    weight_one, weight_two = least_squares(
        rhs_length, upper_left, lower_left, top_two, mid_two, lower_right
    )
    one_scale = weight_one / rhs_length
    two_scale = weight_two / (rhs_length * lower_left)
    sol_b = one_scale + two_scale * shift
    res_b = 1.0 - 0.5 * one_scale - 0.5 * two_scale * shift
    res_1 = one_scale + two_scale * (0.5 + shift)
    width = LANES // packs
    per = REACH // packs
    for half, g_ref in enumerate((gl_ref, gr_ref)):
        for k in range(per):
            b, g, image = b_ref[half * per + k], g_ref[k], image_ref[half * per + k]
            answer = sol_b * b + two_scale * g
            left = res_b * b - res_1 * g - two_scale * image
            for value, out_ref in ((answer, solution_ref), (left, residual_ref)):
                turned = value.T
                for j in range(packs):
                    at = cluster_at(half, j, k, per) * B
                    out_ref[:, at : at + B] = turned[j * width : (j + 1) * width]
    fetch([(solution_ref, outs[0]), (residual_ref, outs[1])], sems)


def finish(totals, b_own, g_own, image, packs):
    operands = (*totals, b_own, *g_own, image)
    out = jax.ShapeDtypeStruct((LANES // packs, CL_DEV * B), F32)
    return pl.pallas_call(
        functools.partial(finish_kernel, packs),
        out_shape=[out] * 2,
        in_specs=[VMEM_SPEC] * len(operands),
        out_specs=[ANY_SPEC] * 2,
        scratch_shapes=buffers([out, out]) + [pltpu.SemaphoreType.DMA((2,))],
        compiler_params=PARAMS,
        cost_estimate=cost(8 * b_own.size, 28 * b_own.size),
        name="finish",
    )(*operands)


def hold_kernel(*refs):
    del refs


def hold(values):
    return list(
        pl.pallas_call(
            hold_kernel,
            out_shape=[jax.ShapeDtypeStruct(v.shape, v.dtype) for v in values],
            in_specs=[ANY_SPEC] * len(values),
            out_specs=[ANY_SPEC] * len(values),
            input_output_aliases={n: n for n in range(len(values))},
            compiler_params=PARAMS,
            cost_estimate=cost(4 * 10**10, 0),
            name="hold",
        )(*values)
    )


def swap_cores(value):
    size = lax.axis_size("far")
    return lax.ppermute(value, "far", [(i, i ^ 1) for i in range(size)])


def along_y(value, shift):
    size = lax.axis_size("far")
    return lax.ppermute(value, "far", [(i, (i + CORES * shift) % size) for i in range(size)])


def along_all_y(value):
    return [value] + [along_y(value, s) for s in range(1, lax.axis_size("far") // CORES)]


def after(values, *earlier):
    flat = lax.optimization_barrier((tuple(values), earlier))
    return list(flat[0])


def to_next(value):
    return lax.ppermute(value, "rows", [(i, i + 1) for i in range(lax.axis_size("rows") - 1)])


def to_previous(value):
    return lax.ppermute(value, "rows", [(i + 1, i) for i in range(lax.axis_size("rows") - 1)])


def sum_rows(value):
    size = lax.axis_size("rows")
    step = 1
    while True:
        other = lax.ppermute(value, "rows", [(i, i ^ step) for i in range(size)])
        step *= 2
        if step >= size:
            return value, other
        value = value + other


def exchange(coef):
    return lax.all_to_all(coef, "rows", split_axis=0, concat_axis=0, tiled=True)


def sum_far(keeps, sends, coef):
    others = []
    for shift in range(1, len(keeps)):
        got, coef = lax.optimization_barrier((swap_cores(sends[shift]), coef))
        others.append(along_y(keeps[shift] + got, shift))
    return [keeps[0], swap_cores(sends[0])], others, coef


def shards(right_side, near_blocks, near_cols, far_src, far_tgt, far_left, far_right):
    far_size = lax.axis_size("far")
    ys = far_size // CORES
    width = right_side.shape[1]
    packs = LANES * far_size // width
    per = REACH // packs
    core = lax.axis_index("far") % CORES
    cols = near_cols.T
    own = right_side.reshape(CL_DEV, B, width)
    groups = far_left.shape[1]

    part, shared, direct = halo_parts(ys)
    at = core * part
    turn = at + lax.axis_index("far") // CORES * shared

    def cut(first, count):
        return lax.dynamic_slice_in_dim(own, first, count, 0)

    ends = [to_next(cut(CL_DEV - REACH + turn, shared)), to_previous(cut(turn, shared))]
    meta = along_all_y(jnp.stack([far_src.reshape(-1), far_tgt.reshape(-1)]))
    factors = [f.reshape(groups, B, R).transpose(0, 2, 1) for f in (far_right, far_left)]
    factors = along_all_y(jnp.concatenate(factors, axis=0))
    b_own = pack(own, far_size, per)
    arrived = hold(ends + meta[1:])
    near, ends, meta = own, arrived[:2], meta[:1] + arrived[2:]
    pieces = list(ends)
    for s in range(1, ys):
        pieces += [along_y(item, s) for item in ends]
    if direct:
        first = at + ys * shared
        pieces += [
            to_next(lax.dynamic_slice_in_dim(near, CL_DEV - REACH + first, direct, 0)),
            to_previous(lax.dynamic_slice_in_dim(near, first, direct, 0)),
        ]
    meta, factors = [items + [swap_cores(item) for item in items] for items in (meta, factors)]
    coef = coefficients(meta, factors, [b_own], far_size)
    pieces = after(pieces, coef)
    pieces += [swap_cores(item) for item in pieces]
    coef = exchange(coef)
    keeps, sends = operator(near_blocks, [own] + pieces, cols, far_size, per, width, False)
    terms, others, coef = sum_far(keeps, sends, coef)
    g_own = add_halves([far_part(meta, factors, coef, terms, far_size, per)] + others)

    head, tail = g_own
    from_left, from_right = to_next(tail), to_previous(head)
    heads, tails = along_all_y(head), along_all_y(tail)
    coef = coefficients(meta, factors, g_own, far_size)
    arrived = after([from_left, from_right] + heads[1:] + tails[1:], coef)
    from_left, from_right = arrived[:2]
    heads, tails = heads[:1] + arrived[2 : 1 + ys], tails[:1] + arrived[1 + ys :]
    halos = [from_left, from_right]
    for s in range(1, ys):
        halos += [along_y(from_left, s), to_previous(heads[s])]
    owns = [item for pair in zip(heads, tails) for item in pair]
    owns += [swap_cores(item) for item in owns]
    halos += [swap_cores(item) for item in halos]
    coef = exchange(coef)
    keeps, sends = operator(near_blocks, owns + halos, cols, far_size, per, width, True)
    terms, others, coef = sum_far(keeps, sends, coef)
    base = far_part(meta, factors, coef, terms, far_size, per)
    early = early_dots(b_own, g_own, packs)
    part_dots, image = dots(b_own, g_own, early, [base] + others, packs)
    answer, residual = finish(sum_rows(part_dots), b_own, g_own, image, packs)
    return answer.T, residual.T


def solution(mesh):
    return jax.shard_map(
        shards,
        mesh=mesh,
        in_specs=(
            P("rows", None),
            P("rows", "far", None, None),
            P("rows", "far"),
            P("rows", None, "far"),
            P("rows", None, "far"),
            P("rows", None, "far", None, None),
            P("rows", None, "far", None, None),
        ),
        out_specs=(P("rows", "far"), P("rows", "far")),
        check_vma=False,
    )
```

```python
import functools

import jax
import jax.numpy as jnp
from jax import lax
from jax.experimental import pallas as pl
from jax.experimental.pallas import tpu as pltpu
from jax.sharding import PartitionSpec as P

B = 128
R = 64
CL_DEV = 16
REACH = 8
CORES = 2
LANES = 128
EPS = 1e-06
F32 = jnp.float32
BF16 = jnp.bfloat16
VMEM_LIMIT = 16 * 1024 * 1024
WIDE_LIMIT = 60 * 1024 * 1024


VMEM_SPEC = pl.BlockSpec(memory_space=pltpu.VMEM)
SMEM_SPEC = pl.BlockSpec(memory_space=pltpu.SMEM)
ANY_SPEC = pl.BlockSpec(memory_space=pl.ANY)
PARAMS = pltpu.CompilerParams(vmem_limit_bytes=VMEM_LIMIT)
WIDE = pltpu.CompilerParams(vmem_limit_bytes=WIDE_LIMIT)


def split(value):
    high = value.astype(BF16)
    low = (value - high.astype(F32)).astype(BF16)
    return high, low


def dot3(left, right, dims=((1,), (0,))):
    (lh, ll), (rh, rl) = left, right
    dot = functools.partial(
        lax.dot_general, dimension_numbers=(dims, ((), ())), preferred_element_type=F32
    )
    return dot(lh, rh) + (dot(ll, rh) + dot(lh, rl))


def cost(flops, size):
    return pl.CostEstimate(flops=flops, bytes_accessed=size, transcendentals=0)


def place(far_size):
    index = lax.axis_index("far")
    return index // CORES, index % CORES, far_size // CORES


def owner_of(n, far_size):
    y, core, ys = place(far_size)
    shift, other = n % ys, n // ys
    return lax.rem(y - shift + ys, ys) * CORES + (1 - core if other else core)


def halo_parts(ys):
    part = REACH // CORES
    shared = max(1, part // ys)
    return part, shared, part - ys * shared


def begin(pairs, sems, first=0):
    copies = [pltpu.make_async_copy(a, b, sems.at[first + n]) for n, (a, b) in enumerate(pairs)]
    for copy in copies:
        copy.start()
    return copies


def fetch(pairs, sems, first=0):
    for copy in begin(pairs, sems, first):
        copy.wait()


def buffers(arrays):
    return [pltpu.VMEM(a.shape, a.dtype) for a in arrays]


def cluster_at(half, j, k, per):
    return half * REACH + j * per + k


def pack_columns(far_size, per, source, out_ref):
    index = lax.axis_index("far")
    packs = REACH // per
    width = LANES // packs
    for owner in range(far_size):

        @pl.when(index == owner)
        def _():
            for half in range(2):
                for k in range(per):
                    out_ref[half * per + k] = jnp.concatenate(
                        [
                            source(cluster_at(half, j, k, per))[:, owner * width : (owner + 1) * width]
                            for j in range(packs)
                        ],
                        axis=1,
                    )


def pack_kernel(far_size, b_ref, out, field, own, sems):
    fetch([(b_ref, field)], sems)
    pack_columns(far_size, own.shape[0] // 2, lambda c: field[c], own)
    fetch([(own, out)], sems)


def pack(field, far_size, per):
    out = jax.ShapeDtypeStruct((2 * per, B, LANES), F32)
    return pl.pallas_call(
        functools.partial(pack_kernel, far_size),
        out_shape=out,
        in_specs=[ANY_SPEC],
        out_specs=ANY_SPEC,
        scratch_shapes=buffers([field, out]) + [pltpu.SemaphoreType.DMA((1,))],
        compiler_params=PARAMS,
        cost_estimate=cost(0, 8 * field.size),
        name="pack",
    )(field)


def coefficient_kernel(far_size, n_fields, n_waits, *refs):
    refs = refs[: 2 * far_size + n_fields] + refs[2 * far_size + n_fields + n_waits :]
    meta, hbm = refs[:far_size], refs[far_size : 2 * far_size + n_fields]
    out, refs = refs[2 * far_size + n_fields], refs[2 * far_size + n_fields + 1 :]
    vmem, (held, high, low, sems) = refs[: far_size + n_fields], refs[far_size + n_fields :]
    groups = held.shape[0]
    hbm = [ref.at[pl.ds(0, groups)] for ref in hbm[:far_size]] + list(hbm[far_size:])
    copies = begin(list(zip(hbm, vmem)), sems)
    factors, fields = vmem[:far_size], vmem[far_size:]
    per = sum(f.shape[0] for f in fields) // 2
    packs = REACH // per
    width = LANES // packs
    for copy in copies[far_size:]:
        copy.wait()
    entries = [f[k] for f in fields for k in range(f.shape[0])]
    for half in range(2):
        for k in range(per):
            entry = entries[half * per + k]
            for j in range(packs):
                h, l = split(entry[:, j * width : (j + 1) * width])
                high[cluster_at(half, j, k, per)] = h
                low[cluster_at(half, j, k, per)] = l
    for copy in copies[:far_size]:
        copy.wait()
    depth = far_size // packs

    def group(t, carry):
        for e in range(depth):
            parts = []
            for j in range(packs):
                n = j * depth + e
                source = meta[n][0, t]
                parts.append(dot3(split(factors[n][t]), (high[source], low[source])))
            held[t, e] = jnp.concatenate(parts, axis=1)
        return carry

    lax.fori_loop(0, held.shape[0], group, 0, unroll=4)
    fetch([(held, out)], sems)


def coefficients(meta, factors, fields, far_size, waits=()):
    groups = factors[0].shape[0] // 2
    per = sum(f.shape[0] for f in fields) // 2
    packs = REACH // per
    width = LANES // packs
    out = jax.ShapeDtypeStruct((groups, far_size // packs, R, LANES), F32)
    return pl.pallas_call(
        functools.partial(coefficient_kernel, far_size, len(fields), len(waits)),
        out_shape=out,
        in_specs=[SMEM_SPEC] * far_size + [ANY_SPEC] * (far_size + len(fields) + len(waits)),
        out_specs=ANY_SPEC,
        scratch_shapes=[pltpu.VMEM((groups, R, B), F32)] * far_size
        + buffers([*fields, out])
        + [
            pltpu.VMEM((CL_DEV, B, width), BF16),
            pltpu.VMEM((CL_DEV, B, width), BF16),
            pltpu.SemaphoreType.DMA((far_size + len(fields),)),
        ],
        compiler_params=PARAMS,
        cost_estimate=cost(6 * groups * far_size * R * B * width, 4 * 1024 * 1024),
        name="coefficients",
    )(*meta, *factors, *fields, *waits)


def far_kernel(far_size, n_terms, *refs):
    n = far_size + 1 + n_terms
    meta, hbm, held = refs[:far_size], refs[far_size : far_size + n], refs[far_size + n]
    vmem, (total, sems) = refs[far_size + n + 1 : -2], refs[-2:]
    groups = vmem[0].shape[0]
    hbm = [ref.at[pl.ds(groups, groups)] for ref in hbm[:far_size]] + list(hbm[far_size:])
    copies = begin(list(zip(hbm, vmem)), sems)
    terms = vmem[far_size + 1 :]
    factors, coef = vmem[:far_size], vmem[far_size]
    per = held.shape[0] // 2
    packs = REACH // per
    width = LANES // packs
    depth = far_size // packs
    total[...] = jnp.zeros_like(total)
    for copy in copies:
        copy.wait()

    def group(a, carry):
        for e in range(depth):
            for j in range(packs):
                n = j * depth + e
                here = coef[a, e][:, j * width : (j + 1) * width]
                target = meta[n][1, a]
                total[target] += dot3(split(factors[n][a]), split(here), ((0,), (0,)))
        return carry

    lax.fori_loop(0, coef.shape[0], group, 0, unroll=4)
    for half in range(2):
        for k in range(per):
            value = jnp.concatenate(
                [total[cluster_at(half, j, k, per)] for j in range(packs)], axis=1
            )
            for term in terms:
                value = value + term[half * per + k]
            held[half * per + k] = value


def far_part(meta, factors, coef, terms, far_size, per):
    groups = coef.shape[0]
    width = LANES * per // REACH
    operands = [*factors, coef, *terms]
    return pl.pallas_call(
        functools.partial(far_kernel, far_size, len(terms)),
        out_shape=jax.ShapeDtypeStruct((2 * per, B, LANES), F32),
        in_specs=[SMEM_SPEC] * far_size + [ANY_SPEC] * len(operands),
        out_specs=VMEM_SPEC,
        scratch_shapes=[pltpu.VMEM((groups, R, B), F32)] * far_size
        + buffers([coef, *terms])
        + [pltpu.VMEM((CL_DEV, B, width), F32), pltpu.SemaphoreType.DMA((len(operands),))],
        compiler_params=PARAMS,
        cost_estimate=cost(6 * groups * far_size * R * B * width, 4 * 1024 * 1024),
        name="far_part",
    )(*meta, *operands)


def unpack(stage, per, put):
    far_size, halves = stage.shape[0], stage.shape[1]
    packs = REACH // per
    width = LANES // packs
    for half in range(halves):
        for k in range(per):
            for block in range(far_size // packs):
                entries = [stage[block * packs + i, half, k] for i in range(packs)]
                for j in range(packs):
                    value = jnp.concatenate(
                        [e[:, j * width : (j + 1) * width] for e in entries], axis=1
                    )
                    put(half, j * per + k, block * LANES, value)


def store_split(high, low, first=0, after=0):
    def put(half, c, lane, value):
        place_ = (after if half else first) + c
        hi, lo = split(value)
        high[place_, :, lane : lane + LANES] = hi
        low[place_, :, lane : lane + LANES] = lo

    return put


def packed_pairs(pieces, far_size, stage):
    pairs = []
    for n in range(far_size):
        owner = owner_of(n, far_size)
        for half in range(2):
            pairs.append((pieces[2 * n + half], stage.at[owner, half]))
    return pairs


def operator_kernel(far_size, per, last, n_pieces, cols_ref, blocks_ref, *refs):
    pieces, refs = refs[:n_pieces], refs[n_pieces:]
    ys = far_size // CORES
    outs, refs = refs[: 2 * ys], refs[2 * ys :]
    blocks, high, low, own_stage, stage, held, own_sems, in_sems, block_sems, out_sems = refs
    slots = cols_ref.shape[0]
    packs = REACH // per
    width = LANES // packs
    y, core, _ = place(far_size)
    base = lax.axis_index("rows") * CL_DEV - REACH

    if last:
        own_pairs = packed_pairs(pieces[: 2 * far_size], far_size, own_stage)
        halo_pairs = packed_pairs(pieces[2 * far_size :], far_size, stage)
    else:
        part, shared, direct = halo_parts(ys)
        own_pairs = [(pieces[0], own_stage)]
        halo_pairs = []
        each = (len(pieces) - 1) // CORES
        for n, piece in enumerate(pieces[1:]):
            turn, side = divmod(n % each, 2)
            first = side * REACH + (core if n < each else 1 - core) * part
            if turn < ys:
                first, count = first + lax.rem(y - turn + ys, ys) * shared, shared
            else:
                first, count = first + ys * shared, direct
            halo_pairs.append((piece, stage.at[pl.ds(first, count)]))
    own_copies = begin(own_pairs, own_sems)
    halo_copies = begin(halo_pairs, in_sems)

    def block_copies(entry):
        half, k = entry // per, entry % per
        at = [cluster_at(half, j, k, per) for j in range(packs)]
        return [pltpu.make_async_copy(blocks_ref.at[c], blocks.at[c], block_sems.at[c]) for c in at]

    for copy in own_copies:
        copy.wait()
    for entry in range(2 * per):
        for copy in block_copies(entry):
            copy.start()
    if last:
        unpack(own_stage, per, store_split(high, low, REACH, 2 * REACH))
    else:
        for c in range(CL_DEV):
            high[REACH + c], low[REACH + c] = split(own_stage[c])
    for copy in halo_copies:
        copy.wait()
    if last:
        unpack(stage, per, store_split(high, low, 0, REACH + CL_DEV))
    else:
        for c in range(2 * REACH):
            at = c if c < REACH else CL_DEV + c
            high[at], low[at] = split(stage[c])

    chunk = max(1, per // 2)

    def out_copies(part):
        rows = pl.ds(part * chunk, chunk)
        copies = []
        for n, out in enumerate(outs):
            taker = core if n < ys else 1 - core
            owner = lax.rem(y + n % ys, ys) * CORES + taker
            copies.append(
                pltpu.make_async_copy(held.at[owner, rows], out.at[rows], out_sems.at[n, part])
            )
        return copies

    def step(entry, carry):
        half, k = entry // per, entry % per
        for copy in block_copies(entry):
            copy.wait()
        images = []
        for j in range(packs):
            cluster = cluster_at(half, j, k, per)
            at = [cols_ref[s, cluster] - base for s in range(slots)]
            right = tuple(jnp.concatenate([ref[p] for p in at], axis=0) for ref in (high, low))
            left = split(jnp.concatenate([blocks[cluster, s] for s in range(slots)], axis=1))
            images.append(dot3(left, right))
        for owner in range(far_size):
            held[owner, entry] = jnp.concatenate(
                [im[:, owner * width : (owner + 1) * width] for im in images], axis=1
            )
        return carry

    parts = 2 * per // chunk
    for part in range(parts):
        lax.fori_loop(part * chunk, (part + 1) * chunk, step, 0, unroll=True)
        for copy in out_copies(part):
            copy.start()
    for part in range(parts):
        for copy in out_copies(part):
            copy.wait()


def operator(blocks, pieces, cols, far_size, per, width, last):
    ys = far_size // CORES
    n_own = 2 * far_size if last else 1
    if last:
        stages = [pltpu.VMEM((far_size, 2, per, B, LANES), F32)] * 2
    else:
        stages = [pltpu.VMEM((CL_DEV, B, width), F32), pltpu.VMEM((2 * REACH, B, width), F32)]
    outs = pl.pallas_call(
        functools.partial(operator_kernel, far_size, per, last, len(pieces)),
        out_shape=[jax.ShapeDtypeStruct((2 * per, B, LANES), F32)] * (2 * ys),
        in_specs=[SMEM_SPEC] + [ANY_SPEC] * (1 + len(pieces)),
        out_specs=[ANY_SPEC] * (2 * ys),
        scratch_shapes=buffers([blocks])
        + [
            pltpu.VMEM((CL_DEV + 2 * REACH, B, width), BF16),
            pltpu.VMEM((CL_DEV + 2 * REACH, B, width), BF16),
            *stages,
            pltpu.VMEM((far_size, 2 * per, B, LANES), F32),
            pltpu.SemaphoreType.DMA((n_own,)),
            pltpu.SemaphoreType.DMA((len(pieces) - n_own,)),
            pltpu.SemaphoreType.DMA((CL_DEV,)),
            pltpu.SemaphoreType.DMA((2 * ys, 2 * per // max(1, per // 2))),
        ],
        compiler_params=WIDE,
        cost_estimate=cost(0, 0),
        name="operator",
    )(cols, blocks, *pieces)
    return outs[:ys], outs[ys:]


def add_kernel(n, *refs):
    parts, outs, (first, second, sems) = refs[:n], refs[n : n + 2], refs[n + 2 :]
    per = first.shape[0]
    copies = []
    for half, held in enumerate((first, second)):
        rows = slice(half * per, (half + 1) * per)
        total = parts[0][rows]
        for part in parts[1:]:
            total = total + part[rows]
        held[...] = total
        copies += begin([(held, outs[half])], sems, half)
    for copy in copies:
        copy.wait()


def add_halves(parts):
    shape = parts[0].shape
    half = jax.ShapeDtypeStruct((shape[0] // 2,) + shape[1:], F32)
    return pl.pallas_call(
        functools.partial(add_kernel, len(parts)),
        out_shape=[half] * 2,
        in_specs=[VMEM_SPEC] * len(parts),
        out_specs=[ANY_SPEC] * 2,
        scratch_shapes=buffers([half] * 2) + [pltpu.SemaphoreType.DMA((2,))],
        compiler_params=PARAMS,
        cost_estimate=cost(4 * parts[0].size, 20 * parts[0].size),
        name="add_halves",
    )(*parts)


PRODUCTS = ((0, 0), (0, 1), (0, 2), (1, 1), (1, 2), (2, 2))


def products(vectors, packs, chosen):
    width = LANES // packs
    rows = []
    for pair in PRODUCTS:
        if pair not in chosen:
            rows.append(jnp.zeros((1, LANES), F32))
            continue
        total = jnp.sum(vectors[pair[0]] * vectors[pair[1]], axis=0)
        total = jnp.sum(total, axis=0, keepdims=True)
        folded = total
        for g in range(1, packs):
            folded = folded + pltpu.roll(total, g * width, 1)
        rows.append(folded)
    rows.append(jnp.zeros((2, LANES), F32))
    return jnp.concatenate(rows, axis=0)


def early_kernel(packs, b_ref, gl_ref, gr_ref, out_ref):
    first = jnp.concatenate([gl_ref[...], gr_ref[...]], axis=0)
    out_ref[...] = products((b_ref[...], first), packs, ((0, 0), (0, 1), (1, 1)))


def early_dots(b_own, g_own, packs):
    return pl.pallas_call(
        functools.partial(early_kernel, packs),
        out_shape=jax.ShapeDtypeStruct((8, LANES), F32),
        in_specs=[VMEM_SPEC] * 3,
        out_specs=VMEM_SPEC,
        compiler_params=PARAMS,
        cost_estimate=cost(6 * b_own.size, 8 * b_own.size),
        name="early_dots",
    )(b_own, *g_own)


def dots_kernel(packs, b_ref, gl_ref, gr_ref, early_ref, *refs):
    parts, (out, image_ref, held, sems) = refs[:-4], refs[-4:]
    image = parts[0][...]
    for part in parts[1:]:
        image = image + part[...]
    image_ref[...] = image
    first = jnp.concatenate([gl_ref[...], gr_ref[...]], axis=0)
    late = products((b_ref[...], first, image), packs, ((0, 2), (1, 2), (2, 2)))
    held[...] = early_ref[...] + late
    fetch([(held, out)], sems)


def dots(b_own, g_own, early, parts, packs):
    operands = (b_own, *g_own, early, *parts)
    outs = [jax.ShapeDtypeStruct((8, LANES), F32), jax.ShapeDtypeStruct(b_own.shape, F32)]
    return pl.pallas_call(
        functools.partial(dots_kernel, packs),
        out_shape=outs,
        in_specs=[VMEM_SPEC] * len(operands),
        out_specs=[ANY_SPEC, VMEM_SPEC],
        scratch_shapes=buffers(outs[:1]) + [pltpu.SemaphoreType.DMA((1,))],
        compiler_params=PARAMS,
        cost_estimate=cost(8 * b_own.size, 20 * b_own.size),
        name="dots",
    )(*operands)


def least_squares(rhs_length, upper_left, lower_left, top_two, mid_two, lower_right):
    radius_one = jnp.sqrt(upper_left * upper_left + lower_left * lower_left)
    cosine_one = upper_left / radius_one
    sine_one = lower_left / radius_one
    rotated_top = cosine_one * rhs_length
    rotated_mid = -sine_one * rhs_length
    coupled = cosine_one * top_two + sine_one * mid_two
    diagonal_two = cosine_one * mid_two - sine_one * top_two
    radius_two = jnp.sqrt(diagonal_two * diagonal_two + lower_right * lower_right)
    weight_two = diagonal_two * rotated_mid / (radius_two * radius_two)
    weight_one = (rotated_top - coupled * weight_two) / radius_one
    return (weight_one, weight_two)


def finish_kernel(packs, *refs):
    mine_ref, other_ref, b_ref, gl_ref, gr_ref, image_ref = refs[:6]
    outs, (solution_ref, residual_ref, sems) = refs[6:8], refs[8:]
    total = mine_ref[...] + other_ref[...]
    bb, b1, b2, s11, s12, s22 = [total[i : i + 1, :] for i in range(6)]
    square = bb + EPS
    rhs_length = jnp.sqrt(square)
    upper_left = (0.5 * bb + b1) / square
    shift = (0.5 * EPS - b1) / square
    one = jnp.maximum(shift * shift * bb + 2.0 * shift * b1 + s11, 0.0) / square
    lower_square = one + EPS
    lower_left = jnp.sqrt(lower_square)
    f_s = (shift * bb + b1) / (square * lower_left)
    f_gs = (shift * b1 + b2) / (square * lower_left)
    s_s = one / lower_square
    s_gs = (shift * shift * b1 + shift * b2 + shift * s11 + s12) / (square * lower_square)
    gs_gs = (shift * shift * s11 + 2.0 * shift * s12 + s22) / (square * lower_square)
    top_two = 0.5 * f_s + f_gs
    mid_two = 0.5 * s_s + s_gs
    rest = 0.5 * (EPS / lower_square) - s_gs
    two = (
        gs_gs
        + top_two * top_two * (bb / square)
        + rest * rest * s_s
        - 2.0 * top_two * f_gs
        + 2.0 * rest * s_gs
        - 2.0 * top_two * rest * f_s
    )
    lower_right = jnp.sqrt(jnp.maximum(two, 0.0) + EPS)
    weight_one, weight_two = least_squares(
        rhs_length, upper_left, lower_left, top_two, mid_two, lower_right
    )
    one_scale = weight_one / rhs_length
    two_scale = weight_two / (rhs_length * lower_left)
    sol_b = one_scale + two_scale * shift
    res_b = 1.0 - 0.5 * one_scale - 0.5 * two_scale * shift
    res_1 = one_scale + two_scale * (0.5 + shift)
    width = LANES // packs
    per = REACH // packs
    for half, g_ref in enumerate((gl_ref, gr_ref)):
        for k in range(per):
            b, g, image = b_ref[half * per + k], g_ref[k], image_ref[half * per + k]
            answer = sol_b * b + two_scale * g
            left = res_b * b - res_1 * g - two_scale * image
            for value, out_ref in ((answer, solution_ref), (left, residual_ref)):
                turned = value.T
                for j in range(packs):
                    at = cluster_at(half, j, k, per) * B
                    out_ref[:, at : at + B] = turned[j * width : (j + 1) * width]
    fetch([(solution_ref, outs[0]), (residual_ref, outs[1])], sems)


def finish(totals, b_own, g_own, image, packs):
    operands = (*totals, b_own, *g_own, image)
    out = jax.ShapeDtypeStruct((LANES // packs, CL_DEV * B), F32)
    return pl.pallas_call(
        functools.partial(finish_kernel, packs),
        out_shape=[out] * 2,
        in_specs=[VMEM_SPEC] * len(operands),
        out_specs=[ANY_SPEC] * 2,
        scratch_shapes=buffers([out, out]) + [pltpu.SemaphoreType.DMA((2,))],
        compiler_params=PARAMS,
        cost_estimate=cost(8 * b_own.size, 28 * b_own.size),
        name="finish",
    )(*operands)


def hold_kernel(*refs):
    del refs


def hold(values):
    return list(
        pl.pallas_call(
            hold_kernel,
            out_shape=[jax.ShapeDtypeStruct(v.shape, v.dtype) for v in values],
            in_specs=[ANY_SPEC] * len(values),
            out_specs=[ANY_SPEC] * len(values),
            input_output_aliases={n: n for n in range(len(values))},
            compiler_params=PARAMS,
            cost_estimate=cost(4 * 10**10, 0),
            name="hold",
        )(*values)
    )


def swap_cores(value):
    size = lax.axis_size("far")
    return lax.ppermute(value, "far", [(i, i ^ 1) for i in range(size)])


def along_y(value, shift):
    size = lax.axis_size("far")
    return lax.ppermute(value, "far", [(i, (i + CORES * shift) % size) for i in range(size)])


def along_all_y(value):
    return [value] + [along_y(value, s) for s in range(1, lax.axis_size("far") // CORES)]


def after(values, *earlier):
    flat = lax.optimization_barrier((tuple(values), earlier))
    return list(flat[0])


def to_next(value):
    return lax.ppermute(value, "rows", [(i, i + 1) for i in range(lax.axis_size("rows") - 1)])


def to_previous(value):
    return lax.ppermute(value, "rows", [(i + 1, i) for i in range(lax.axis_size("rows") - 1)])


def sum_rows(value):
    size = lax.axis_size("rows")
    step = 1
    while True:
        other = lax.ppermute(value, "rows", [(i, i ^ step) for i in range(size)])
        step *= 2
        if step >= size:
            return value, other
        value = value + other


def exchange(coef):
    return lax.all_to_all(coef, "rows", split_axis=0, concat_axis=0, tiled=True)


def sum_far(keeps, sends, coef):
    others = []
    for shift in range(1, len(keeps)):
        got, coef = lax.optimization_barrier((swap_cores(sends[shift]), coef))
        others.append(along_y(keeps[shift] + got, shift))
    return [keeps[0], swap_cores(sends[0])], others, coef


def shards(right_side, near_blocks, near_cols, far_src, far_tgt, far_left, far_right):
    far_size = lax.axis_size("far")
    ys = far_size // CORES
    width = right_side.shape[1]
    packs = LANES * far_size // width
    per = REACH // packs
    core = lax.axis_index("far") % CORES
    cols = near_cols.T
    own = right_side.reshape(CL_DEV, B, width)
    groups = far_left.shape[1]

    factors = [f.reshape(groups, B, R).transpose(0, 2, 1) for f in (far_right, far_left)]
    part, shared, _ = halo_parts(ys)
    first = core * part + lax.axis_index("far") // CORES * shared
    ends = [
        to_next(lax.dynamic_slice_in_dim(own, CL_DEV - REACH + first, shared, 0)),
        to_previous(lax.dynamic_slice_in_dim(own, first, shared, 0)),
    ]
    meta = along_all_y(jnp.stack([far_src.reshape(-1), far_tgt.reshape(-1)]))
    factors = along_all_y(jnp.concatenate(factors, axis=0))
    b_own = pack(own, far_size, per)
    arrived = hold(ends + meta[1:])
    ends, meta = arrived[:2], meta[:1] + arrived[2:]
    pieces = list(ends)
    for s in range(1, ys):
        pieces += [along_y(item, s) for item in ends]
    meta, factors = [items + [swap_cores(item) for item in items] for items in (meta, factors)]
    coef = coefficients(meta, factors, [b_own], far_size)
    pieces = after(pieces, coef)
    pieces += [swap_cores(item) for item in pieces]
    coef = exchange(coef)
    keeps, sends = operator(near_blocks, [own] + pieces, cols, far_size, per, width, False)
    terms, others, coef = sum_far(keeps, sends, coef)
    g_own = add_halves([far_part(meta, factors, coef, terms, far_size, per)] + others)

    head, tail = g_own
    from_left, from_right = to_next(tail), to_previous(head)
    heads, tails = along_all_y(head), along_all_y(tail)
    coef = coefficients(meta, factors, g_own, far_size)
    arrived = after([from_left, from_right] + heads[1:] + tails[1:], coef)
    from_left, from_right = arrived[:2]
    heads, tails = heads[:1] + arrived[2 : 1 + ys], tails[:1] + arrived[1 + ys :]
    halos = [from_left, from_right]
    for s in range(1, ys):
        halos += [along_y(from_left, s), to_previous(heads[s])]
    owns = [item for pair in zip(heads, tails) for item in pair]
    owns += [swap_cores(item) for item in owns]
    halos += [swap_cores(item) for item in halos]
    coef = exchange(coef)
    keeps, sends = operator(near_blocks, owns + halos, cols, far_size, per, width, True)
    terms, others, coef = sum_far(keeps, sends, coef)
    base = far_part(meta, factors, coef, terms, far_size, per)
    early = early_dots(b_own, g_own, packs)
    part_dots, image = dots(b_own, g_own, early, [base] + others, packs)
    answer, residual = finish(sum_rows(part_dots), b_own, g_own, image, packs)
    return answer.T, residual.T


def solution(mesh):
    return jax.shard_map(
        shards,
        mesh=mesh,
        in_specs=(
            P("rows", None),
            P("rows", "far", None, None),
            P("rows", "far"),
            P("rows", None, "far"),
            P("rows", None, "far"),
            P("rows", None, "far", None, None),
            P("rows", None, "far", None, None),
        ),
        out_specs=(P("rows", "far"), P("rows", "far")),
        check_vma=False,
    )
```

```python
import functools

import jax
import jax.numpy as jnp
from jax import lax
from jax.experimental import pallas as pl
from jax.experimental.pallas import tpu as pltpu
from jax.sharding import PartitionSpec as P

B = 128
R = 64
CL_DEV = 16
REACH = 8
CORES = 2
LANES = 128
EPS = 1e-06
F32 = jnp.float32
BF16 = jnp.bfloat16
VMEM_LIMIT = 16 * 1024 * 1024
WIDE_LIMIT = 60 * 1024 * 1024


VMEM_SPEC = pl.BlockSpec(memory_space=pltpu.VMEM)
SMEM_SPEC = pl.BlockSpec(memory_space=pltpu.SMEM)
ANY_SPEC = pl.BlockSpec(memory_space=pl.ANY)
PARAMS = pltpu.CompilerParams(vmem_limit_bytes=VMEM_LIMIT)
WIDE = pltpu.CompilerParams(vmem_limit_bytes=WIDE_LIMIT)


def split(value):
    high = value.astype(BF16)
    low = (value - high.astype(F32)).astype(BF16)
    return high, low


def dot3(left, right, dims=((1,), (0,))):
    (lh, ll), (rh, rl) = left, right
    dot = functools.partial(
        lax.dot_general, dimension_numbers=(dims, ((), ())), preferred_element_type=F32
    )
    return dot(lh, rh) + (dot(ll, rh) + dot(lh, rl))


def cost(flops, size):
    return pl.CostEstimate(flops=flops, bytes_accessed=size, transcendentals=0)


def place(far_size):
    index = lax.axis_index("far")
    return index // CORES, index % CORES, far_size // CORES


def owner_of(n, far_size):
    y, core, ys = place(far_size)
    shift, other = n % ys, n // ys
    return lax.rem(y - shift + ys, ys) * CORES + (1 - core if other else core)


def halo_parts(ys):
    part = REACH // CORES
    shared = max(1, part // ys)
    return part, shared, part - ys * shared


def begin(pairs, sems, first=0):
    copies = [pltpu.make_async_copy(a, b, sems.at[first + n]) for n, (a, b) in enumerate(pairs)]
    for copy in copies:
        copy.start()
    return copies


def fetch(pairs, sems, first=0):
    for copy in begin(pairs, sems, first):
        copy.wait()


def buffers(arrays):
    return [pltpu.VMEM(a.shape, a.dtype) for a in arrays]


def cluster_at(half, j, k, per):
    return half * REACH + j * per + k


def pack_columns(far_size, per, source, out_ref):
    index = lax.axis_index("far")
    packs = REACH // per
    width = LANES // packs
    for owner in range(far_size):

        @pl.when(index == owner)
        def _():
            for half in range(2):
                for k in range(per):
                    out_ref[half * per + k] = jnp.concatenate(
                        [
                            source(cluster_at(half, j, k, per))[:, owner * width : (owner + 1) * width]
                            for j in range(packs)
                        ],
                        axis=1,
                    )


def pack_kernel(far_size, b_ref, out, field, own, sems):
    fetch([(b_ref, field)], sems)
    pack_columns(far_size, own.shape[0] // 2, lambda c: field[c], own)
    fetch([(own, out)], sems)


def pack(field, far_size, per):
    out = jax.ShapeDtypeStruct((2 * per, B, LANES), F32)
    return pl.pallas_call(
        functools.partial(pack_kernel, far_size),
        out_shape=out,
        in_specs=[ANY_SPEC],
        out_specs=ANY_SPEC,
        scratch_shapes=buffers([field, out]) + [pltpu.SemaphoreType.DMA((1,))],
        compiler_params=PARAMS,
        cost_estimate=cost(0, 8 * field.size),
        name="pack",
    )(field)


def coefficient_kernel(far_size, n_fields, n_waits, *refs):
    refs = refs[: 2 * far_size + n_fields] + refs[2 * far_size + n_fields + n_waits :]
    meta, hbm = refs[:far_size], refs[far_size : 2 * far_size + n_fields]
    out, refs = refs[2 * far_size + n_fields], refs[2 * far_size + n_fields + 1 :]
    vmem, (held, high, low, sems) = refs[: far_size + n_fields], refs[far_size + n_fields :]
    groups = held.shape[0]
    hbm = [ref.at[pl.ds(0, groups)] for ref in hbm[:far_size]] + list(hbm[far_size:])
    copies = begin(list(zip(hbm, vmem)), sems)
    factors, fields = vmem[:far_size], vmem[far_size:]
    per = sum(f.shape[0] for f in fields) // 2
    packs = REACH // per
    width = LANES // packs
    for copy in copies[far_size:]:
        copy.wait()
    entries = [f[k] for f in fields for k in range(f.shape[0])]
    for half in range(2):
        for k in range(per):
            entry = entries[half * per + k]
            for j in range(packs):
                h, l = split(entry[:, j * width : (j + 1) * width])
                high[cluster_at(half, j, k, per)] = h
                low[cluster_at(half, j, k, per)] = l
    for copy in copies[:far_size]:
        copy.wait()
    depth = far_size // packs

    def group(t, carry):
        for e in range(depth):
            parts = []
            for j in range(packs):
                n = j * depth + e
                source = meta[n][0, t]
                parts.append(dot3(split(factors[n][t]), (high[source], low[source])))
            held[t, e] = jnp.concatenate(parts, axis=1)
        return carry

    lax.fori_loop(0, held.shape[0], group, 0, unroll=4)
    fetch([(held, out)], sems)


def coefficients(meta, factors, fields, far_size, waits=()):
    groups = factors[0].shape[0] // 2
    per = sum(f.shape[0] for f in fields) // 2
    packs = REACH // per
    width = LANES // packs
    out = jax.ShapeDtypeStruct((groups, far_size // packs, R, LANES), F32)
    return pl.pallas_call(
        functools.partial(coefficient_kernel, far_size, len(fields), len(waits)),
        out_shape=out,
        in_specs=[SMEM_SPEC] * far_size + [ANY_SPEC] * (far_size + len(fields) + len(waits)),
        out_specs=ANY_SPEC,
        scratch_shapes=[pltpu.VMEM((groups, R, B), F32)] * far_size
        + buffers([*fields, out])
        + [
            pltpu.VMEM((CL_DEV, B, width), BF16),
            pltpu.VMEM((CL_DEV, B, width), BF16),
            pltpu.SemaphoreType.DMA((far_size + len(fields),)),
        ],
        compiler_params=PARAMS,
        cost_estimate=cost(6 * groups * far_size * R * B * width, 4 * 1024 * 1024),
        name="coefficients",
    )(*meta, *factors, *fields, *waits)


def far_kernel(far_size, n_terms, *refs):
    n = far_size + 1 + n_terms
    meta, hbm, held = refs[:far_size], refs[far_size : far_size + n], refs[far_size + n]
    vmem, (total, sems) = refs[far_size + n + 1 : -2], refs[-2:]
    groups = vmem[0].shape[0]
    hbm = [ref.at[pl.ds(groups, groups)] for ref in hbm[:far_size]] + list(hbm[far_size:])
    copies = begin(list(zip(hbm, vmem)), sems)
    terms = vmem[far_size + 1 :]
    factors, coef = vmem[:far_size], vmem[far_size]
    per = held.shape[0] // 2
    packs = REACH // per
    width = LANES // packs
    depth = far_size // packs
    total[...] = jnp.zeros_like(total)
    for copy in copies:
        copy.wait()

    def group(a, carry):
        for e in range(depth):
            for j in range(packs):
                n = j * depth + e
                here = coef[a, e][:, j * width : (j + 1) * width]
                target = meta[n][1, a]
                total[target] += dot3(split(factors[n][a]), split(here), ((0,), (0,)))
        return carry

    lax.fori_loop(0, coef.shape[0], group, 0, unroll=4)
    for half in range(2):
        for k in range(per):
            value = jnp.concatenate(
                [total[cluster_at(half, j, k, per)] for j in range(packs)], axis=1
            )
            for term in terms:
                value = value + term[half * per + k]
            held[half * per + k] = value


def far_part(meta, factors, coef, terms, far_size, per):
    groups = coef.shape[0]
    width = LANES * per // REACH
    operands = [*factors, coef, *terms]
    return pl.pallas_call(
        functools.partial(far_kernel, far_size, len(terms)),
        out_shape=jax.ShapeDtypeStruct((2 * per, B, LANES), F32),
        in_specs=[SMEM_SPEC] * far_size + [ANY_SPEC] * len(operands),
        out_specs=VMEM_SPEC,
        scratch_shapes=[pltpu.VMEM((groups, R, B), F32)] * far_size
        + buffers([coef, *terms])
        + [pltpu.VMEM((CL_DEV, B, width), F32), pltpu.SemaphoreType.DMA((len(operands),))],
        compiler_params=PARAMS,
        cost_estimate=cost(6 * groups * far_size * R * B * width, 4 * 1024 * 1024),
        name="far_part",
    )(*meta, *operands)


def unpack(stage, per, put):
    far_size, halves = stage.shape[0], stage.shape[1]
    packs = REACH // per
    width = LANES // packs
    for half in range(halves):
        for k in range(per):
            for block in range(far_size // packs):
                entries = [stage[block * packs + i, half, k] for i in range(packs)]
                for j in range(packs):
                    value = jnp.concatenate(
                        [e[:, j * width : (j + 1) * width] for e in entries], axis=1
                    )
                    put(half, j * per + k, block * LANES, value)


def store_split(high, low, first=0, after=0):
    def put(half, c, lane, value):
        place_ = (after if half else first) + c
        hi, lo = split(value)
        high[place_, :, lane : lane + LANES] = hi
        low[place_, :, lane : lane + LANES] = lo

    return put


def packed_pairs(pieces, far_size, stage):
    pairs = []
    for n in range(far_size):
        owner = owner_of(n, far_size)
        for half in range(2):
            pairs.append((pieces[2 * n + half], stage.at[owner, half]))
    return pairs


def operator_kernel(far_size, per, last, n_pieces, cols_ref, blocks_ref, *refs):
    pieces, refs = refs[:n_pieces], refs[n_pieces:]
    ys = far_size // CORES
    outs, refs = refs[: 2 * ys], refs[2 * ys :]
    blocks, high, low, own_stage, stage, held, own_sems, in_sems, block_sems, out_sems = refs
    slots = cols_ref.shape[0]
    packs = REACH // per
    width = LANES // packs
    y, core, _ = place(far_size)
    base = lax.axis_index("rows") * CL_DEV - REACH

    if last:
        own_pairs = packed_pairs(pieces[: 2 * far_size], far_size, own_stage)
        halo_pairs = packed_pairs(pieces[2 * far_size :], far_size, stage)
    else:
        part, shared, direct = halo_parts(ys)
        own_pairs = [(pieces[0], own_stage)]
        halo_pairs = []
        each = (len(pieces) - 1) // CORES
        for n, piece in enumerate(pieces[1:]):
            turn, side = divmod(n % each, 2)
            first = side * REACH + (core if n < each else 1 - core) * part
            if turn < ys:
                first, count = first + lax.rem(y - turn + ys, ys) * shared, shared
            else:
                first, count = first + ys * shared, direct
            halo_pairs.append((piece, stage.at[pl.ds(first, count)]))
    own_copies = begin(own_pairs, own_sems)
    halo_copies = begin(halo_pairs, in_sems)

    def block_copies(entry):
        half, k = entry // per, entry % per
        at = [cluster_at(half, j, k, per) for j in range(packs)]
        return [pltpu.make_async_copy(blocks_ref.at[c], blocks.at[c], block_sems.at[c]) for c in at]

    for copy in own_copies:
        copy.wait()
    for entry in range(2 * per):
        for copy in block_copies(entry):
            copy.start()
    if last:
        unpack(own_stage, per, store_split(high, low, REACH, 2 * REACH))
    else:
        for c in range(CL_DEV):
            high[REACH + c], low[REACH + c] = split(own_stage[c])
    for copy in halo_copies:
        copy.wait()
    if last:
        unpack(stage, per, store_split(high, low, 0, REACH + CL_DEV))
    else:
        for c in range(2 * REACH):
            at = c if c < REACH else CL_DEV + c
            high[at], low[at] = split(stage[c])

    chunk = max(1, per // 2)

    def out_copies(part):
        rows = pl.ds(part * chunk, chunk)
        copies = []
        for n, out in enumerate(outs):
            taker = core if n < ys else 1 - core
            owner = lax.rem(y + n % ys, ys) * CORES + taker
            copies.append(
                pltpu.make_async_copy(held.at[owner, rows], out.at[rows], out_sems.at[n, part])
            )
        return copies

    def step(entry, carry):
        half, k = entry // per, entry % per
        for copy in block_copies(entry):
            copy.wait()
        images = []
        for j in range(packs):
            cluster = cluster_at(half, j, k, per)
            at = [cols_ref[s, cluster] - base for s in range(slots)]
            right = tuple(jnp.concatenate([ref[p] for p in at], axis=0) for ref in (high, low))
            left = split(jnp.concatenate([blocks[cluster, s] for s in range(slots)], axis=1))
            images.append(dot3(left, right))
        for owner in range(far_size):
            held[owner, entry] = jnp.concatenate(
                [im[:, owner * width : (owner + 1) * width] for im in images], axis=1
            )
        return carry

    parts = 2 * per // chunk
    for part in range(parts):
        lax.fori_loop(part * chunk, (part + 1) * chunk, step, 0, unroll=True)
        for copy in out_copies(part):
            copy.start()
    for part in range(parts):
        for copy in out_copies(part):
            copy.wait()


def operator(blocks, pieces, cols, far_size, per, width, last):
    ys = far_size // CORES
    n_own = 2 * far_size if last else 1
    if last:
        stages = [pltpu.VMEM((far_size, 2, per, B, LANES), F32)] * 2
    else:
        stages = [pltpu.VMEM((CL_DEV, B, width), F32), pltpu.VMEM((2 * REACH, B, width), F32)]
    outs = pl.pallas_call(
        functools.partial(operator_kernel, far_size, per, last, len(pieces)),
        out_shape=[jax.ShapeDtypeStruct((2 * per, B, LANES), F32)] * (2 * ys),
        in_specs=[SMEM_SPEC] + [ANY_SPEC] * (1 + len(pieces)),
        out_specs=[ANY_SPEC] * (2 * ys),
        scratch_shapes=buffers([blocks])
        + [
            pltpu.VMEM((CL_DEV + 2 * REACH, B, width), BF16),
            pltpu.VMEM((CL_DEV + 2 * REACH, B, width), BF16),
            *stages,
            pltpu.VMEM((far_size, 2 * per, B, LANES), F32),
            pltpu.SemaphoreType.DMA((n_own,)),
            pltpu.SemaphoreType.DMA((len(pieces) - n_own,)),
            pltpu.SemaphoreType.DMA((CL_DEV,)),
            pltpu.SemaphoreType.DMA((2 * ys, 2 * per // max(1, per // 2))),
        ],
        compiler_params=WIDE,
        cost_estimate=cost(0, 0),
        name="operator",
    )(cols, blocks, *pieces)
    return outs[:ys], outs[ys:]


def add_kernel(half, n_whole, *refs):
    parts, (out, held, sems) = refs[:-3], refs[-3:]
    per = held.shape[0]
    total = parts[0][half * per : (half + 1) * per]
    for part in parts[1:n_whole]:
        total = total + part[half * per : (half + 1) * per]
    for part in parts[n_whole:]:
        total = total + part[...]
    held[...] = total
    fetch([(held, out)], sems)


def add_half(half, wholes, halves):
    out = jax.ShapeDtypeStruct(halves[0].shape, F32)
    parts = list(wholes) + list(halves)
    return pl.pallas_call(
        functools.partial(add_kernel, half, len(wholes)),
        out_shape=out,
        in_specs=[VMEM_SPEC] * len(parts),
        out_specs=ANY_SPEC,
        scratch_shapes=buffers([out]) + [pltpu.SemaphoreType.DMA((1,))],
        compiler_params=PARAMS,
        cost_estimate=cost(0, 0),
        name="add_half",
    )(*parts)


PRODUCTS = ((0, 0), (0, 1), (0, 2), (1, 1), (1, 2), (2, 2))


def products(vectors, packs, chosen):
    width = LANES // packs
    rows = []
    for pair in PRODUCTS:
        if pair not in chosen:
            rows.append(jnp.zeros((1, LANES), F32))
            continue
        total = jnp.sum(vectors[pair[0]] * vectors[pair[1]], axis=0)
        total = jnp.sum(total, axis=0, keepdims=True)
        folded = total
        for g in range(1, packs):
            folded = folded + pltpu.roll(total, g * width, 1)
        rows.append(folded)
    rows.append(jnp.zeros((2, LANES), F32))
    return jnp.concatenate(rows, axis=0)


def early_kernel(packs, b_ref, gl_ref, gr_ref, out_ref):
    first = jnp.concatenate([gl_ref[...], gr_ref[...]], axis=0)
    out_ref[...] = products((b_ref[...], first), packs, ((0, 0), (0, 1), (1, 1)))


def early_dots(b_own, g_own, packs):
    return pl.pallas_call(
        functools.partial(early_kernel, packs),
        out_shape=jax.ShapeDtypeStruct((8, LANES), F32),
        in_specs=[VMEM_SPEC] * 3,
        out_specs=VMEM_SPEC,
        compiler_params=PARAMS,
        cost_estimate=cost(6 * b_own.size, 8 * b_own.size),
        name="early_dots",
    )(b_own, *g_own)


def dots_kernel(packs, b_ref, gl_ref, gr_ref, early_ref, *refs):
    parts, (out, image_ref, held, sems) = refs[:-4], refs[-4:]
    image = parts[0][...]
    for part in parts[1:]:
        image = image + part[...]
    image_ref[...] = image
    first = jnp.concatenate([gl_ref[...], gr_ref[...]], axis=0)
    late = products((b_ref[...], first, image), packs, ((0, 2), (1, 2), (2, 2)))
    held[...] = early_ref[...] + late
    fetch([(held, out)], sems)


def dots(b_own, g_own, early, parts, packs):
    operands = (b_own, *g_own, early, *parts)
    outs = [jax.ShapeDtypeStruct((8, LANES), F32), jax.ShapeDtypeStruct(b_own.shape, F32)]
    return pl.pallas_call(
        functools.partial(dots_kernel, packs),
        out_shape=outs,
        in_specs=[VMEM_SPEC] * len(operands),
        out_specs=[ANY_SPEC, VMEM_SPEC],
        scratch_shapes=buffers(outs[:1]) + [pltpu.SemaphoreType.DMA((1,))],
        compiler_params=PARAMS,
        cost_estimate=cost(8 * b_own.size, 20 * b_own.size),
        name="dots",
    )(*operands)


def least_squares(rhs_length, upper_left, lower_left, top_two, mid_two, lower_right):
    radius_one = jnp.sqrt(upper_left * upper_left + lower_left * lower_left)
    cosine_one = upper_left / radius_one
    sine_one = lower_left / radius_one
    rotated_top = cosine_one * rhs_length
    rotated_mid = -sine_one * rhs_length
    coupled = cosine_one * top_two + sine_one * mid_two
    diagonal_two = cosine_one * mid_two - sine_one * top_two
    radius_two = jnp.sqrt(diagonal_two * diagonal_two + lower_right * lower_right)
    weight_two = diagonal_two * rotated_mid / (radius_two * radius_two)
    weight_one = (rotated_top - coupled * weight_two) / radius_one
    return (weight_one, weight_two)


def finish_kernel(packs, *refs):
    mine_ref, other_ref, b_ref, gl_ref, gr_ref, image_ref = refs[:6]
    outs, (solution_ref, residual_ref, sems) = refs[6:8], refs[8:]
    total = mine_ref[...] + other_ref[...]
    bb, b1, b2, s11, s12, s22 = [total[i : i + 1, :] for i in range(6)]
    square = bb + EPS
    rhs_length = jnp.sqrt(square)
    upper_left = (0.5 * bb + b1) / square
    shift = (0.5 * EPS - b1) / square
    one = jnp.maximum(shift * shift * bb + 2.0 * shift * b1 + s11, 0.0) / square
    lower_square = one + EPS
    lower_left = jnp.sqrt(lower_square)
    f_s = (shift * bb + b1) / (square * lower_left)
    f_gs = (shift * b1 + b2) / (square * lower_left)
    s_s = one / lower_square
    s_gs = (shift * shift * b1 + shift * b2 + shift * s11 + s12) / (square * lower_square)
    gs_gs = (shift * shift * s11 + 2.0 * shift * s12 + s22) / (square * lower_square)
    top_two = 0.5 * f_s + f_gs
    mid_two = 0.5 * s_s + s_gs
    rest = 0.5 * (EPS / lower_square) - s_gs
    two = (
        gs_gs
        + top_two * top_two * (bb / square)
        + rest * rest * s_s
        - 2.0 * top_two * f_gs
        + 2.0 * rest * s_gs
        - 2.0 * top_two * rest * f_s
    )
    lower_right = jnp.sqrt(jnp.maximum(two, 0.0) + EPS)
    weight_one, weight_two = least_squares(
        rhs_length, upper_left, lower_left, top_two, mid_two, lower_right
    )
    one_scale = weight_one / rhs_length
    two_scale = weight_two / (rhs_length * lower_left)
    sol_b = one_scale + two_scale * shift
    res_b = 1.0 - 0.5 * one_scale - 0.5 * two_scale * shift
    res_1 = one_scale + two_scale * (0.5 + shift)
    width = LANES // packs
    per = REACH // packs
    for half, g_ref in enumerate((gl_ref, gr_ref)):
        for k in range(per):
            b, g, image = b_ref[half * per + k], g_ref[k], image_ref[half * per + k]
            answer = sol_b * b + two_scale * g
            left = res_b * b - res_1 * g - two_scale * image
            for value, out_ref in ((answer, solution_ref), (left, residual_ref)):
                turned = value.T
                for j in range(packs):
                    at = cluster_at(half, j, k, per) * B
                    out_ref[:, at : at + B] = turned[j * width : (j + 1) * width]
    fetch([(solution_ref, outs[0]), (residual_ref, outs[1])], sems)


def finish(totals, b_own, g_own, image, packs):
    operands = (*totals, b_own, *g_own, image)
    out = jax.ShapeDtypeStruct((LANES // packs, CL_DEV * B), F32)
    return pl.pallas_call(
        functools.partial(finish_kernel, packs),
        out_shape=[out] * 2,
        in_specs=[VMEM_SPEC] * len(operands),
        out_specs=[ANY_SPEC] * 2,
        scratch_shapes=buffers([out, out]) + [pltpu.SemaphoreType.DMA((2,))],
        compiler_params=PARAMS,
        cost_estimate=cost(8 * b_own.size, 28 * b_own.size),
        name="finish",
    )(*operands)


def hold_kernel(*refs):
    del refs


def hold(values):
    return list(
        pl.pallas_call(
            hold_kernel,
            out_shape=[jax.ShapeDtypeStruct(v.shape, v.dtype) for v in values],
            in_specs=[ANY_SPEC] * len(values),
            out_specs=[ANY_SPEC] * len(values),
            input_output_aliases={n: n for n in range(len(values))},
            compiler_params=PARAMS,
            cost_estimate=cost(4 * 10**10, 0),
            name="hold",
        )(*values)
    )


def swap_cores(value):
    size = lax.axis_size("far")
    return lax.ppermute(value, "far", [(i, i ^ 1) for i in range(size)])


def along_y(value, shift):
    size = lax.axis_size("far")
    return lax.ppermute(value, "far", [(i, (i + CORES * shift) % size) for i in range(size)])


def along_all_y(value):
    return [value] + [along_y(value, s) for s in range(1, lax.axis_size("far") // CORES)]


def after(values, *earlier):
    flat = lax.optimization_barrier((tuple(values), earlier))
    return list(flat[0])


def to_next(value):
    return lax.ppermute(value, "rows", [(i, i + 1) for i in range(lax.axis_size("rows") - 1)])


def to_previous(value):
    return lax.ppermute(value, "rows", [(i + 1, i) for i in range(lax.axis_size("rows") - 1)])


def sum_rows(value):
    size = lax.axis_size("rows")
    step = 1
    while True:
        other = lax.ppermute(value, "rows", [(i, i ^ step) for i in range(size)])
        step *= 2
        if step >= size:
            return value, other
        value = value + other


def exchange(coef):
    return lax.all_to_all(coef, "rows", split_axis=0, concat_axis=0, tiled=True)


def sum_far(keeps, sends, coef, pieces):
    others = [[] for _ in range(pieces)]
    size = keeps[0].shape[0] // pieces
    for turn in range(1, len(keeps)):
        got, coef = lax.optimization_barrier((swap_cores(sends[turn]), coef))
        for n in range(pieces):
            rows = slice(n * size, (n + 1) * size)
            others[n].append(along_y(keeps[turn][rows] + got[rows], turn))
    return [keeps[0], swap_cores(sends[0])], others, coef


def shards(right_side, near_blocks, near_cols, far_src, far_tgt, far_left, far_right):
    far_size = lax.axis_size("far")
    ys = far_size // CORES
    width = right_side.shape[1]
    packs = LANES * far_size // width
    per = REACH // packs
    core = lax.axis_index("far") % CORES
    cols = near_cols.T
    own = right_side.reshape(CL_DEV, B, width)
    groups = far_left.shape[1]

    factors = [f.reshape(groups, B, R).transpose(0, 2, 1) for f in (far_right, far_left)]
    part, shared, _ = halo_parts(ys)
    first = core * part + lax.axis_index("far") // CORES * shared
    ends = [
        to_next(lax.dynamic_slice_in_dim(own, CL_DEV - REACH + first, shared, 0)),
        to_previous(lax.dynamic_slice_in_dim(own, first, shared, 0)),
    ]
    meta = along_all_y(jnp.stack([far_src.reshape(-1), far_tgt.reshape(-1)]))
    factors = along_all_y(jnp.concatenate(factors, axis=0))
    b_own = pack(own, far_size, per)
    arrived = hold(ends + meta[1:])
    ends, meta = arrived[:2], meta[:1] + arrived[2:]
    pieces = list(ends)
    for s in range(1, ys):
        pieces += [along_y(item, s) for item in ends]
    meta, factors = [items + [swap_cores(item) for item in items] for items in (meta, factors)]
    coef = coefficients(meta, factors, [b_own], far_size)
    pieces = after(pieces, coef)
    pieces += [swap_cores(item) for item in pieces]
    coef = exchange(coef)
    keeps, sends = operator(near_blocks, [own] + pieces, cols, far_size, per, width, False)
    terms, others, coef = sum_far(keeps, sends, coef, 2)
    base = far_part(meta, factors, coef, terms, far_size, per)
    g_own = [add_half(half, [base], others[half]) for half in range(2)]

    head, tail = g_own
    from_left, from_right = to_next(tail), to_previous(head)
    heads, tails = along_all_y(head), along_all_y(tail)
    coef = coefficients(meta, factors, g_own, far_size)
    arrived = after([from_left, from_right] + heads[1:] + tails[1:], coef)
    from_left, from_right = arrived[:2]
    heads, tails = heads[:1] + arrived[2 : 1 + ys], tails[:1] + arrived[1 + ys :]
    halos = [from_left, from_right]
    for s in range(1, ys):
        halos += [along_y(from_left, s), to_previous(heads[s])]
    owns = [item for pair in zip(heads, tails) for item in pair]
    owns += [swap_cores(item) for item in owns]
    halos += [swap_cores(item) for item in halos]
    coef = exchange(coef)
    keeps, sends = operator(near_blocks, owns + halos, cols, far_size, per, width, True)
    terms, (others,), coef = sum_far(keeps, sends, coef, 1)
    base = far_part(meta, factors, coef, terms, far_size, per)
    early = early_dots(b_own, g_own, packs)
    part_dots, image = dots(b_own, g_own, early, [base] + others, packs)
    answer, residual = finish(sum_rows(part_dots), b_own, g_own, image, packs)
    return answer.T, residual.T


def solution(mesh):
    return jax.shard_map(
        shards,
        mesh=mesh,
        in_specs=(
            P("rows", None),
            P("rows", "far", None, None),
            P("rows", "far"),
            P("rows", None, "far"),
            P("rows", None, "far"),
            P("rows", None, "far", None, None),
            P("rows", None, "far", None, None),
        ),
        out_specs=(P("rows", "far"), P("rows", "far")),
        check_vma=False,
    )
```

```python
import functools

import jax
import jax.numpy as jnp
from jax import lax
from jax.experimental import pallas as pl
from jax.experimental.pallas import tpu as pltpu
from jax.sharding import PartitionSpec as P

B = 128
R = 64
CL_DEV = 16
REACH = 8
CORES = 2
LANES = 128
EPS = 1e-06
F32 = jnp.float32
BF16 = jnp.bfloat16
VMEM_LIMIT = 16 * 1024 * 1024
WIDE_LIMIT = 60 * 1024 * 1024


VMEM_SPEC = pl.BlockSpec(memory_space=pltpu.VMEM)
SMEM_SPEC = pl.BlockSpec(memory_space=pltpu.SMEM)
ANY_SPEC = pl.BlockSpec(memory_space=pl.ANY)
PARAMS = pltpu.CompilerParams(vmem_limit_bytes=VMEM_LIMIT)
WIDE = pltpu.CompilerParams(vmem_limit_bytes=WIDE_LIMIT)


def split(value):
    high = value.astype(BF16)
    low = (value - high.astype(F32)).astype(BF16)
    return high, low


def dot3(left, right, dims=((1,), (0,))):
    (lh, ll), (rh, rl) = left, right
    dot = functools.partial(
        lax.dot_general, dimension_numbers=(dims, ((), ())), preferred_element_type=F32
    )
    return dot(lh, rh) + (dot(ll, rh) + dot(lh, rl))


def cost(flops, size):
    return pl.CostEstimate(flops=flops, bytes_accessed=size, transcendentals=0)


def place(far_size):
    index = lax.axis_index("far")
    return index // CORES, index % CORES, far_size // CORES


def owner_of(n, far_size):
    y, core, ys = place(far_size)
    shift, other = n % ys, n // ys
    return lax.rem(y - shift + ys, ys) * CORES + (1 - core if other else core)


def halo_parts(ys):
    part = REACH // CORES
    shared = max(1, part // ys)
    return part, shared, part - ys * shared


def begin(pairs, sems, first=0):
    copies = [pltpu.make_async_copy(a, b, sems.at[first + n]) for n, (a, b) in enumerate(pairs)]
    for copy in copies:
        copy.start()
    return copies


def fetch(pairs, sems, first=0):
    for copy in begin(pairs, sems, first):
        copy.wait()


def buffers(arrays):
    return [pltpu.VMEM(a.shape, a.dtype) for a in arrays]


def cluster_at(half, j, k, per):
    return half * REACH + j * per + k


def pack_columns(far_size, per, source, out_ref):
    index = lax.axis_index("far")
    packs = REACH // per
    width = LANES // packs
    for owner in range(far_size):

        @pl.when(index == owner)
        def _():
            for half in range(2):
                for k in range(per):
                    out_ref[half * per + k] = jnp.concatenate(
                        [
                            source(cluster_at(half, j, k, per))[:, owner * width : (owner + 1) * width]
                            for j in range(packs)
                        ],
                        axis=1,
                    )


def pack_kernel(far_size, b_ref, out, field, own, sems):
    fetch([(b_ref, field)], sems)
    pack_columns(far_size, own.shape[0] // 2, lambda c: field[c], own)
    fetch([(own, out)], sems)


def pack(field, far_size, per):
    out = jax.ShapeDtypeStruct((2 * per, B, LANES), F32)
    return pl.pallas_call(
        functools.partial(pack_kernel, far_size),
        out_shape=out,
        in_specs=[ANY_SPEC],
        out_specs=ANY_SPEC,
        scratch_shapes=buffers([field, out]) + [pltpu.SemaphoreType.DMA((1,))],
        compiler_params=PARAMS,
        cost_estimate=cost(0, 8 * field.size),
        name="pack",
    )(field)


def coefficient_kernel(far_size, n_fields, n_waits, *refs):
    refs = refs[: 2 * far_size + n_fields] + refs[2 * far_size + n_fields + n_waits :]
    meta, hbm = refs[:far_size], refs[far_size : 2 * far_size + n_fields]
    out, refs = refs[2 * far_size + n_fields], refs[2 * far_size + n_fields + 1 :]
    vmem, (held, high, low, sems) = refs[: far_size + n_fields], refs[far_size + n_fields :]
    copies = begin(list(zip(hbm, vmem)), sems)
    factors, fields = vmem[:far_size], vmem[far_size:]
    per = sum(f.shape[0] for f in fields) // 2
    packs = REACH // per
    width = LANES // packs
    for copy in copies[far_size:]:
        copy.wait()
    entries = [f[k] for f in fields for k in range(f.shape[0])]
    for half in range(2):
        for k in range(per):
            entry = entries[half * per + k]
            for j in range(packs):
                h, l = split(entry[:, j * width : (j + 1) * width])
                high[cluster_at(half, j, k, per)] = h
                low[cluster_at(half, j, k, per)] = l
    for copy in copies[:far_size]:
        copy.wait()
    depth = far_size // packs

    def group(t, carry):
        for e in range(depth):
            parts = []
            for j in range(packs):
                n = j * depth + e
                source = meta[n][0, t]
                parts.append(dot3(split(factors[n][t]), (high[source], low[source])))
            held[t, e] = jnp.concatenate(parts, axis=1)
        return carry

    lax.fori_loop(0, held.shape[0], group, 0, unroll=4)
    fetch([(held, out)], sems)


def coefficients(meta, factors, fields, far_size, waits=()):
    groups = factors[0].shape[0]
    per = sum(f.shape[0] for f in fields) // 2
    packs = REACH // per
    width = LANES // packs
    out = jax.ShapeDtypeStruct((groups, far_size // packs, R, LANES), F32)
    return pl.pallas_call(
        functools.partial(coefficient_kernel, far_size, len(fields), len(waits)),
        out_shape=out,
        in_specs=[SMEM_SPEC] * far_size + [ANY_SPEC] * (far_size + len(fields) + len(waits)),
        out_specs=ANY_SPEC,
        scratch_shapes=[pltpu.VMEM((groups, R, B), F32)] * far_size
        + buffers([*fields, out])
        + [
            pltpu.VMEM((CL_DEV, B, width), BF16),
            pltpu.VMEM((CL_DEV, B, width), BF16),
            pltpu.SemaphoreType.DMA((far_size + len(fields),)),
        ],
        compiler_params=PARAMS,
        cost_estimate=cost(6 * groups * far_size * R * B * width, 4 * 1024 * 1024),
        name="coefficients",
    )(*meta, *factors, *fields, *waits)


def far_kernel(far_size, n_terms, *refs):
    n = far_size + 1 + n_terms
    meta, hbm, held = refs[:far_size], refs[far_size : far_size + n], refs[far_size + n]
    vmem, (total, sems) = refs[far_size + n + 1 : -2], refs[-2:]
    copies = begin(list(zip(hbm, vmem)), sems)
    terms = vmem[far_size + 1 :]
    factors, coef = vmem[:far_size], vmem[far_size]
    per = held.shape[0] // 2
    packs = REACH // per
    width = LANES // packs
    depth = far_size // packs
    total[...] = jnp.zeros_like(total)
    for copy in copies:
        copy.wait()

    def group(a, carry):
        for e in range(depth):
            for j in range(packs):
                n = j * depth + e
                here = coef[a, e][:, j * width : (j + 1) * width]
                target = meta[n][1, a]
                total[target] += dot3(split(factors[n][a]), split(here), ((0,), (0,)))
        return carry

    lax.fori_loop(0, coef.shape[0], group, 0, unroll=4)
    for half in range(2):
        for k in range(per):
            value = jnp.concatenate(
                [total[cluster_at(half, j, k, per)] for j in range(packs)], axis=1
            )
            for term in terms:
                value = value + term[half * per + k]
            held[half * per + k] = value


def far_part(meta, factors, coef, terms, far_size, per):
    groups = coef.shape[0]
    width = LANES * per // REACH
    operands = [*factors, coef, *terms]
    return pl.pallas_call(
        functools.partial(far_kernel, far_size, len(terms)),
        out_shape=jax.ShapeDtypeStruct((2 * per, B, LANES), F32),
        in_specs=[SMEM_SPEC] * far_size + [ANY_SPEC] * len(operands),
        out_specs=VMEM_SPEC,
        scratch_shapes=[pltpu.VMEM((groups, R, B), F32)] * far_size
        + buffers([coef, *terms])
        + [pltpu.VMEM((CL_DEV, B, width), F32), pltpu.SemaphoreType.DMA((len(operands),))],
        compiler_params=PARAMS,
        cost_estimate=cost(6 * groups * far_size * R * B * width, 4 * 1024 * 1024),
        name="far_part",
    )(*meta, *operands)


def unpack(stage, per, put):
    far_size, halves = stage.shape[0], stage.shape[1]
    packs = REACH // per
    width = LANES // packs
    for half in range(halves):
        for k in range(per):
            for block in range(far_size // packs):
                entries = [stage[block * packs + i, half, k] for i in range(packs)]
                for j in range(packs):
                    value = jnp.concatenate(
                        [e[:, j * width : (j + 1) * width] for e in entries], axis=1
                    )
                    put(half, j * per + k, block * LANES, value)


def store_split(high, low, first=0, after=0):
    def put(half, c, lane, value):
        place_ = (after if half else first) + c
        hi, lo = split(value)
        high[place_, :, lane : lane + LANES] = hi
        low[place_, :, lane : lane + LANES] = lo

    return put


def packed_pairs(pieces, far_size, stage):
    pairs = []
    for n in range(far_size):
        owner = owner_of(n, far_size)
        for half in range(2):
            pairs.append((pieces[2 * n + half], stage.at[owner, half]))
    return pairs


def operator_kernel(far_size, per, last, n_pieces, cols_ref, blocks_ref, *refs):
    pieces, refs = refs[:n_pieces], refs[n_pieces:]
    ys = far_size // CORES
    outs, refs = refs[: 2 * ys], refs[2 * ys :]
    blocks, high, low, own_stage, stage, held, own_sems, in_sems, block_sems, out_sems = refs
    slots = cols_ref.shape[0]
    packs = REACH // per
    width = LANES // packs
    y, core, _ = place(far_size)
    base = lax.axis_index("rows") * CL_DEV - REACH

    if last:
        own_pairs = packed_pairs(pieces[: 2 * far_size], far_size, own_stage)
        halo_pairs = packed_pairs(pieces[2 * far_size :], far_size, stage)
    else:
        part, shared, direct = halo_parts(ys)
        own_pairs = [(pieces[0], own_stage)]
        halo_pairs = []
        each = (len(pieces) - 1) // CORES
        for n, piece in enumerate(pieces[1:]):
            turn, side = divmod(n % each, 2)
            first = side * REACH + (core if n < each else 1 - core) * part
            if turn < ys:
                first, count = first + lax.rem(y - turn + ys, ys) * shared, shared
            else:
                first, count = first + ys * shared, direct
            halo_pairs.append((piece, stage.at[pl.ds(first, count)]))
    own_copies = begin(own_pairs, own_sems)
    halo_copies = begin(halo_pairs, in_sems)

    def block_copies(entry):
        half, k = entry // per, entry % per
        at = [cluster_at(half, j, k, per) for j in range(packs)]
        return [pltpu.make_async_copy(blocks_ref.at[c], blocks.at[c], block_sems.at[c]) for c in at]

    for copy in own_copies:
        copy.wait()
    for entry in range(2 * per):
        for copy in block_copies(entry):
            copy.start()
    if last:
        unpack(own_stage, per, store_split(high, low, REACH, 2 * REACH))
    else:
        for c in range(CL_DEV):
            high[REACH + c], low[REACH + c] = split(own_stage[c])
    for copy in halo_copies:
        copy.wait()
    if last:
        unpack(stage, per, store_split(high, low, 0, REACH + CL_DEV))
    else:
        for c in range(2 * REACH):
            at = c if c < REACH else CL_DEV + c
            high[at], low[at] = split(stage[c])

    chunk = max(1, per // 2)

    def out_copies(part):
        rows = pl.ds(part * chunk, chunk)
        copies = []
        for n, out in enumerate(outs):
            taker = core if n < ys else 1 - core
            owner = lax.rem(y + n % ys, ys) * CORES + taker
            copies.append(
                pltpu.make_async_copy(held.at[owner, rows], out.at[rows], out_sems.at[n, part])
            )
        return copies

    def step(entry, carry):
        half, k = entry // per, entry % per
        for copy in block_copies(entry):
            copy.wait()
        images = []
        for j in range(packs):
            cluster = cluster_at(half, j, k, per)
            at = [cols_ref[s, cluster] - base for s in range(slots)]
            right = tuple(jnp.concatenate([ref[p] for p in at], axis=0) for ref in (high, low))
            left = split(jnp.concatenate([blocks[cluster, s] for s in range(slots)], axis=1))
            images.append(dot3(left, right))
        for owner in range(far_size):
            held[owner, entry] = jnp.concatenate(
                [im[:, owner * width : (owner + 1) * width] for im in images], axis=1
            )
        return carry

    parts = 2 * per // chunk
    for part in range(parts):
        lax.fori_loop(part * chunk, (part + 1) * chunk, step, 0, unroll=True)
        for copy in out_copies(part):
            copy.start()
    for part in range(parts):
        for copy in out_copies(part):
            copy.wait()


def operator(blocks, pieces, cols, far_size, per, width, last):
    ys = far_size // CORES
    n_own = 2 * far_size if last else 1
    if last:
        stages = [pltpu.VMEM((far_size, 2, per, B, LANES), F32)] * 2
    else:
        stages = [pltpu.VMEM((CL_DEV, B, width), F32), pltpu.VMEM((2 * REACH, B, width), F32)]
    outs = pl.pallas_call(
        functools.partial(operator_kernel, far_size, per, last, len(pieces)),
        out_shape=[jax.ShapeDtypeStruct((2 * per, B, LANES), F32)] * (2 * ys),
        in_specs=[SMEM_SPEC] + [ANY_SPEC] * (1 + len(pieces)),
        out_specs=[ANY_SPEC] * (2 * ys),
        scratch_shapes=buffers([blocks])
        + [
            pltpu.VMEM((CL_DEV + 2 * REACH, B, width), BF16),
            pltpu.VMEM((CL_DEV + 2 * REACH, B, width), BF16),
            *stages,
            pltpu.VMEM((far_size, 2 * per, B, LANES), F32),
            pltpu.SemaphoreType.DMA((n_own,)),
            pltpu.SemaphoreType.DMA((len(pieces) - n_own,)),
            pltpu.SemaphoreType.DMA((CL_DEV,)),
            pltpu.SemaphoreType.DMA((2 * ys, 2 * per // max(1, per // 2))),
        ],
        compiler_params=WIDE,
        cost_estimate=cost(0, 0),
        name="operator",
    )(cols, blocks, *pieces)
    return outs[:ys], outs[ys:]


def add_kernel(half, n_whole, *refs):
    parts, (out, held, sems) = refs[:-3], refs[-3:]
    per = held.shape[0]
    total = parts[0][half * per : (half + 1) * per]
    for part in parts[1:n_whole]:
        total = total + part[half * per : (half + 1) * per]
    for part in parts[n_whole:]:
        total = total + part[...]
    held[...] = total
    fetch([(held, out)], sems)


def add_half(half, wholes, halves):
    out = jax.ShapeDtypeStruct(halves[0].shape, F32)
    parts = list(wholes) + list(halves)
    return pl.pallas_call(
        functools.partial(add_kernel, half, len(wholes)),
        out_shape=out,
        in_specs=[VMEM_SPEC] * len(parts),
        out_specs=ANY_SPEC,
        scratch_shapes=buffers([out]) + [pltpu.SemaphoreType.DMA((1,))],
        compiler_params=PARAMS,
        cost_estimate=cost(0, 0),
        name="add_half",
    )(*parts)


PRODUCTS = ((0, 0), (0, 1), (0, 2), (1, 1), (1, 2), (2, 2))


def products(vectors, packs, chosen):
    width = LANES // packs
    rows = []
    for pair in PRODUCTS:
        if pair not in chosen:
            rows.append(jnp.zeros((1, LANES), F32))
            continue
        total = jnp.sum(vectors[pair[0]] * vectors[pair[1]], axis=0)
        total = jnp.sum(total, axis=0, keepdims=True)
        folded = total
        for g in range(1, packs):
            folded = folded + pltpu.roll(total, g * width, 1)
        rows.append(folded)
    rows.append(jnp.zeros((2, LANES), F32))
    return jnp.concatenate(rows, axis=0)


def early_kernel(packs, b_ref, gl_ref, gr_ref, out_ref):
    first = jnp.concatenate([gl_ref[...], gr_ref[...]], axis=0)
    out_ref[...] = products((b_ref[...], first), packs, ((0, 0), (0, 1), (1, 1)))


def early_dots(b_own, g_own, packs):
    return pl.pallas_call(
        functools.partial(early_kernel, packs),
        out_shape=jax.ShapeDtypeStruct((8, LANES), F32),
        in_specs=[VMEM_SPEC] * 3,
        out_specs=VMEM_SPEC,
        compiler_params=PARAMS,
        cost_estimate=cost(6 * b_own.size, 8 * b_own.size),
        name="early_dots",
    )(b_own, *g_own)


def dots_kernel(packs, b_ref, gl_ref, gr_ref, early_ref, *refs):
    parts, (out, image_ref, held, sems) = refs[:-4], refs[-4:]
    image = parts[0][...]
    for part in parts[1:]:
        image = image + part[...]
    image_ref[...] = image
    first = jnp.concatenate([gl_ref[...], gr_ref[...]], axis=0)
    late = products((b_ref[...], first, image), packs, ((0, 2), (1, 2), (2, 2)))
    held[...] = early_ref[...] + late
    fetch([(held, out)], sems)


def dots(b_own, g_own, early, parts, packs):
    operands = (b_own, *g_own, early, *parts)
    outs = [jax.ShapeDtypeStruct((8, LANES), F32), jax.ShapeDtypeStruct(b_own.shape, F32)]
    return pl.pallas_call(
        functools.partial(dots_kernel, packs),
        out_shape=outs,
        in_specs=[VMEM_SPEC] * len(operands),
        out_specs=[ANY_SPEC, VMEM_SPEC],
        scratch_shapes=buffers(outs[:1]) + [pltpu.SemaphoreType.DMA((1,))],
        compiler_params=PARAMS,
        cost_estimate=cost(8 * b_own.size, 20 * b_own.size),
        name="dots",
    )(*operands)


def least_squares(rhs_length, upper_left, lower_left, top_two, mid_two, lower_right):
    radius_one = jnp.sqrt(upper_left * upper_left + lower_left * lower_left)
    cosine_one = upper_left / radius_one
    sine_one = lower_left / radius_one
    rotated_top = cosine_one * rhs_length
    rotated_mid = -sine_one * rhs_length
    coupled = cosine_one * top_two + sine_one * mid_two
    diagonal_two = cosine_one * mid_two - sine_one * top_two
    radius_two = jnp.sqrt(diagonal_two * diagonal_two + lower_right * lower_right)
    weight_two = diagonal_two * rotated_mid / (radius_two * radius_two)
    weight_one = (rotated_top - coupled * weight_two) / radius_one
    return (weight_one, weight_two)


def finish_kernel(packs, *refs):
    mine_ref, other_ref, b_ref, gl_ref, gr_ref, image_ref = refs[:6]
    outs, (solution_ref, residual_ref, sems) = refs[6:8], refs[8:]
    total = mine_ref[...] + other_ref[...]
    bb, b1, b2, s11, s12, s22 = [total[i : i + 1, :] for i in range(6)]
    square = bb + EPS
    rhs_length = jnp.sqrt(square)
    upper_left = (0.5 * bb + b1) / square
    shift = (0.5 * EPS - b1) / square
    one = jnp.maximum(shift * shift * bb + 2.0 * shift * b1 + s11, 0.0) / square
    lower_square = one + EPS
    lower_left = jnp.sqrt(lower_square)
    f_s = (shift * bb + b1) / (square * lower_left)
    f_gs = (shift * b1 + b2) / (square * lower_left)
    s_s = one / lower_square
    s_gs = (shift * shift * b1 + shift * b2 + shift * s11 + s12) / (square * lower_square)
    gs_gs = (shift * shift * s11 + 2.0 * shift * s12 + s22) / (square * lower_square)
    top_two = 0.5 * f_s + f_gs
    mid_two = 0.5 * s_s + s_gs
    rest = 0.5 * (EPS / lower_square) - s_gs
    two = (
        gs_gs
        + top_two * top_two * (bb / square)
        + rest * rest * s_s
        - 2.0 * top_two * f_gs
        + 2.0 * rest * s_gs
        - 2.0 * top_two * rest * f_s
    )
    lower_right = jnp.sqrt(jnp.maximum(two, 0.0) + EPS)
    weight_one, weight_two = least_squares(
        rhs_length, upper_left, lower_left, top_two, mid_two, lower_right
    )
    one_scale = weight_one / rhs_length
    two_scale = weight_two / (rhs_length * lower_left)
    sol_b = one_scale + two_scale * shift
    res_b = 1.0 - 0.5 * one_scale - 0.5 * two_scale * shift
    res_1 = one_scale + two_scale * (0.5 + shift)
    width = LANES // packs
    per = REACH // packs
    for half, g_ref in enumerate((gl_ref, gr_ref)):
        for k in range(per):
            b, g, image = b_ref[half * per + k], g_ref[k], image_ref[half * per + k]
            answer = sol_b * b + two_scale * g
            left = res_b * b - res_1 * g - two_scale * image
            for value, out_ref in ((answer, solution_ref), (left, residual_ref)):
                turned = value.T
                for j in range(packs):
                    at = cluster_at(half, j, k, per) * B
                    out_ref[:, at : at + B] = turned[j * width : (j + 1) * width]
    fetch([(solution_ref, outs[0]), (residual_ref, outs[1])], sems)


def finish(totals, b_own, g_own, image, packs):
    operands = (*totals, b_own, *g_own, image)
    out = jax.ShapeDtypeStruct((LANES // packs, CL_DEV * B), F32)
    return pl.pallas_call(
        functools.partial(finish_kernel, packs),
        out_shape=[out] * 2,
        in_specs=[VMEM_SPEC] * len(operands),
        out_specs=[ANY_SPEC] * 2,
        scratch_shapes=buffers([out, out]) + [pltpu.SemaphoreType.DMA((2,))],
        compiler_params=PARAMS,
        cost_estimate=cost(8 * b_own.size, 28 * b_own.size),
        name="finish",
    )(*operands)


def hold_kernel(*refs):
    del refs


def hold(values):
    return list(
        pl.pallas_call(
            hold_kernel,
            out_shape=[jax.ShapeDtypeStruct(v.shape, v.dtype) for v in values],
            in_specs=[ANY_SPEC] * len(values),
            out_specs=[ANY_SPEC] * len(values),
            input_output_aliases={n: n for n in range(len(values))},
            compiler_params=PARAMS,
            cost_estimate=cost(4 * 10**10, 0),
            name="hold",
        )(*values)
    )


def swap_cores(value):
    size = lax.axis_size("far")
    return lax.ppermute(value, "far", [(i, i ^ 1) for i in range(size)])


def along_y(value, shift):
    size = lax.axis_size("far")
    return lax.ppermute(value, "far", [(i, (i + CORES * shift) % size) for i in range(size)])


def along_all_y(value):
    return [value] + [along_y(value, s) for s in range(1, lax.axis_size("far") // CORES)]


def after(values, *earlier):
    flat = lax.optimization_barrier((tuple(values), earlier))
    return list(flat[0])


def to_next(value):
    return lax.ppermute(value, "rows", [(i, i + 1) for i in range(lax.axis_size("rows") - 1)])


def to_previous(value):
    return lax.ppermute(value, "rows", [(i + 1, i) for i in range(lax.axis_size("rows") - 1)])


def sum_rows(value):
    size = lax.axis_size("rows")
    step = 1
    while True:
        other = lax.ppermute(value, "rows", [(i, i ^ step) for i in range(size)])
        step *= 2
        if step >= size:
            return value, other
        value = value + other


def exchange(coef):
    return lax.all_to_all(coef, "rows", split_axis=0, concat_axis=0, tiled=True)


def sum_far(keeps, sends, coef, pieces):
    others = [[] for _ in range(pieces)]
    size = keeps[0].shape[0] // pieces
    for turn in range(1, len(keeps)):
        got, coef = lax.optimization_barrier((swap_cores(sends[turn]), coef))
        for n in range(pieces):
            rows = slice(n * size, (n + 1) * size)
            others[n].append(along_y(keeps[turn][rows] + got[rows], turn))
    return [keeps[0], swap_cores(sends[0])], others, coef


def shards(right_side, near_blocks, near_cols, far_src, far_tgt, far_left, far_right):
    far_size = lax.axis_size("far")
    ys = far_size // CORES
    width = right_side.shape[1]
    packs = LANES * far_size // width
    per = REACH // packs
    core = lax.axis_index("far") % CORES
    cols = near_cols.T
    own = right_side.reshape(CL_DEV, B, width)
    groups = far_left.shape[1]

    factors = [f.reshape(groups, B, R).transpose(0, 2, 1) for f in (far_right, far_left)]
    part, shared, _ = halo_parts(ys)
    first = core * part + lax.axis_index("far") // CORES * shared
    ends = [
        to_next(lax.dynamic_slice_in_dim(own, CL_DEV - REACH + first, shared, 0)),
        to_previous(lax.dynamic_slice_in_dim(own, first, shared, 0)),
    ]
    meta = along_all_y(jnp.stack([far_src.reshape(-1), far_tgt.reshape(-1)]))
    rights, lefts = [along_all_y(item) for item in factors]
    b_own = pack(own, far_size, per)
    second, *arrived = hold(ends[1:] + meta[1:])
    first, *held = hold(ends[:1] + lefts[1:])
    meta, lefts = meta[:1] + arrived, lefts[:1] + held
    pieces = [first, second]
    for s in range(1, ys):
        pieces += [along_y(item, s) for item in (first, second)]
    meta, rights, lefts = [
        items + [swap_cores(item) for item in items] for items in (meta, rights, lefts)
    ]
    coef = coefficients(meta, rights, [b_own], far_size)
    pieces = after(pieces, coef)
    pieces += [swap_cores(item) for item in pieces]
    coef = exchange(coef)
    keeps, sends = operator(near_blocks, [own] + pieces, cols, far_size, per, width, False)
    terms, others, coef = sum_far(keeps, sends, coef, 2)
    base = far_part(meta, lefts, coef, terms, far_size, per)
    g_own = [add_half(half, [base], others[half]) for half in range(2)]

    head, tail = g_own
    from_left, from_right = to_next(tail), to_previous(head)
    heads, tails = along_all_y(head), along_all_y(tail)
    coef = coefficients(meta, rights, g_own, far_size)
    arrived = after([from_left, from_right] + heads[1:] + tails[1:], coef)
    from_left, from_right = arrived[:2]
    heads, tails = heads[:1] + arrived[2 : 1 + ys], tails[:1] + arrived[1 + ys :]
    halos = [from_left, from_right]
    for s in range(1, ys):
        halos += [along_y(from_left, s), to_previous(heads[s])]
    owns = [item for pair in zip(heads, tails) for item in pair]
    owns += [swap_cores(item) for item in owns]
    halos += [swap_cores(item) for item in halos]
    coef = exchange(coef)
    keeps, sends = operator(near_blocks, owns + halos, cols, far_size, per, width, True)
    terms, (others,), coef = sum_far(keeps, sends, coef, 1)
    base = far_part(meta, lefts, coef, terms, far_size, per)
    early = early_dots(b_own, g_own, packs)
    part_dots, image = dots(b_own, g_own, early, [base] + others, packs)
    answer, residual = finish(sum_rows(part_dots), b_own, g_own, image, packs)
    return answer.T, residual.T


def solution(mesh):
    return jax.shard_map(
        shards,
        mesh=mesh,
        in_specs=(
            P("rows", None),
            P("rows", "far", None, None),
            P("rows", "far"),
            P("rows", None, "far"),
            P("rows", None, "far"),
            P("rows", None, "far", None, None),
            P("rows", None, "far", None, None),
        ),
        out_specs=(P("rows", "far"), P("rows", "far")),
        check_vma=False,
    )
```

```python
import functools

import jax
import jax.numpy as jnp
from jax import lax
from jax.experimental import pallas as pl
from jax.experimental.pallas import tpu as pltpu
from jax.sharding import PartitionSpec as P

B = 128
R = 64
CL_DEV = 16
REACH = 8
CORES = 2
LANES = 128
EPS = 1e-06
F32 = jnp.float32
BF16 = jnp.bfloat16
VMEM_LIMIT = 16 * 1024 * 1024
WIDE_LIMIT = 60 * 1024 * 1024


VMEM_SPEC = pl.BlockSpec(memory_space=pltpu.VMEM)
SMEM_SPEC = pl.BlockSpec(memory_space=pltpu.SMEM)
ANY_SPEC = pl.BlockSpec(memory_space=pl.ANY)
PARAMS = pltpu.CompilerParams(vmem_limit_bytes=VMEM_LIMIT)
WIDE = pltpu.CompilerParams(vmem_limit_bytes=WIDE_LIMIT)


def split(value):
    high = value.astype(BF16)
    low = (value - high.astype(F32)).astype(BF16)
    return high, low


def dot3(left, right, dims=((1,), (0,))):
    (lh, ll), (rh, rl) = left, right
    dot = functools.partial(
        lax.dot_general, dimension_numbers=(dims, ((), ())), preferred_element_type=F32
    )
    return dot(lh, rh) + (dot(ll, rh) + dot(lh, rl))


def cost(flops, size):
    return pl.CostEstimate(flops=flops, bytes_accessed=size, transcendentals=0)


def place(far_size):
    index = lax.axis_index("far")
    return index // CORES, index % CORES, far_size // CORES


def owner_of(n, far_size):
    y, core, ys = place(far_size)
    shift, other = n % ys, n // ys
    return lax.rem(y - shift + ys, ys) * CORES + (1 - core if other else core)


def halo_parts(ys):
    part = REACH // CORES
    shared = max(1, part // ys)
    return part, shared, part - ys * shared


def begin(pairs, sems, first=0):
    copies = [pltpu.make_async_copy(a, b, sems.at[first + n]) for n, (a, b) in enumerate(pairs)]
    for copy in copies:
        copy.start()
    return copies


def fetch(pairs, sems, first=0):
    for copy in begin(pairs, sems, first):
        copy.wait()


def buffers(arrays):
    return [pltpu.VMEM(a.shape, a.dtype) for a in arrays]


def cluster_at(half, j, k, per):
    return half * REACH + j * per + k


def pack_columns(far_size, per, source, out_ref):
    index = lax.axis_index("far")
    packs = REACH // per
    width = LANES // packs
    for owner in range(far_size):

        @pl.when(index == owner)
        def _():
            for half in range(2):
                for k in range(per):
                    out_ref[half * per + k] = jnp.concatenate(
                        [
                            source(cluster_at(half, j, k, per))[:, owner * width : (owner + 1) * width]
                            for j in range(packs)
                        ],
                        axis=1,
                    )


def pack_kernel(far_size, b_ref, out, field, own, sems):
    fetch([(b_ref, field)], sems)
    pack_columns(far_size, own.shape[0] // 2, lambda c: field[c], own)
    fetch([(own, out)], sems)


def pack(field, far_size, per):
    out = jax.ShapeDtypeStruct((2 * per, B, LANES), F32)
    return pl.pallas_call(
        functools.partial(pack_kernel, far_size),
        out_shape=out,
        in_specs=[ANY_SPEC],
        out_specs=ANY_SPEC,
        scratch_shapes=buffers([field, out]) + [pltpu.SemaphoreType.DMA((1,))],
        compiler_params=PARAMS,
        cost_estimate=cost(0, 8 * field.size),
        name="pack",
    )(field)


def coefficient_kernel(far_size, n_fields, n_waits, *refs):
    refs = refs[: 2 * far_size + n_fields] + refs[2 * far_size + n_fields + n_waits :]
    meta, hbm = refs[:far_size], refs[far_size : 2 * far_size + n_fields]
    out, refs = refs[2 * far_size + n_fields], refs[2 * far_size + n_fields + 1 :]
    vmem, (held, high, low, sems) = refs[: far_size + n_fields], refs[far_size + n_fields :]
    copies = begin(list(zip(hbm, vmem)), sems)
    factors, fields = vmem[:far_size], vmem[far_size:]
    per = sum(f.shape[0] for f in fields) // 2
    packs = REACH // per
    width = LANES // packs
    for copy in copies[far_size:]:
        copy.wait()
    entries = [f[k] for f in fields for k in range(f.shape[0])]
    for half in range(2):
        for k in range(per):
            entry = entries[half * per + k]
            for j in range(packs):
                h, l = split(entry[:, j * width : (j + 1) * width])
                high[cluster_at(half, j, k, per)] = h
                low[cluster_at(half, j, k, per)] = l
    for copy in copies[:far_size]:
        copy.wait()
    depth = far_size // packs

    def group(t, carry):
        for e in range(depth):
            parts = []
            for j in range(packs):
                n = j * depth + e
                source = meta[n][0, t]
                parts.append(dot3(split(factors[n][t]), (high[source], low[source])))
            held[t, e] = jnp.concatenate(parts, axis=1)
        return carry

    lax.fori_loop(0, held.shape[0], group, 0, unroll=4)
    fetch([(held, out)], sems)


def coefficients(meta, factors, fields, far_size, waits=()):
    groups = factors[0].shape[0]
    per = sum(f.shape[0] for f in fields) // 2
    packs = REACH // per
    width = LANES // packs
    out = jax.ShapeDtypeStruct((groups, far_size // packs, R, LANES), F32)
    return pl.pallas_call(
        functools.partial(coefficient_kernel, far_size, len(fields), len(waits)),
        out_shape=out,
        in_specs=[SMEM_SPEC] * far_size + [ANY_SPEC] * (far_size + len(fields) + len(waits)),
        out_specs=ANY_SPEC,
        scratch_shapes=[pltpu.VMEM((groups, R, B), F32)] * far_size
        + buffers([*fields, out])
        + [
            pltpu.VMEM((CL_DEV, B, width), BF16),
            pltpu.VMEM((CL_DEV, B, width), BF16),
            pltpu.SemaphoreType.DMA((far_size + len(fields),)),
        ],
        compiler_params=PARAMS,
        cost_estimate=cost(6 * groups * far_size * R * B * width, 4 * 1024 * 1024),
        name="coefficients",
    )(*meta, *factors, *fields, *waits)


def far_kernel(far_size, n_terms, *refs):
    n = far_size + 1 + n_terms
    meta, hbm, held = refs[:far_size], refs[far_size : far_size + n], refs[far_size + n]
    vmem, (total, sems) = refs[far_size + n + 1 : -2], refs[-2:]
    copies = begin(list(zip(hbm, vmem)), sems)
    terms = vmem[far_size + 1 :]
    factors, coef = vmem[:far_size], vmem[far_size]
    per = held.shape[0] // 2
    packs = REACH // per
    width = LANES // packs
    depth = far_size // packs
    total[...] = jnp.zeros_like(total)
    for copy in copies:
        copy.wait()

    def group(a, carry):
        for e in range(depth):
            for j in range(packs):
                n = j * depth + e
                here = coef[a, e][:, j * width : (j + 1) * width]
                target = meta[n][1, a]
                total[target] += dot3(split(factors[n][a]), split(here), ((0,), (0,)))
        return carry

    lax.fori_loop(0, coef.shape[0], group, 0, unroll=4)
    for half in range(2):
        for k in range(per):
            value = jnp.concatenate(
                [total[cluster_at(half, j, k, per)] for j in range(packs)], axis=1
            )
            for term in terms:
                value = value + term[half * per + k]
            held[half * per + k] = value


def far_part(meta, factors, coef, terms, far_size, per):
    groups = coef.shape[0]
    width = LANES * per // REACH
    operands = [*factors, coef, *terms]
    return pl.pallas_call(
        functools.partial(far_kernel, far_size, len(terms)),
        out_shape=jax.ShapeDtypeStruct((2 * per, B, LANES), F32),
        in_specs=[SMEM_SPEC] * far_size + [ANY_SPEC] * len(operands),
        out_specs=VMEM_SPEC,
        scratch_shapes=[pltpu.VMEM((groups, R, B), F32)] * far_size
        + buffers([coef, *terms])
        + [pltpu.VMEM((CL_DEV, B, width), F32), pltpu.SemaphoreType.DMA((len(operands),))],
        compiler_params=PARAMS,
        cost_estimate=cost(6 * groups * far_size * R * B * width, 4 * 1024 * 1024),
        name="far_part",
    )(*meta, *operands)


def unpack(stage, per, put):
    far_size, halves = stage.shape[0], stage.shape[1]
    packs = REACH // per
    width = LANES // packs
    for half in range(halves):
        for k in range(per):
            for block in range(far_size // packs):
                entries = [stage[block * packs + i, half, k] for i in range(packs)]
                for j in range(packs):
                    value = jnp.concatenate(
                        [e[:, j * width : (j + 1) * width] for e in entries], axis=1
                    )
                    put(half, j * per + k, block * LANES, value)


def store_split(high, low, first=0, after=0):
    def put(half, c, lane, value):
        place_ = (after if half else first) + c
        hi, lo = split(value)
        high[place_, :, lane : lane + LANES] = hi
        low[place_, :, lane : lane + LANES] = lo

    return put


def packed_pairs(pieces, far_size, stage):
    pairs = []
    for n in range(far_size):
        owner = owner_of(n, far_size)
        for half in range(2):
            pairs.append((pieces[2 * n + half], stage.at[owner, half]))
    return pairs


def operator_kernel(far_size, per, last, n_pieces, cols_ref, blocks_ref, *refs):
    pieces, refs = refs[:n_pieces], refs[n_pieces:]
    ys = far_size // CORES
    outs, refs = refs[: 2 * ys], refs[2 * ys :]
    blocks, high, low, own_stage, stage, held, own_sems, in_sems, block_sems, out_sems = refs
    slots = cols_ref.shape[0]
    packs = REACH // per
    width = LANES // packs
    y, core, _ = place(far_size)
    base = lax.axis_index("rows") * CL_DEV - REACH

    if last:
        own_pairs = packed_pairs(pieces[: 2 * far_size], far_size, own_stage)
        halo_pairs = packed_pairs(pieces[2 * far_size :], far_size, stage)
    else:
        part, shared, direct = halo_parts(ys)
        own_pairs = [(pieces[0], own_stage)]
        halo_pairs = []
        each = (len(pieces) - 1) // CORES
        for n, piece in enumerate(pieces[1:]):
            turn, side = divmod(n % each, 2)
            first = side * REACH + (core if n < each else 1 - core) * part
            if turn < ys:
                first, count = first + lax.rem(y - turn + ys, ys) * shared, shared
            else:
                first, count = first + ys * shared, direct
            halo_pairs.append((piece, stage.at[pl.ds(first, count)]))
    own_copies = begin(own_pairs, own_sems)
    halo_copies = begin(halo_pairs, in_sems)

    def block_copies(entry):
        half, k = entry // per, entry % per
        at = [cluster_at(half, j, k, per) for j in range(packs)]
        return [pltpu.make_async_copy(blocks_ref.at[c], blocks.at[c], block_sems.at[c]) for c in at]

    for copy in own_copies:
        copy.wait()
    for entry in range(2 * per):
        for copy in block_copies(entry):
            copy.start()
    if last:
        unpack(own_stage, per, store_split(high, low, REACH, 2 * REACH))
    else:
        for c in range(CL_DEV):
            high[REACH + c], low[REACH + c] = split(own_stage[c])
    for copy in halo_copies:
        copy.wait()
    if last:
        unpack(stage, per, store_split(high, low, 0, REACH + CL_DEV))
    else:
        for c in range(2 * REACH):
            at = c if c < REACH else CL_DEV + c
            high[at], low[at] = split(stage[c])

    chunk = max(1, per // 2)

    def out_copies(part):
        rows = pl.ds(part * chunk, chunk)
        copies = []
        for n, out in enumerate(outs):
            taker = core if n < ys else 1 - core
            owner = lax.rem(y + n % ys, ys) * CORES + taker
            copies.append(
                pltpu.make_async_copy(held.at[owner, rows], out.at[rows], out_sems.at[n, part])
            )
        return copies

    def step(entry, carry):
        half, k = entry // per, entry % per
        for copy in block_copies(entry):
            copy.wait()
        images = []
        for j in range(packs):
            cluster = cluster_at(half, j, k, per)
            at = [cols_ref[s, cluster] - base for s in range(slots)]
            right = tuple(jnp.concatenate([ref[p] for p in at], axis=0) for ref in (high, low))
            left = split(jnp.concatenate([blocks[cluster, s] for s in range(slots)], axis=1))
            images.append(dot3(left, right))
        for owner in range(far_size):
            held[owner, entry] = jnp.concatenate(
                [im[:, owner * width : (owner + 1) * width] for im in images], axis=1
            )
        return carry

    parts = 2 * per // chunk
    for part in range(parts):
        lax.fori_loop(part * chunk, (part + 1) * chunk, step, 0, unroll=True)
        for copy in out_copies(part):
            copy.start()
    for part in range(parts):
        for copy in out_copies(part):
            copy.wait()


def operator(blocks, pieces, cols, far_size, per, width, last):
    ys = far_size // CORES
    n_own = 2 * far_size if last else 1
    if last:
        stages = [pltpu.VMEM((far_size, 2, per, B, LANES), F32)] * 2
    else:
        stages = [pltpu.VMEM((CL_DEV, B, width), F32), pltpu.VMEM((2 * REACH, B, width), F32)]
    outs = pl.pallas_call(
        functools.partial(operator_kernel, far_size, per, last, len(pieces)),
        out_shape=[jax.ShapeDtypeStruct((2 * per, B, LANES), F32)] * (2 * ys),
        in_specs=[SMEM_SPEC] + [ANY_SPEC] * (1 + len(pieces)),
        out_specs=[ANY_SPEC] * (2 * ys),
        scratch_shapes=buffers([blocks])
        + [
            pltpu.VMEM((CL_DEV + 2 * REACH, B, width), BF16),
            pltpu.VMEM((CL_DEV + 2 * REACH, B, width), BF16),
            *stages,
            pltpu.VMEM((far_size, 2 * per, B, LANES), F32),
            pltpu.SemaphoreType.DMA((n_own,)),
            pltpu.SemaphoreType.DMA((len(pieces) - n_own,)),
            pltpu.SemaphoreType.DMA((CL_DEV,)),
            pltpu.SemaphoreType.DMA((2 * ys, 2 * per // max(1, per // 2))),
        ],
        compiler_params=WIDE,
        cost_estimate=cost(0, 0),
        name="operator",
    )(cols, blocks, *pieces)
    return outs[:ys], outs[ys:]


def add_kernel(half, n_whole, *refs):
    parts, (out, held, sems) = refs[:-3], refs[-3:]
    per = held.shape[0]
    total = parts[0][half * per : (half + 1) * per]
    for part in parts[1:n_whole]:
        total = total + part[half * per : (half + 1) * per]
    for part in parts[n_whole:]:
        total = total + part[...]
    held[...] = total
    fetch([(held, out)], sems)


def add_half(half, wholes, halves):
    out = jax.ShapeDtypeStruct(halves[0].shape, F32)
    parts = list(wholes) + list(halves)
    return pl.pallas_call(
        functools.partial(add_kernel, half, len(wholes)),
        out_shape=out,
        in_specs=[VMEM_SPEC] * len(parts),
        out_specs=ANY_SPEC,
        scratch_shapes=buffers([out]) + [pltpu.SemaphoreType.DMA((1,))],
        compiler_params=PARAMS,
        cost_estimate=cost(0, 0),
        name="add_half",
    )(*parts)


PRODUCTS = ((0, 0), (0, 1), (0, 2), (1, 1), (1, 2), (2, 2))


def products(vectors, packs, chosen):
    width = LANES // packs
    rows = []
    for pair in PRODUCTS:
        if pair not in chosen:
            rows.append(jnp.zeros((1, LANES), F32))
            continue
        total = jnp.sum(vectors[pair[0]] * vectors[pair[1]], axis=0)
        total = jnp.sum(total, axis=0, keepdims=True)
        folded = total
        for g in range(1, packs):
            folded = folded + pltpu.roll(total, g * width, 1)
        rows.append(folded)
    rows.append(jnp.zeros((2, LANES), F32))
    return jnp.concatenate(rows, axis=0)


def early_kernel(packs, b_ref, gl_ref, gr_ref, out_ref):
    first = jnp.concatenate([gl_ref[...], gr_ref[...]], axis=0)
    out_ref[...] = products((b_ref[...], first), packs, ((0, 0), (0, 1), (1, 1)))


def early_dots(b_own, g_own, packs):
    return pl.pallas_call(
        functools.partial(early_kernel, packs),
        out_shape=jax.ShapeDtypeStruct((8, LANES), F32),
        in_specs=[VMEM_SPEC] * 3,
        out_specs=VMEM_SPEC,
        compiler_params=PARAMS,
        cost_estimate=cost(6 * b_own.size, 8 * b_own.size),
        name="early_dots",
    )(b_own, *g_own)


def dots_kernel(packs, b_ref, gl_ref, gr_ref, early_ref, *refs):
    parts, (out, image_ref, held, sems) = refs[:-4], refs[-4:]
    image = parts[0][...]
    for part in parts[1:]:
        image = image + part[...]
    image_ref[...] = image
    first = jnp.concatenate([gl_ref[...], gr_ref[...]], axis=0)
    late = products((b_ref[...], first, image), packs, ((0, 2), (1, 2), (2, 2)))
    held[...] = early_ref[...] + late
    fetch([(held, out)], sems)


def dots(b_own, g_own, early, parts, packs):
    operands = (b_own, *g_own, early, *parts)
    outs = [jax.ShapeDtypeStruct((8, LANES), F32), jax.ShapeDtypeStruct(b_own.shape, F32)]
    return pl.pallas_call(
        functools.partial(dots_kernel, packs),
        out_shape=outs,
        in_specs=[VMEM_SPEC] * len(operands),
        out_specs=[ANY_SPEC, VMEM_SPEC],
        scratch_shapes=buffers(outs[:1]) + [pltpu.SemaphoreType.DMA((1,))],
        compiler_params=PARAMS,
        cost_estimate=cost(8 * b_own.size, 20 * b_own.size),
        name="dots",
    )(*operands)


def least_squares(rhs_length, upper_left, lower_left, top_two, mid_two, lower_right):
    radius_one = jnp.sqrt(upper_left * upper_left + lower_left * lower_left)
    cosine_one = upper_left / radius_one
    sine_one = lower_left / radius_one
    rotated_top = cosine_one * rhs_length
    rotated_mid = -sine_one * rhs_length
    coupled = cosine_one * top_two + sine_one * mid_two
    diagonal_two = cosine_one * mid_two - sine_one * top_two
    radius_two = jnp.sqrt(diagonal_two * diagonal_two + lower_right * lower_right)
    weight_two = diagonal_two * rotated_mid / (radius_two * radius_two)
    weight_one = (rotated_top - coupled * weight_two) / radius_one
    return (weight_one, weight_two)


def finish_kernel(packs, *refs):
    mine_ref, other_ref, b_ref, gl_ref, gr_ref, image_ref = refs[:6]
    outs, (solution_ref, residual_ref, sems) = refs[6:8], refs[8:]
    total = mine_ref[...] + other_ref[...]
    bb, b1, b2, s11, s12, s22 = [total[i : i + 1, :] for i in range(6)]
    square = bb + EPS
    rhs_length = jnp.sqrt(square)
    upper_left = (0.5 * bb + b1) / square
    shift = (0.5 * EPS - b1) / square
    one = jnp.maximum(shift * shift * bb + 2.0 * shift * b1 + s11, 0.0) / square
    lower_square = one + EPS
    lower_left = jnp.sqrt(lower_square)
    f_s = (shift * bb + b1) / (square * lower_left)
    f_gs = (shift * b1 + b2) / (square * lower_left)
    s_s = one / lower_square
    s_gs = (shift * shift * b1 + shift * b2 + shift * s11 + s12) / (square * lower_square)
    gs_gs = (shift * shift * s11 + 2.0 * shift * s12 + s22) / (square * lower_square)
    top_two = 0.5 * f_s + f_gs
    mid_two = 0.5 * s_s + s_gs
    rest = 0.5 * (EPS / lower_square) - s_gs
    two = (
        gs_gs
        + top_two * top_two * (bb / square)
        + rest * rest * s_s
        - 2.0 * top_two * f_gs
        + 2.0 * rest * s_gs
        - 2.0 * top_two * rest * f_s
    )
    lower_right = jnp.sqrt(jnp.maximum(two, 0.0) + EPS)
    weight_one, weight_two = least_squares(
        rhs_length, upper_left, lower_left, top_two, mid_two, lower_right
    )
    one_scale = weight_one / rhs_length
    two_scale = weight_two / (rhs_length * lower_left)
    sol_b = one_scale + two_scale * shift
    res_b = 1.0 - 0.5 * one_scale - 0.5 * two_scale * shift
    res_1 = one_scale + two_scale * (0.5 + shift)
    width = LANES // packs
    per = REACH // packs
    for half, g_ref in enumerate((gl_ref, gr_ref)):
        for k in range(per):
            b, g, image = b_ref[half * per + k], g_ref[k], image_ref[half * per + k]
            answer = sol_b * b + two_scale * g
            left = res_b * b - res_1 * g - two_scale * image
            for value, out_ref in ((answer, solution_ref), (left, residual_ref)):
                turned = value.T
                for j in range(packs):
                    at = cluster_at(half, j, k, per) * B
                    out_ref[:, at : at + B] = turned[j * width : (j + 1) * width]
    fetch([(solution_ref, outs[0]), (residual_ref, outs[1])], sems)


def finish(totals, b_own, g_own, image, packs):
    operands = (*totals, b_own, *g_own, image)
    out = jax.ShapeDtypeStruct((LANES // packs, CL_DEV * B), F32)
    return pl.pallas_call(
        functools.partial(finish_kernel, packs),
        out_shape=[out] * 2,
        in_specs=[VMEM_SPEC] * len(operands),
        out_specs=[ANY_SPEC] * 2,
        scratch_shapes=buffers([out, out]) + [pltpu.SemaphoreType.DMA((2,))],
        compiler_params=PARAMS,
        cost_estimate=cost(8 * b_own.size, 28 * b_own.size),
        name="finish",
    )(*operands)


def hold_kernel(*refs):
    del refs


def hold(values):
    return list(
        pl.pallas_call(
            hold_kernel,
            out_shape=[jax.ShapeDtypeStruct(v.shape, v.dtype) for v in values],
            in_specs=[ANY_SPEC] * len(values),
            out_specs=[ANY_SPEC] * len(values),
            input_output_aliases={n: n for n in range(len(values))},
            compiler_params=PARAMS,
            cost_estimate=cost(4 * 10**10, 0),
            name="hold",
        )(*values)
    )


def swap_cores(value):
    size = lax.axis_size("far")
    return lax.ppermute(value, "far", [(i, i ^ 1) for i in range(size)])


def along_y(value, shift):
    size = lax.axis_size("far")
    return lax.ppermute(value, "far", [(i, (i + CORES * shift) % size) for i in range(size)])


def along_all_y(value):
    return [value] + [along_y(value, s) for s in range(1, lax.axis_size("far") // CORES)]


def after(values, *earlier):
    flat = lax.optimization_barrier((tuple(values), earlier))
    return list(flat[0])


def to_next(value):
    return lax.ppermute(value, "rows", [(i, i + 1) for i in range(lax.axis_size("rows") - 1)])


def to_previous(value):
    return lax.ppermute(value, "rows", [(i + 1, i) for i in range(lax.axis_size("rows") - 1)])


def sum_rows(value):
    size = lax.axis_size("rows")
    step = 1
    while True:
        other = lax.ppermute(value, "rows", [(i, i ^ step) for i in range(size)])
        step *= 2
        if step >= size:
            return value, other
        value = value + other


def exchange(coef):
    return lax.all_to_all(coef, "rows", split_axis=0, concat_axis=0, tiled=True)


def sum_far(keeps, sends, coef, pieces):
    others = [[] for _ in range(pieces)]
    size = keeps[0].shape[0] // pieces
    for turn in range(1, len(keeps)):
        got, coef = lax.optimization_barrier((swap_cores(sends[turn]), coef))
        for n in range(pieces):
            rows = slice(n * size, (n + 1) * size)
            others[n].append(along_y(keeps[turn][rows] + got[rows], turn))
    return [keeps[0], swap_cores(sends[0])], others, coef


def shards(right_side, near_blocks, near_cols, far_src, far_tgt, far_left, far_right):
    far_size = lax.axis_size("far")
    ys = far_size // CORES
    width = right_side.shape[1]
    packs = LANES * far_size // width
    per = REACH // packs
    core = lax.axis_index("far") % CORES
    cols = near_cols.T
    own = right_side.reshape(CL_DEV, B, width)
    groups = far_left.shape[1]

    factors = [f.reshape(groups, B, R).transpose(0, 2, 1) for f in (far_right, far_left)]
    part, shared, _ = halo_parts(ys)
    first = core * part + lax.axis_index("far") // CORES * shared
    ends = [
        to_next(lax.dynamic_slice_in_dim(own, CL_DEV - REACH + first, shared, 0)),
        to_previous(lax.dynamic_slice_in_dim(own, first, shared, 0)),
    ]
    meta = along_all_y(jnp.stack([far_src.reshape(-1), far_tgt.reshape(-1)]))
    rights, lefts = [along_all_y(item) for item in factors]
    b_own = pack(own, far_size, per)
    second, *arrived = hold(ends[1:] + meta[1:])
    first, *held = hold(ends[:1] + lefts[1:])
    meta, lefts = meta[:1] + arrived, lefts[:1] + held
    pieces = [first, second]
    for s in range(1, ys):
        pieces += [along_y(item, s) for item in (first, second)]
    meta, rights, lefts = [
        items + [swap_cores(item) for item in items] for items in (meta, rights, lefts)
    ]
    coef = coefficients(meta, rights, [b_own], far_size)
    pieces = after(pieces, coef)
    pieces += [swap_cores(item) for item in pieces]
    coef = exchange(coef)
    keeps, sends = operator(near_blocks, [own] + pieces, cols, far_size, per, width, False)
    terms, others, coef = sum_far(keeps, sends, coef, 2)
    base = far_part(meta, lefts, coef, terms, far_size, per)
    g_own = [add_half(half, [base], others[half]) for half in range(2)]

    head, tail = g_own
    from_left, from_right = to_next(tail), to_previous(head)
    heads, tails = along_all_y(head), along_all_y(tail)
    coef = coefficients(meta, rights, g_own, far_size)
    arrived = after([from_left, from_right] + heads[1:] + tails[1:], coef)
    from_left, from_right = arrived[:2]
    heads, tails = heads[:1] + arrived[2 : 1 + ys], tails[:1] + arrived[1 + ys :]
    halos = [from_left, from_right]
    for s in range(1, ys):
        halos += [to_next(tails[s]), along_y(from_right, s)]
    owns = [item for pair in zip(heads, tails) for item in pair]
    owns += [swap_cores(item) for item in owns]
    halos += [swap_cores(item) for item in halos]
    coef = exchange(coef)
    keeps, sends = operator(near_blocks, owns + halos, cols, far_size, per, width, True)
    terms, (others,), coef = sum_far(keeps, sends, coef, 1)
    base = far_part(meta, lefts, coef, terms, far_size, per)
    early = early_dots(b_own, g_own, packs)
    part_dots, image = dots(b_own, g_own, early, [base] + others, packs)
    answer, residual = finish(sum_rows(part_dots), b_own, g_own, image, packs)
    return answer.T, residual.T


def solution(mesh):
    return jax.shard_map(
        shards,
        mesh=mesh,
        in_specs=(
            P("rows", None),
            P("rows", "far", None, None),
            P("rows", "far"),
            P("rows", None, "far"),
            P("rows", None, "far"),
            P("rows", None, "far", None, None),
            P("rows", None, "far", None, None),
        ),
        out_specs=(P("rows", "far"), P("rows", "far")),
        check_vma=False,
    )
```
